32 devices in a mesh: expert: 8 (over z, y), inner: 2 (over x), outer: 2 (over core).
Axes of the slice: x: 2, y: 2, z: 4, core: 2. Of those that a mesh axis runs over, the one named last changes fastest.
Arguments:
- token_grads: bfloat16 [4096, 8192], P(('expert', 'inner', 'outer')), may hold values from -6 to 6
- router_gates: bfloat16 [4096, 2], P(('expert', 'inner', 'outer')), may hold values from 0.099609375 to 1
- expert_ids: int32 [4096, 2], P(('expert', 'inner', 'outer')), may hold values from 0 to 15, all different within a row; in each aligned block of 128 rows (0 to 127, 128 to 255, ...) at most 20 rows name the same one
- saved_hidden: bfloat16 [4096, 128], P(('expert', 'inner', 'outer')), may hold values from -6 to 6
- up_weight: bfloat16 [16, 64, 8192], P('expert', None, ('inner', 'outer')), may hold values from -0.75 to 0.75
- down_weight: bfloat16 [16, 64, 8192], P('expert', None, ('inner', 'outer')), may hold values from -0.0625 to 0.0625
Outputs:
- input_grads: bfloat16 [4096, 8192], P(('expert', 'inner', 'outer'))
- gate_grads: bfloat16 [4096, 2], P(('expert', 'inner', 'outer'))
- down_grads: bfloat16 [16, 64, 8192], P('expert', None, ('inner', 'outer'))
The draws below stay inside these ranges and needn't reach their ends.
Inputs may be any that keep to these rules, and one draw needn't show every extreme that they name: `expert_ids`: each row names 2 different experts; within the rows of one device (aligned blocks of 128 rows) no expert is named more than 20 times.
All inputs are finite; a program needn't handle non-finite values.
Results may differ from the reference program's by a relative error of at most 0.0067.
Values may be sent and summed in bfloat16 or wider, within the bound.
No kernel may reach another device: no remote copies, remote signals or barrier semaphores. Data moves between devices by JAX's collectives and lax.ppermute only.
A program may use at most 128 MiB of HBM per device.

```python
import math
import jax
import jax.numpy as jnp
import numpy as np
from jax import lax

D = 8192
F = 64
TOP = 2
TOK_DEV = 128
EXPERTS = 16
CAP = 20
TOKENS = 4096
N_EXPERT = 8
N_INNER = 2
N_OUTER = 2


def with_spikes(result, key, source, target, parts, factor):
    owner, partner = [(jnp.arange(result.shape[axis_at]) // (result.shape[axis_at] // parts)).reshape([-1 if axis == axis_at else 1 for axis in range(result.ndim)]) for axis_at in (source, target)]
    chosen = jax.random.permutation(key, parts)[partner]
    strong = (owner == chosen) | (owner == (partner + parts // 2) % parts)
    return jnp.where(strong, factor * result, result)


def block_scale(rng, shape, shards, low, largest):
    level, own = 1.0, jax.random.fold_in(rng, 6)
    for position, shards_of in shards:
        draws = jnp.exp(jax.random.uniform(jax.random.fold_in(own, position), (shards_of,), jnp.float32, low / len(shards), largest / len(shards)))
        level = level * jnp.repeat(draws, shape[position] // shards_of).reshape([-1 if axis == position else 1 for axis in range(len(shape))])
    return level


def deal_out(own_key, own, number, rows, amount, top, most, lean):
    order = jax.random.permutation(own_key, amount)
    packed, ordinary = load_shares(amount, rows * top, most, lean, True), load_shares(amount, rows * top, most, lean, False)
    places = jnp.arange(amount)

    def named(tallies, rotation):
        used = int((tallies > 0).sum())
        fixed = max(1, used // 4)
        passed = fixed + (places - fixed + rotation * (used - fixed)) % max(1, amount - fixed)
        return jnp.zeros((amount,), jnp.int32).at[order[jnp.where(places < fixed, places, passed)]].set(jnp.asarray(tallies, jnp.int32))

    tallies = jnp.where(number % 4 == 0, named(packed, number // 4), named(ordinary, number - number // 4 - 1))
    mixed = jax.random.permutation(jax.random.fold_in(own, 3), amount)
    donor, taker = mixed[0:amount // 2 * 2:2], mixed[1:amount // 2 * 2:2]
    room = jnp.minimum(tallies[donor] - 1, most - tallies[taker]) // 2
    room = jnp.where((donor == order[0]) | (taker == order[0]) | (tallies[taker] == 0), 0, jnp.maximum(room, 0))
    passed = jax.random.randint(jax.random.fold_in(own, 4), (amount // 2,), 0, 1 << 20) % (room + 1)
    tallies = tallies.at[donor].add(-passed).at[taker].add(passed)
    labels = jnp.searchsorted(jnp.cumsum(tallies), jnp.arange(rows * top), side="right").astype(jnp.int32)
    grid = labels.reshape(top, rows).T
    grid = grid[jax.random.permutation(jax.random.fold_in(own, 1), rows)]
    rotation = jax.random.randint(jax.random.fold_in(own, 2), (rows, 1), 0, top)
    return jnp.take_along_axis(grid, (jnp.arange(top)[None, :] + rotation) % top, axis=1)


def load_shares(amount, total, most, lean, full):
    portions = [(1 << 20) // math.isqrt(grade ** lean) + 1 for grade in range(1, amount + 1)]
    largest = most if full else min(most, max(-(-total // amount), total * portions[0] // sum(portions)))
    least = 1 if total - largest >= amount - 1 else 0
    given, rest = [largest] + [least] * (amount - 1), total - largest - least * (amount - 1)
    while rest > 0:
        free = [i for i in range(1, amount) if given[i] < largest] or [i for i in range(1, amount) if given[i] < most]
        mass, budget = sum([portions[i] for i in free]), rest
        for i in free:
            addition = min(most - given[i], max(1, budget * portions[i] // mass), rest)
            given[i] = given[i] + addition
            rest = rest - addition
    return np.array(given)


def noise(own_key, shape, scale, limit, shards=(), kind=jnp.bfloat16):
    array = jax.random.normal(own_key, shape, jnp.float32) * scale
    if len(shards) > 0:
        array = block_scale(own_key, shape, shards, -0.22, 0.18) * array
    return jnp.clip(array, min=-limit, max=limit).astype(kind)


def noise_with(key, dims, width, most, split, heavy, kind=jnp.bfloat16):
    values = width * jax.random.normal(key, dims, jnp.float32)
    if split:
        values = values * block_scale(key, dims, split, -0.22, 0.18)
    return jnp.clip(with_spikes(values, jax.random.fold_in(key, 3), *heavy), -most, most).astype(kind)


def setup_inputs(seed: int = 0) -> dict:
    seeds = jax.random.split(jax.random.key(seed), 7)
    token_grads = noise_with(seeds[0], (TOKENS, D), 1.0, 6.0, ((0, 32),), (0, 1, 32, 2.75))
    router_gates = jnp.clip(0.099609375 + 0.9003906 * jax.random.uniform(seeds[1], (TOKENS, TOP), jnp.float32) ** block_scale(seeds[1], (TOKENS, TOP), ((0, 32),), -0.2, 0.2), 0.099609375, 1.0).astype(jnp.bfloat16)
    expert_ids_keys = jax.random.split(jax.random.fold_in(seeds[2], 1), TOKENS // TOK_DEV)
    expert_ids_turns = jax.random.permutation(jax.random.fold_in(seeds[2], 3), TOKENS // TOK_DEV)
    expert_ids = jax.vmap(lambda own, number: deal_out(jax.random.fold_in(seeds[2], 2), own, number, TOK_DEV, EXPERTS, TOP, CAP, 2))(expert_ids_keys, expert_ids_turns).reshape((TOKENS, TOP))
    saved_hidden = noise(seeds[3], (TOKENS, TOP * F), 1.5, 6.0, ((0, 32),))
    up_weight = noise(seeds[4], (EXPERTS, F, D), F ** -0.5, 0.75, ((0, 8), (2, 4)))
    down_weight = noise(seeds[5], (EXPERTS, F, D), D ** -0.5, 0.0625, ((0, 8), (2, 4)))
    return dict(token_grads=token_grads, router_gates=router_gates, expert_ids=expert_ids, saved_hidden=saved_hidden, up_weight=up_weight, down_weight=down_weight)


root_half = 0.7071067811865476
inv_root_tau = 0.3989422804014327


def gelu_parts(preact):
    cumulative = 0.5 * (1.0 + lax.erf(preact * root_half))
    density = inv_root_tau * jnp.exp(-0.5 * preact * preact)
    return preact * cumulative, cumulative + preact * density


def slot_numbers(route_ids):
    flat_ids = route_ids.reshape(-1)
    matches = (flat_ids[:, None] == jnp.arange(EXPERTS, dtype=jnp.int32)[None, :]).astype(jnp.int32)
    earlier = jnp.cumsum(matches, axis=0) - matches
    return (flat_ids * CAP + jnp.sum(earlier * matches, axis=1)).astype(jnp.int32)


def fill_slots(values, slot_row):
    empty = jnp.zeros((EXPERTS * CAP,) + values.shape[1:], values.dtype)
    return empty.at[slot_row].set(values)


def group_pass(token_block, gate_block, route_block, hidden_block, up_weight, down_weight):
    slot_ids = jax.vmap(slot_numbers)(route_block)
    spread = jnp.repeat(token_block, TOP, axis=1)
    slot_grads = jax.vmap(fill_slots)(spread, slot_ids).reshape(N_EXPERT, EXPERTS, CAP, D)
    slot_gates = jax.vmap(fill_slots)(gate_block.reshape(N_EXPERT, TOK_DEV * TOP), slot_ids).reshape(N_EXPERT, EXPERTS, CAP)
    slot_hidden = jax.vmap(fill_slots)(hidden_block.reshape(N_EXPERT, TOK_DEV * TOP, F), slot_ids).reshape(N_EXPERT, EXPERTS, CAP, F)
    grads_wide = slot_grads.astype(jnp.float32)
    projected = jnp.einsum('secd,efd->secf', grads_wide, down_weight.astype(jnp.float32))
    activation, gelu_slope = gelu_parts(slot_hidden.astype(jnp.float32))
    gate_values = slot_gates.astype(jnp.float32)[..., None]
    gate_grad = jnp.sum(activation * projected, axis=-1).astype(jnp.bfloat16)
    hidden_grad = (gate_values * projected * gelu_slope).astype(jnp.bfloat16)
    route_rows = jnp.einsum('secf,efd->secd', hidden_grad.astype(jnp.float32), up_weight.astype(jnp.float32)).astype(jnp.bfloat16)
    weighted = (gate_values * activation).astype(jnp.bfloat16)
    partial_value = jnp.einsum('secf,secd->efd', weighted.astype(jnp.float32), grads_wide).astype(jnp.bfloat16)
    back_rows = route_rows.reshape(N_EXPERT, EXPERTS * CAP, D)
    picked = jnp.take_along_axis(back_rows, slot_ids[..., None], axis=1)
    token_out = jnp.sum(picked.astype(jnp.float32).reshape(N_EXPERT, TOK_DEV, TOP, D), axis=2).astype(jnp.bfloat16)
    route_out = jnp.take_along_axis(gate_grad.reshape(N_EXPERT, EXPERTS * CAP), slot_ids, axis=1).reshape(N_EXPERT, TOK_DEV, TOP)
    return token_out, route_out, partial_value


def arrange(source):
    shaped = source.reshape((N_EXPERT, N_INNER, N_OUTER, TOK_DEV) + source.shape[1:])
    return jnp.moveaxis(shaped, (2, 1), (0, 1))


def reference(token_grads, router_gates, expert_ids, saved_hidden, up_weight, down_weight):
    blocks_in = (arrange(token_grads), arrange(router_gates), arrange(expert_ids), arrange(saved_hidden))

    def outer_step(grad_total, blocks):
        token_part, gate_part, route_part, hidden_part = blocks
        pair_total = jnp.zeros((EXPERTS, F, D), jnp.float32)
        token_list = []
        route_list = []
        for inner_idx in range(N_INNER):
            token_out, route_out, partial_value = group_pass(token_part[inner_idx], gate_part[inner_idx], route_part[inner_idx], hidden_part[inner_idx], up_weight, down_weight)
            pair_total = pair_total + partial_value.astype(jnp.float32)
            token_list.append(token_out)
            route_list.append(route_out)
        rounded = lax.optimization_barrier(pair_total.astype(jnp.bfloat16))
        grad_total = grad_total + rounded.astype(jnp.float32)
        return grad_total, (jnp.stack(token_list), jnp.stack(route_list))

    start = jnp.zeros((EXPERTS, F, D), jnp.float32)
    grad_total, (token_stack, route_stack) = lax.scan(outer_step, start, blocks_in)
    input_grads = jnp.moveaxis(token_stack, (0, 1), (2, 1)).reshape(TOKENS, D)
    gate_grads = jnp.moveaxis(route_stack, (0, 1), (2, 1)).reshape(TOKENS, TOP)
    return input_grads, gate_grads, grad_total.astype(jnp.bfloat16)
```

```python
import functools
import jax
import jax.numpy as jnp
from jax import lax
from jax.experimental import pallas as pl
from jax.experimental.pallas import tpu as pltpu
from jax.sharding import Mesh, PartitionSpec as P

root_half = 0.7071067811865476
inv_root_tau = 0.3989422804014327
GROUP = ("inner", "outer", "near")
BLOCK = 256
MIB = 1 << 20


def gelu_parts(preact):
    cumulative = 0.5 * (1.0 + lax.erf(preact * root_half))
    density = inv_root_tau * jnp.exp(-0.5 * preact * preact)
    return (preact * cumulative, cumulative + preact * density)


def params():
    return pltpu.CompilerParams(vmem_limit_bytes=40 * MIB)


def low_half(shape):
    return lax.broadcasted_iota(jnp.int32, shape, len(shape) - 1) < shape[-1] // 2


def down_kernel(hidden, ids_ref, weighted_ref, tokens_ref, out_ref, spread):
    first = pl.program_id(0) * (out_ref.shape[0] // hidden)
    for expert in range(out_ref.shape[0] // hidden):
        number = first + expert
        spread[expert * hidden : (expert + 1) * hidden, :] = jnp.where(
            ids_ref[0:1, :] == number,
            weighted_ref[0:hidden, :],
            jnp.where(ids_ref[1:2, :] == number, weighted_ref[hidden:, :], 0.0),
        ).astype(jnp.bfloat16)
    out_ref[...] = jnp.dot(
        spread[...], tokens_ref[...], preferred_element_type=jnp.float32
    ).astype(out_ref.dtype)


def down_partial(ids_t, weighted_t, tokens, experts, hidden):
    total, features = tokens.shape
    return pl.pallas_call(
        functools.partial(down_kernel, hidden),
        grid=(experts * hidden // BLOCK,),
        in_specs=[
            pl.BlockSpec((2, total), lambda i: (0, 0)),
            pl.BlockSpec((2 * hidden, total), lambda i: (0, 0)),
            pl.BlockSpec((total, features), lambda i: (0, 0)),
        ],
        out_specs=pl.BlockSpec((BLOCK, features), lambda i: (i, 0)),
        out_shape=jax.ShapeDtypeStruct((experts * hidden, features), jnp.bfloat16),
        scratch_shapes=[pltpu.VMEM((BLOCK, total), jnp.bfloat16)],
        compiler_params=params(),
        cost_estimate=pl.CostEstimate(
            flops=2 * experts * hidden * features * total,
            bytes_accessed=2 * features * (total + experts * hidden),
            transcendentals=0,
        ),
    )(ids_t, weighted_t, tokens)


def project_kernel(ids_ref, tokens_ref, weight_ref, out_ref):
    rows, wide = out_ref.shape
    odd = jnp.where(low_half((rows, wide)), 0, 1)
    first = ids_ref[:, 0:1] - odd
    second = ids_ref[:, 1:2] - odd
    sums = [jnp.zeros((rows, wide), jnp.float32) for _ in range(2)]
    for start in range(0, weight_ref.shape[0], BLOCK):
        product = lax.dot_general(
            tokens_ref[...],
            weight_ref[start : start + BLOCK, :],
            (((1,), (1,)), ((), ())),
            preferred_element_type=jnp.float32,
        )
        for at in range(0, BLOCK, wide):
            part = product[:, at : at + wide]
            number = (start + at) // wide * 2
            sums[0] = jnp.where(first == number, part, sums[0])
            sums[1] = jnp.where(second == number, part, sums[1])
    folded = [value + pltpu.roll(value, wide // 2, 1) for value in sums]
    out_ref[...] = jnp.where(odd == 0, folded[0], folded[1])


def project(ids, tokens, weight, hidden):
    total, features = tokens.shape
    return pl.pallas_call(
        project_kernel,
        grid=(total // BLOCK,),
        in_specs=[
            pl.BlockSpec((BLOCK, 2), lambda i: (i, 0)),
            pl.BlockSpec((BLOCK, features), lambda i: (i, 0)),
            pl.BlockSpec(weight.shape, lambda i: (0, 0)),
        ],
        out_specs=pl.BlockSpec((BLOCK, 2 * hidden), lambda i: (i, 0)),
        out_shape=jax.ShapeDtypeStruct((total, 2 * hidden), jnp.float32),
        compiler_params=params(),
        cost_estimate=pl.CostEstimate(
            flops=2 * weight.shape[0] * features * total,
            bytes_accessed=2 * features * (total + weight.shape[0]),
            transcendentals=0,
        ),
    )(ids, tokens, weight)


def hidden_kernel(parts_ref, gates_ref, activation_ref, slope_ref, hidden_ref, gate_ref):
    projected = parts_ref[0]
    for source in range(1, parts_ref.shape[0]):
        projected = projected + parts_ref[source]
    low = low_half(projected.shape)
    gate_terms = activation_ref[...] * projected
    first = jnp.sum(jnp.where(low, gate_terms, 0.0), axis=1, keepdims=True)
    second = jnp.sum(jnp.where(low, 0.0, gate_terms), axis=1, keepdims=True)
    gate_ref[:, 0:1] = first.astype(gate_ref.dtype)
    gate_ref[:, 1:2] = second.astype(gate_ref.dtype)
    hidden_ref[...] = (gates_ref[...] * projected * slope_ref[...]).astype(hidden_ref.dtype)


def input_kernel(ids_ref, hidden_ref, weight_ref, out_ref, spread):
    rows, wide = hidden_ref.shape
    low = low_half((rows, wide))
    odd = jnp.where(low, 0, 1)
    first = ids_ref[:, 0:1] - odd
    second = ids_ref[:, 1:2] - odd
    values = hidden_ref[...].astype(jnp.float32)
    swapped = pltpu.roll(values, wide // 2, 1)
    one = jnp.where(low, values, swapped)
    two = jnp.where(low, swapped, values)
    for start in range(0, weight_ref.shape[0], wide):
        number = start // wide * 2
        spread[:, start : start + wide] = jnp.where(
            first == number, one, jnp.where(second == number, two, 0.0)
        ).astype(jnp.bfloat16)
    out_ref[...] = jnp.dot(
        spread[...], weight_ref[...], preferred_element_type=jnp.float32
    ).astype(out_ref.dtype)


def input_rows(ids, hidden_grad, weight):
    total, wide = hidden_grad.shape
    features = weight.shape[1]
    return pl.pallas_call(
        input_kernel,
        grid=(total // BLOCK,),
        in_specs=[
            pl.BlockSpec((BLOCK, 2), lambda i: (i, 0)),
            pl.BlockSpec((BLOCK, wide), lambda i: (i, 0)),
            pl.BlockSpec(weight.shape, lambda i: (0, 0)),
        ],
        out_specs=pl.BlockSpec((BLOCK, features), lambda i: (i, 0)),
        out_shape=jax.ShapeDtypeStruct((total, features), jnp.bfloat16),
        scratch_shapes=[pltpu.VMEM((BLOCK, weight.shape[0]), jnp.bfloat16)],
        compiler_params=params(),
        cost_estimate=pl.CostEstimate(
            flops=2 * weight.shape[0] * features * total,
            bytes_accessed=2 * features * (total + weight.shape[0]),
            transcendentals=0,
        ),
    )(ids, hidden_grad, weight)


def body(token_grads, router_gates, expert_ids, saved_hidden, up_weight, down_weight):
    tok_count, model_width = token_grads.shape
    local_experts, hidden = up_weight.shape[:2]
    experts = local_experts * lax.axis_size("far") * lax.axis_size("near")
    members = lax.axis_size(GROUP)
    wide = 2 * hidden

    def everywhere(weight):
        mine = lax.all_to_all(weight, "near", split_axis=2, concat_axis=0, tiled=True)
        full = lax.all_gather(mine, "far", axis=0, tiled=True)
        return full.reshape(experts * hidden, full.shape[2])

    gates = router_gates.astype(jnp.float32)
    gates = jnp.where(low_half((tok_count, wide)), gates[:, 0:1], gates[:, 1:2])
    activation, slope = gelu_parts(saved_hidden.astype(jnp.float32))
    weighted = (gates * activation).astype(jnp.bfloat16)
    tokens = lax.all_to_all(token_grads, GROUP, split_axis=1, concat_axis=0, tiled=True)
    ids = lax.all_gather(expert_ids, GROUP, axis=0, tiled=True)
    weighted = lax.all_gather(weighted, GROUP, axis=0, tiled=True)
    down_full = everywhere(down_weight)
    up_full = everywhere(up_weight)

    partial_value = down_partial(
        ids.T, weighted.T.astype(jnp.float32), tokens, experts, hidden
    ).reshape(experts, hidden, tokens.shape[1])
    far_sum = lax.psum_scatter(partial_value, "far", scatter_dimension=0, tiled=True)
    down_grads = lax.all_to_all(far_sum, "near", split_axis=0, concat_axis=2, tiled=True)

    parts = project(ids, tokens, down_full, hidden).reshape(members, tok_count, wide)
    parts = lax.all_to_all(parts, GROUP, split_axis=0, concat_axis=0, tiled=True)
    hidden_grad, gate_grads = pl.pallas_call(
        hidden_kernel,
        out_shape=(
            jax.ShapeDtypeStruct((tok_count, wide), jnp.bfloat16),
            jax.ShapeDtypeStruct(router_gates.shape, jnp.bfloat16),
        ),
        compiler_params=params(),
    )(parts, gates, activation, slope)
    hidden_grad = lax.all_gather(hidden_grad, GROUP, axis=0, tiled=True)
    rows = input_rows(ids, hidden_grad, up_full)
    input_grads = lax.all_to_all(rows, GROUP, split_axis=0, concat_axis=1, tiled=True)
    return (input_grads, gate_grads, down_grads)


def solution(mesh):
    sizes = [mesh.shape[name] for name in ("expert", "inner", "outer")]
    split = Mesh(
        mesh.devices.reshape(sizes[0] // 2, 2, *sizes[1:]), ("far", "near", "inner", "outer")
    )
    rows = P(("far", "near", "inner", "outer"), None)
    weights = P(("far", "near"), None, ("inner", "outer"))
    return jax.shard_map(
        body,
        mesh=split,
        in_specs=(rows, rows, rows, rows, weights, weights),
        out_specs=(rows, rows, weights),
        check_vma=False,
    )
```

```python
import functools
import jax
import jax.numpy as jnp
from jax import lax
from jax.experimental import pallas as pl
from jax.experimental.pallas import tpu as pltpu
from jax.sharding import Mesh, PartitionSpec as P

root_half = 0.7071067811865476
inv_root_tau = 0.3989422804014327
GROUP = ("inner", "outer", "near")
BLOCK = 256
MIB = 1 << 20
CHAIN = ((0, 1, 2, 3), (1, 0, 2, 3), (3, 2, 0, 1), (3, 2, 1, 0))
SIDES = ((0, 1), (1, 0), (2, 3), (3, 2))
MIDDLE = ((1, 2), (2, 1))
OUTWARD = ((1, 0), (2, 3))
INWARD = ((0, 1), (3, 2))
SWAP = ((0, 1), (1, 0))


def gelu_parts(preact):
    cumulative = 0.5 * (1.0 + lax.erf(preact * root_half))
    density = inv_root_tau * jnp.exp(-0.5 * preact * preact)
    return (preact * cumulative, cumulative + preact * density)


def params():
    return pltpu.CompilerParams(vmem_limit_bytes=40 * MIB)


def cost(rows, inner, columns):
    return pl.CostEstimate(
        flops=2 * rows * inner * columns,
        bytes_accessed=2 * (rows * inner + inner * columns + rows * columns),
        transcendentals=0,
    )


def low_half(shape):
    return lax.broadcasted_iota(jnp.int32, shape, len(shape) - 1) < shape[-1] // 2


def columns_of(pair, wide):
    wanted = lax.broadcasted_iota(jnp.int32, (2, wide), 0)
    return [
        lax.dot_general(
            pair.astype(jnp.bfloat16),
            jnp.where(wanted == k, 1.0, 0.0).astype(jnp.bfloat16),
            (((0,), (0,)), ((), ())),
            preferred_element_type=jnp.float32,
        )
        for k in range(2)
    ]


def prepare_kernel(ids_ref, gates_ref, preact_ref, sent_ref, activation_ref, scaled_ref):
    rows, wide = preact_ref.shape
    activation, slope = gelu_parts(preact_ref[...].astype(jnp.float32))
    gates = jnp.where(low_half((rows, wide)), *columns_of(gates_ref[...], wide))
    activation_ref[...] = activation
    scaled_ref[...] = gates * slope
    sent_ref[0:rows, :] = (gates * activation).astype(jnp.bfloat16)
    sent_ref[rows:, :] = jnp.zeros((sent_ref.shape[0] - rows, wide), jnp.bfloat16)
    sent_ref[rows : rows + 2, :] = ids_ref[...].astype(jnp.bfloat16)


def down_kernel(hidden, ids_ref, weighted_ref, tokens_ref, *refs):
    out_refs, spread = refs[:-1], refs[-1]
    turned = weighted_ref[...].astype(jnp.float32).T
    each = BLOCK // hidden
    at = 0
    for out_ref in out_refs:
        for start in range(0, out_ref.shape[0], BLOCK):
            for expert in range(each):
                spread[expert * hidden : (expert + 1) * hidden, :] = jnp.where(
                    ids_ref[0:1, :] == at + expert,
                    turned[0:hidden, :],
                    jnp.where(ids_ref[1:2, :] == at + expert, turned[hidden:, :], 0.0),
                ).astype(jnp.bfloat16)
            at += each
            out_ref[start : start + BLOCK, :] = jnp.dot(
                spread[...], tokens_ref[...], preferred_element_type=jnp.float32
            ).astype(out_ref.dtype)


def down_partial(ids, weighted, tokens, rows, count):
    total, features = tokens.shape
    return pl.pallas_call(
        functools.partial(down_kernel, weighted.shape[1] // 2),
        out_shape=[jax.ShapeDtypeStruct((rows // count, features), jnp.bfloat16)] * count,
        scratch_shapes=[pltpu.VMEM((BLOCK, total), jnp.bfloat16)],
        compiler_params=params(),
        cost_estimate=cost(rows, total, features),
    )(ids, weighted, tokens)


def join(pieces, piece_refs, full):
    at = start = 0
    for terms in pieces:
        value = piece_refs[at][...]
        for ref in piece_refs[at + 1 : at + terms]:
            value = value + ref[...]
        full[start : start + value.shape[0], :] = value
        at, start = at + terms, start + value.shape[0]


def project_kernel(pieces, ids_ref, tokens_ref, *refs):
    piece_refs, out_ref, full = refs[:-2], refs[-2], refs[-1]
    pl.when(pl.program_id(0) == 0)(lambda: join(pieces, piece_refs, full))
    rows, wide = out_ref.shape
    low = low_half((rows, wide))
    odd = jnp.where(low, 0.0, 1.0)
    first, second = [value - odd for value in columns_of(ids_ref[...], wide)]
    sums = [jnp.zeros((rows, wide), jnp.float32) for _ in range(2)]
    for start in range(0, full.shape[0], BLOCK):
        product = lax.dot_general(
            tokens_ref[...],
            full[start : start + BLOCK, :],
            (((1,), (1,)), ((), ())),
            preferred_element_type=jnp.float32,
        )
        for at in range(0, BLOCK, wide):
            part = product[:, at : at + wide]
            number = (start + at) // wide * 2.0
            sums[0] = jnp.where(first == number, part, sums[0])
            sums[1] = jnp.where(second == number, part, sums[1])
    folded = [value + pltpu.roll(value, wide // 2, 1) for value in sums]
    out_ref[...] = jnp.where(low, folded[0], folded[1])


def whole_block(array):
    return pl.BlockSpec(array.shape, lambda i: (0, 0))


def project(ids, tokens, pieces, hidden):
    total, features = tokens.shape
    flat = [term for terms in pieces for term in terms]
    rows = sum(terms[0].shape[0] for terms in pieces)
    return pl.pallas_call(
        functools.partial(project_kernel, [len(terms) for terms in pieces]),
        grid=(total // BLOCK,),
        in_specs=[
            pl.BlockSpec((2, BLOCK), lambda i: (0, i)),
            pl.BlockSpec((BLOCK, features), lambda i: (i, 0)),
            *map(whole_block, flat),
        ],
        out_specs=pl.BlockSpec((BLOCK, 2 * hidden), lambda i: (i, 0)),
        out_shape=jax.ShapeDtypeStruct((total, 2 * hidden), jnp.float32),
        scratch_shapes=[pltpu.VMEM((rows, features), jnp.bfloat16)],
        compiler_params=params(),
        cost_estimate=cost(total, features, rows),
    )(ids, tokens, *flat)


def hidden_kernel(parts_ref, activation_ref, scaled_ref, hidden_ref, gate_ref):
    projected = parts_ref[0]
    for source in range(1, parts_ref.shape[0]):
        projected = projected + parts_ref[source]
    wide = projected.shape[1]
    half = lax.broadcasted_iota(jnp.int32, (8, wide), 1) // (wide // 2)
    wanted = lax.broadcasted_iota(jnp.int32, (8, wide), 0)
    sums = lax.dot_general(
        jnp.where(wanted == half, 1.0, 0.0),
        activation_ref[...] * projected,
        (((1,), (1,)), ((), ())),
        precision=lax.Precision.HIGHEST,
        preferred_element_type=jnp.float32,
    )
    gate_ref[...] = sums[0:2, :].astype(gate_ref.dtype)
    hidden_ref[...] = (projected * scaled_ref[...]).astype(hidden_ref.dtype)


def input_kernel(pieces, ids_ref, hidden_ref, *refs):
    piece_refs, out_ref, full, spread = refs[:-3], refs[-3], refs[-2], refs[-1]
    pl.when(pl.program_id(0) == 0)(lambda: join(pieces, piece_refs, full))
    rows, wide = hidden_ref.shape
    low = low_half((rows, wide))
    odd = jnp.where(low, 0.0, 1.0)
    first, second = [value - odd for value in columns_of(ids_ref[...], wide)]
    values = hidden_ref[...].astype(jnp.float32)
    swapped = pltpu.roll(values, wide // 2, 1)
    one = jnp.where(low, values, swapped)
    two = jnp.where(low, swapped, values)
    for start in range(0, full.shape[0], wide):
        number = start // wide * 2.0
        spread[:, start : start + wide] = jnp.where(
            first == number, one, jnp.where(second == number, two, 0.0)
        ).astype(jnp.bfloat16)
    out_ref[...] = jnp.dot(
        spread[...], full[...], preferred_element_type=jnp.float32
    ).astype(out_ref.dtype)


def input_rows(ids, hidden_grad, pieces):
    total, wide = hidden_grad.shape
    flat = [term for terms in pieces for term in terms]
    rows, features = sum(terms[0].shape[0] for terms in pieces), flat[0].shape[1]
    return pl.pallas_call(
        functools.partial(input_kernel, [len(terms) for terms in pieces]),
        grid=(total // BLOCK,),
        in_specs=[
            pl.BlockSpec((2, BLOCK), lambda i: (0, i)),
            pl.BlockSpec((BLOCK, wide), lambda i: (i, 0)),
            *map(whole_block, flat),
        ],
        out_specs=pl.BlockSpec((BLOCK, features), lambda i: (i, 0)),
        out_shape=jax.ShapeDtypeStruct((total, features), jnp.bfloat16),
        scratch_shapes=[
            pltpu.VMEM((rows, features), jnp.bfloat16),
            pltpu.VMEM((BLOCK, rows), jnp.bfloat16),
        ],
        compiler_params=params(),
        cost_estimate=cost(total, rows, features),
    )(ids, hidden_grad, *flat)


def gather_far(mine):
    if lax.axis_size("far") != len(CHAIN):
        return [(lax.all_gather(mine, "far", axis=0, tiled=True),)]
    beside = lax.ppermute(mine, "far", SIDES)
    across = lax.ppermute(mine, "far", MIDDLE)
    across_far = lax.ppermute(beside, "far", MIDDLE)
    second = lax.ppermute(across, "far", OUTWARD)
    third = lax.ppermute(across_far, "far", OUTWARD)
    return [(mine,), (beside,), (across, second), (across_far, third)]


def add(*terms):
    return sum(term.astype(jnp.float32) for term in terms).astype(jnp.bfloat16)


def scatter_far(blocks):
    if lax.axis_size("far") != len(CHAIN):
        return lax.psum_scatter(blocks[0], "far", scatter_dimension=0, tiled=True)
    own, beside, second, third = blocks
    third = add(third, lax.ppermute(third, "far", INWARD))
    second = add(second, lax.ppermute(second, "far", INWARD))
    beside = add(beside, lax.ppermute(third, "far", MIDDLE))
    across = lax.ppermute(second, "far", MIDDLE)
    return add(own, across, lax.ppermute(beside, "far", SIDES))


def gather_group(value):
    value = value[None]
    for axis in reversed(GROUP):
        if lax.axis_size(axis) == 2:
            other = lax.ppermute(value, axis, SWAP)
            swapped = lax.axis_index(axis) == 1
            value = jnp.concatenate(
                [jnp.where(swapped, other, value), jnp.where(swapped, value, other)], axis=0
            )
        else:
            value = lax.all_gather(value, axis, axis=0, tiled=True)
    return value


def body(token_grads, router_gates, expert_ids, saved_hidden, up_weight, down_weight):
    tok_count, model_width = token_grads.shape
    local_experts, hidden, width = up_weight.shape
    far_count, near_count = lax.axis_size("far"), lax.axis_size("near")
    experts = local_experts * far_count * near_count
    members = lax.axis_size(GROUP)
    total, wide, half = members * tok_count, 2 * hidden, width // near_count
    rows = local_experts * hidden
    far, near = lax.axis_index("far"), lax.axis_index("near")

    def halves(weight):
        flat = weight.reshape(rows, width)
        own = lax.dynamic_slice_in_dim(flat, near * half, half, axis=1)
        other = lax.dynamic_slice_in_dim(flat, (1 - near) * half, half, axis=1)
        return own, lax.ppermute(other, "near", SWAP)

    down_own, down_other = halves(down_weight)
    up_own, up_other = halves(up_weight)
    down_pieces = gather_far(down_own) + gather_far(down_other)
    up_pieces = gather_far(up_own) + gather_far(up_other)

    sent, activation, scaled = pl.pallas_call(
        prepare_kernel,
        out_shape=(
            jax.ShapeDtypeStruct((tok_count + 16, wide), jnp.bfloat16),
            jax.ShapeDtypeStruct((tok_count, wide), jnp.float32),
            jax.ShapeDtypeStruct((tok_count, wide), jnp.float32),
        ),
        compiler_params=params(),
    )(expert_ids.T, router_gates.T, saved_hidden)
    tokens = lax.all_to_all(token_grads, GROUP, split_axis=1, concat_axis=0, tiled=True)
    sent = gather_group(sent)
    weighted = sent[:, :tok_count].reshape(total, wide)
    ids = sent[:, tok_count : tok_count + 2].astype(jnp.int32)
    ids = jnp.swapaxes(ids, 0, 1).reshape(2, total)
    far_place = ids // (near_count * local_experts)
    if far_count == len(CHAIN):
        places = jnp.asarray(CHAIN, jnp.int32)[far]
        far_place = sum(jnp.where(far_place == at, places[at], 0) for at in range(len(CHAIN)))
    near_place = (ids // local_experts % near_count) ^ near
    local = ids % local_experts
    place = (near_place * far_count + far_place) * local_experts + local
    grad_place = (far_place * near_count + near_place) * local_experts + local

    blocks = down_partial(
        grad_place, weighted, tokens, experts * hidden,
        len(CHAIN) if far_count == len(CHAIN) else 1,
    )
    sums = scatter_far(blocks)
    kept, passed = sums[:rows], lax.ppermute(sums[rows:], "near", SWAP)
    down_grads = jnp.concatenate(
        [jnp.where(near == 0, kept, passed), jnp.where(near == 0, passed, kept)], axis=1
    ).reshape(down_weight.shape)

    parts = project(place, tokens, down_pieces, hidden).reshape(members, tok_count, wide)
    parts = lax.all_to_all(parts, GROUP, split_axis=0, concat_axis=0, tiled=True)
    hidden_grad, gate_grads = pl.pallas_call(
        hidden_kernel,
        out_shape=(
            jax.ShapeDtypeStruct((tok_count, wide), jnp.bfloat16),
            jax.ShapeDtypeStruct((2, tok_count), jnp.bfloat16),
        ),
        compiler_params=params(),
    )(parts, activation, scaled)
    hidden_grad = gather_group(hidden_grad).reshape(total, wide)
    rows_back = input_rows(place, hidden_grad, up_pieces)
    input_grads = lax.all_to_all(rows_back, GROUP, split_axis=0, concat_axis=1, tiled=True)
    return (input_grads, gate_grads.T, down_grads)


def solution(mesh):
    sizes = [mesh.shape[name] for name in ("expert", "inner", "outer")]
    split = Mesh(
        mesh.devices.reshape(sizes[0] // 2, 2, *sizes[1:]), ("far", "near", "inner", "outer")
    )
    rows = P(("far", "near", "inner", "outer"), None)
    weights = P(("far", "near"), None, ("inner", "outer"))
    return jax.shard_map(
        body,
        mesh=split,
        in_specs=(rows, rows, rows, rows, weights, weights),
        out_specs=(rows, rows, weights),
        check_vma=False,
    )
```

```python
import functools
import jax
import jax.numpy as jnp
from jax import lax
from jax.experimental import pallas as pl
from jax.experimental.pallas import tpu as pltpu
from jax.sharding import Mesh, PartitionSpec as P

root_half = 0.7071067811865476
inv_root_tau = 0.3989422804014327
GROUP = ("inner", "outer", "near")
NEAR = 4
BLOCK = 256
EXTRA = 16
MIB = 1 << 20


def gelu_parts(preact):
    cumulative = 0.5 * (1.0 + lax.erf(preact * root_half))
    density = inv_root_tau * jnp.exp(-0.5 * preact * preact)
    return (preact * cumulative, cumulative + preact * density)


def params():
    return pltpu.CompilerParams(vmem_limit_bytes=40 * MIB)


def cost(rows, inner, columns):
    return pl.CostEstimate(
        flops=2 * rows * inner * columns,
        bytes_accessed=2 * (rows * inner + inner * columns + rows * columns),
        transcendentals=0,
    )


def low_half(shape):
    return lax.broadcasted_iota(jnp.int32, shape, len(shape) - 1) < shape[-1] // 2


def columns_of(pair, wide):
    wanted = lax.broadcasted_iota(jnp.int32, (2, wide), 0)
    return [
        lax.dot_general(
            pair.astype(jnp.bfloat16),
            jnp.where(wanted == k, 1.0, 0.0).astype(jnp.bfloat16),
            (((0,), (0,)), ((), ())),
            preferred_element_type=jnp.float32,
        )
        for k in range(2)
    ]


def prepare_kernel(gates_ref, preact_ref, weighted_ref, activation_ref, scaled_ref):
    rows, wide = preact_ref.shape
    activation, slope = gelu_parts(preact_ref[...].astype(jnp.float32))
    gates = jnp.where(low_half((rows, wide)), *columns_of(gates_ref[...], wide))
    activation_ref[...] = activation
    scaled_ref[...] = gates * slope
    weighted_ref[...] = (gates * activation).astype(jnp.bfloat16)


def weights_kernel(down_ref, up_ref, out_ref):
    rows = out_ref.shape[2]
    out_ref[0, 0] = down_ref[...].reshape(rows, out_ref.shape[3])
    out_ref[0, 1] = up_ref[...].reshape(rows, out_ref.shape[3])


def pack_weights(down, up):
    local_experts, hidden, width = down.shape
    piece = width // NEAR
    spec = pl.BlockSpec((local_experts, hidden, piece), lambda i: (0, 0, i))
    rows = local_experts * hidden
    return pl.pallas_call(
        weights_kernel,
        grid=(NEAR,),
        in_specs=[spec, spec],
        out_specs=pl.BlockSpec((1, 2, rows, piece), lambda i: (i, 0, 0, 0)),
        out_shape=jax.ShapeDtypeStruct((NEAR, 2, rows, piece), jnp.bfloat16),
        compiler_params=params(),
    )(down, up)


def pack_kernel(ids_ref, tokens_ref, out_ref):
    blocks, rows, features = out_ref.shape
    rows -= EXTRA
    ids = ids_ref[...].astype(jnp.bfloat16)
    for block in range(blocks):
        out_ref[block, 0:rows, :] = tokens_ref[:, block * features : (block + 1) * features]
        out_ref[block, rows:, :] = jnp.zeros((EXTRA, features), jnp.bfloat16)
        out_ref[block, rows : rows + 2, 0:rows] = ids


def pack_tokens(ids, tokens, members):
    rows, width = tokens.shape
    features = width // members
    each = members // 4
    return pl.pallas_call(
        pack_kernel,
        grid=(4,),
        in_specs=[
            pl.BlockSpec(ids.shape, lambda i: (0, 0)),
            pl.BlockSpec((rows, each * features), lambda i: (0, i)),
        ],
        out_specs=pl.BlockSpec((each, rows + EXTRA, features), lambda i: (i, 0, 0)),
        out_shape=jax.ShapeDtypeStruct((members, rows + EXTRA, features), jnp.bfloat16),
        compiler_params=params(),
    )(ids, tokens)


def unpack_kernel(parts_ref, out_ref):
    blocks, _, features = parts_ref.shape
    for block in range(blocks):
        out_ref[:, block * features : (block + 1) * features] = parts_ref[block]


def unpack_tokens(parts):
    members, rows, features = parts.shape
    each = members // 4
    return pl.pallas_call(
        unpack_kernel,
        grid=(4,),
        in_specs=[pl.BlockSpec((each, rows, features), lambda i: (i, 0, 0))],
        out_specs=pl.BlockSpec((rows, each * features), lambda i: (0, i)),
        out_shape=jax.ShapeDtypeStruct((rows, members * features), jnp.bfloat16),
        compiler_params=params(),
    )(parts)


def down_kernel(received_ref, weighted_ref, out_ref, turned, numbers, spread):
    sources, rows, wide = weighted_ref.shape
    hidden, each = wide // 2, BLOCK // (wide // 2)

    @pl.when(pl.program_id(0) == 0)
    def _():
        for source in range(sources):
            at = slice(source * rows, (source + 1) * rows)
            turned[:, at] = weighted_ref[source].astype(jnp.float32).T
            numbers[:, at] = received_ref[source, rows : rows + 2, 0:rows].astype(jnp.float32)

    first = pl.program_id(0) * each
    for expert in range(each):
        number = (first + expert).astype(jnp.float32)
        spread[expert * hidden : (expert + 1) * hidden, :] = jnp.where(
            numbers[0:1, :] == number,
            turned[0:hidden, :],
            jnp.where(numbers[1:2, :] == number, turned[hidden:, :], 0.0),
        ).astype(jnp.bfloat16)
    tokens = received_ref[:, 0:rows, :].reshape(sources * rows, received_ref.shape[2])
    out_ref[...] = jnp.dot(
        spread[...], tokens, preferred_element_type=jnp.float32
    ).astype(out_ref.dtype)


def down_partial(received, weighted, rows):
    sources, _, features = received.shape
    total, wide = sources * weighted.shape[1], weighted.shape[2]
    return pl.pallas_call(
        down_kernel,
        grid=(rows // BLOCK,),
        in_specs=[
            pl.BlockSpec(received.shape, lambda i: (0, 0, 0)),
            pl.BlockSpec(weighted.shape, lambda i: (0, 0, 0)),
        ],
        out_specs=pl.BlockSpec((BLOCK, features), lambda i: (i, 0)),
        out_shape=jax.ShapeDtypeStruct((rows, features), jnp.bfloat16),
        scratch_shapes=[
            pltpu.VMEM((wide, total), jnp.float32),
            pltpu.VMEM((2, total), jnp.float32),
            pltpu.VMEM((BLOCK, total), jnp.bfloat16),
        ],
        compiler_params=params(),
        cost_estimate=cost(rows, total, features),
    )(received, weighted)


def lane_numbers(received_ref, rows, wide):
    low = low_half((received_ref.shape[0] * rows, wide))
    found = [
        columns_of(received_ref[source, rows : rows + 2, 0:rows], wide)
        for source in range(received_ref.shape[0])
    ]
    odd = jnp.where(low, 0.0, 1.0)
    return low, *[jnp.concatenate([pair[k] for pair in found]) - odd for k in range(2)]


def project_kernel(received_ref, weight_ref, out_ref):
    sources, rows, wide = out_ref.shape
    low, first, second = lane_numbers(received_ref, rows, wide)
    tokens = received_ref[:, 0:rows, :].reshape(sources * rows, received_ref.shape[2])
    sums = [jnp.zeros((sources * rows, wide), jnp.float32) for _ in range(2)]
    for start in range(0, weight_ref.shape[0], BLOCK):
        product = lax.dot_general(
            tokens,
            weight_ref[start : start + BLOCK, :],
            (((1,), (1,)), ((), ())),
            preferred_element_type=jnp.float32,
        )
        for at in range(0, BLOCK, wide):
            part = product[:, at : at + wide]
            number = (start + at) // wide * 2.0
            sums[0] = jnp.where(first == number, part, sums[0])
            sums[1] = jnp.where(second == number, part, sums[1])
    folded = [value + pltpu.roll(value, wide // 2, 1) for value in sums]
    value = jnp.where(low, folded[0], folded[1]).astype(out_ref.dtype)
    out_ref[...] = value.reshape(out_ref.shape)


def project(received, weight, hidden):
    sources, rows, features = received.shape
    return pl.pallas_call(
        project_kernel,
        grid=(sources // 2,),
        in_specs=[
            pl.BlockSpec((2, rows, features), lambda i: (i, 0, 0)),
            pl.BlockSpec(weight.shape, lambda i: (0, 0)),
        ],
        out_specs=pl.BlockSpec((2, rows - EXTRA, 2 * hidden), lambda i: (i, 0, 0)),
        out_shape=jax.ShapeDtypeStruct((sources, rows - EXTRA, 2 * hidden), jnp.bfloat16),
        compiler_params=params(),
        cost_estimate=cost(sources * rows, features, weight.shape[0]),
    )(received, weight)


def hidden_kernel(parts_ref, activation_ref, scaled_ref, hidden_ref, gate_ref):
    projected = parts_ref[0].astype(jnp.float32)
    for source in range(1, parts_ref.shape[0]):
        projected = projected + parts_ref[source].astype(jnp.float32)
    wide = projected.shape[1]
    half = lax.broadcasted_iota(jnp.int32, (8, wide), 1) // (wide // 2)
    wanted = lax.broadcasted_iota(jnp.int32, (8, wide), 0)
    sums = lax.dot_general(
        jnp.where(wanted == half, 1.0, 0.0),
        activation_ref[...] * projected,
        (((1,), (1,)), ((), ())),
        precision=lax.Precision.HIGHEST,
        preferred_element_type=jnp.float32,
    )
    gate_ref[...] = sums[0:2, :].astype(gate_ref.dtype)
    hidden = (projected * scaled_ref[...]).astype(hidden_ref.dtype)
    for source in range(hidden_ref.shape[0]):
        hidden_ref[source] = hidden


def input_kernel(received_ref, hidden_ref, weight_ref, out_ref, spread):
    sources, rows, wide = hidden_ref.shape
    low, first, second = lane_numbers(received_ref, rows, wide)
    values = hidden_ref[...].reshape(sources * rows, wide).astype(jnp.float32)
    swapped = pltpu.roll(values, wide // 2, 1)
    one = jnp.where(low, values, swapped)
    two = jnp.where(low, swapped, values)
    for start in range(0, weight_ref.shape[0], wide):
        number = start // wide * 2.0
        spread[:, start : start + wide] = jnp.where(
            first == number, one, jnp.where(second == number, two, 0.0)
        ).astype(jnp.bfloat16)
    out_ref[...] = (
        jnp.dot(spread[...], weight_ref[...], preferred_element_type=jnp.float32)
        .astype(out_ref.dtype)
        .reshape(out_ref.shape)
    )


def input_rows(received, hidden_grad, weight):
    sources, rows, wide = hidden_grad.shape
    features = weight.shape[1]
    return pl.pallas_call(
        input_kernel,
        grid=(sources // 2,),
        in_specs=[
            pl.BlockSpec((2, rows + EXTRA, features), lambda i: (i, 0, 0)),
            pl.BlockSpec((2, rows, wide), lambda i: (i, 0, 0)),
            pl.BlockSpec(weight.shape, lambda i: (0, 0)),
        ],
        out_specs=pl.BlockSpec((2, rows, features), lambda i: (i, 0, 0)),
        out_shape=jax.ShapeDtypeStruct((sources, rows, features), jnp.bfloat16),
        scratch_shapes=[pltpu.VMEM((2 * rows, weight.shape[0]), jnp.bfloat16)],
        compiler_params=params(),
        cost_estimate=cost(sources * rows, weight.shape[0], features),
    )(received, hidden_grad, weight)


def exchange(value, axes):
    return lax.all_to_all(value, axes, split_axis=0, concat_axis=0, tiled=True)


def body(token_grads, router_gates, expert_ids, saved_hidden, up_weight, down_weight):
    tok_count = token_grads.shape[0]
    local_experts, hidden, width = up_weight.shape
    members = lax.axis_size(GROUP)
    wide, features = 2 * hidden, width // NEAR
    own_rows = local_experts * hidden
    all_rows = own_rows * NEAR * lax.axis_size("far")

    pieces = exchange(pack_weights(down_weight, up_weight), "near")
    down_full, up_full = [
        lax.all_gather(pieces[:, k].reshape(NEAR * own_rows, features), "far", axis=0, tiled=True)
        for k in range(2)
    ]
    received = exchange(pack_tokens(expert_ids.T, token_grads, members), GROUP)
    weighted, activation, scaled = pl.pallas_call(
        prepare_kernel,
        out_shape=(
            jax.ShapeDtypeStruct((tok_count, wide), jnp.bfloat16),
            jax.ShapeDtypeStruct((tok_count, wide), jnp.float32),
            jax.ShapeDtypeStruct((tok_count, wide), jnp.float32),
        ),
        compiler_params=params(),
    )(router_gates.T, saved_hidden)

    parts = project(received, down_full, hidden)
    weighted = jnp.broadcast_to(weighted, parts.shape)
    back = exchange(jnp.concatenate([parts, weighted], axis=1), GROUP)
    parts, weighted = back[:, :tok_count], back[:, tok_count:]
    hidden_grad, gate_grads = pl.pallas_call(
        hidden_kernel,
        out_shape=(
            jax.ShapeDtypeStruct((members, tok_count, wide), jnp.bfloat16),
            jax.ShapeDtypeStruct((2, tok_count), jnp.bfloat16),
        ),
        compiler_params=params(),
    )(parts, activation, scaled)
    hidden_grad = exchange(hidden_grad, GROUP)
    rows_back = exchange(input_rows(received, hidden_grad, up_full), GROUP)
    input_grads = unpack_tokens(rows_back)

    partial_value = down_partial(received, weighted, all_rows)
    sums = lax.psum_scatter(partial_value, "far", scatter_dimension=0, tiled=True)
    sums = exchange(sums.reshape(NEAR, own_rows, features), "near")
    down_grads = jnp.swapaxes(sums, 0, 1).reshape(down_weight.shape)
    return (input_grads, gate_grads.T, down_grads)


def solution(mesh):
    sizes = [mesh.shape[name] for name in ("expert", "inner", "outer")]
    split = Mesh(
        mesh.devices.reshape(sizes[0] // NEAR, NEAR, *sizes[1:]),
        ("far", "near", "inner", "outer"),
    )
    rows = P(("far", "near", "inner", "outer"), None)
    weights = P(("far", "near"), None, ("inner", "outer"))
    return jax.shard_map(
        body,
        mesh=split,
        in_specs=(rows, rows, rows, rows, weights, weights),
        out_specs=(rows, rows, weights),
        check_vma=False,
    )
```

```python
import functools
import jax
import jax.numpy as jnp
from jax import lax
from jax.experimental import pallas as pl
from jax.experimental.pallas import tpu as pltpu
from jax.sharding import Mesh, PartitionSpec as P

root_half = 0.7071067811865476
inv_root_tau = 0.3989422804014327
GROUP = ("inner", "outer", "near")
NEAR = 2
BLOCK = 256
TILE = 16
MIB = 1 << 20
CHAIN = ((0, 1, 2, 3), (1, 0, 2, 3), (3, 2, 0, 1), (3, 2, 1, 0))
SIDES = ((0, 1), (1, 0), (2, 3), (3, 2))
MIDDLE = ((1, 2), (2, 1))
OUTWARD = ((1, 0), (2, 3))
INWARD = ((0, 1), (3, 2))
SWAP = ((0, 1), (1, 0))
DOWN, UP, GRADS = 0, 2, 4


def gelu_parts(preact):
    cumulative = 0.5 * (1.0 + lax.erf(preact * root_half))
    density = inv_root_tau * jnp.exp(-0.5 * preact * preact)
    return (preact * cumulative, cumulative + preact * density)


def params():
    return pltpu.CompilerParams(vmem_limit_bytes=40 * MIB)


def cost(rows, inner, columns):
    return pl.CostEstimate(
        flops=2 * rows * inner * columns,
        bytes_accessed=2 * (rows * inner + inner * columns + rows * columns),
        transcendentals=0,
    )


def low_half(shape):
    return lax.broadcasted_iota(jnp.int32, shape, len(shape) - 1) < shape[-1] // 2


def columns_of(pair, wide):
    wanted = lax.broadcasted_iota(jnp.int32, (2, wide), 0)
    return [
        lax.dot_general(
            pair.astype(jnp.bfloat16),
            jnp.where(wanted == k, 1.0, 0.0).astype(jnp.bfloat16),
            (((0,), (0,)), ((), ())),
            preferred_element_type=jnp.float32,
        )
        for k in range(2)
    ]


def pack_kernel(
    local_experts, far_ref, ids_ref, gates_ref, preact_ref, tokens_ref,
    out_ref, activation_ref, scaled_ref, weighted,
):
    blocks, height, features = out_ref.shape
    rows, wide = preact_ref.shape
    far_count = far_ref.shape[0]
    taken = rows * wide // features

    @pl.when(pl.program_id(0) == 0)
    def _():
        activation, slope = gelu_parts(preact_ref[...].astype(jnp.float32))
        gates = jnp.where(low_half((rows, wide)), *columns_of(gates_ref[...], wide))
        activation_ref[...] = activation
        scaled_ref[...] = gates * slope
        weighted[...] = (gates * activation).astype(jnp.bfloat16)

    ids = ids_ref[...]
    local = lax.rem(ids, local_experts)
    line = lax.div(ids, local_experts)
    far, near = lax.div(line, NEAR), lax.rem(line, NEAR)
    far_place = jnp.zeros_like(far)
    for at in range(far_count):
        far_place = jnp.where(far == at, far_ref[at], far_place)
    for block in range(blocks):
        side = lax.rem(near + block, NEAR)
        places = (
            (side * far_count + far_place) * local_experts + local,
            (far * NEAR + side) * local_experts + local,
            (far_place * NEAR + side) * local_experts + local,
        )
        out_ref[block, 0:rows, :] = tokens_ref[:, block * features : (block + 1) * features]
        for at in range(0, features, wide):
            start = at // wide * taken
            out_ref[block, rows : rows + taken, at : at + wide] = weighted[start : start + taken, :]
        last = height - TILE
        out_ref[block, last:, :] = jnp.zeros((TILE, features), jnp.bfloat16)
        for at, place in zip((DOWN, UP, GRADS), places):
            out_ref[block, last + at : last + at + 2, 0:rows] = place.astype(jnp.bfloat16)


def pack_tokens(far_places, ids, gates, preact, tokens, members, local_experts):
    rows, width = tokens.shape
    features = width // members
    each = members // 4
    height = rows + preact.size // features + TILE
    small = jax.ShapeDtypeStruct(preact.shape, jnp.float32)
    whole = [pl.BlockSpec(array.shape, lambda i: (0, 0)) for array in (ids, gates, preact)]
    return pl.pallas_call(
        functools.partial(pack_kernel, local_experts),
        grid=(4,),
        in_specs=[
            pl.BlockSpec(memory_space=pltpu.SMEM),
            *whole,
            pl.BlockSpec((rows, each * features), lambda i: (0, i)),
        ],
        out_specs=(pl.BlockSpec((each, height, features), lambda i: (i, 0, 0)), whole[2], whole[2]),
        out_shape=(
            jax.ShapeDtypeStruct((members, height, features), jnp.bfloat16), small, small,
        ),
        scratch_shapes=[pltpu.VMEM(preact.shape, jnp.bfloat16)],
        compiler_params=params(),
    )(far_places, ids, gates, preact, tokens)


def unpack_kernel(parts_ref, out_ref):
    blocks, _, features = parts_ref.shape
    for block in range(blocks):
        out_ref[:, block * features : (block + 1) * features] = parts_ref[block]


def unpack_tokens(parts):
    members, rows, features = parts.shape
    each = members // 4
    return pl.pallas_call(
        unpack_kernel,
        grid=(4,),
        in_specs=[pl.BlockSpec((each, rows, features), lambda i: (i, 0, 0))],
        out_specs=pl.BlockSpec((rows, each * features), lambda i: (0, i)),
        out_shape=jax.ShapeDtypeStruct((rows, members * features), jnp.bfloat16),
        compiler_params=params(),
    )(parts)


def places_of(received_ref, source, which, rows):
    at = received_ref.shape[1] - TILE + which
    return received_ref[source, at : at + 2, 0:rows]


def token_rows(received_ref, rows):
    sources, _, features = received_ref.shape
    return received_ref[:, 0:rows, :].reshape(sources * rows, features)


def down_kernel(rows, wide, received_ref, *refs):
    out_refs, (turned, numbers, spread) = refs[:-3], refs[-3:]
    sources, _, features = received_ref.shape
    hidden, each = wide // 2, BLOCK // (wide // 2)
    taken = rows * wide // features
    for source in range(sources):
        weighted = jnp.concatenate(
            [
                received_ref[source, rows : rows + taken, at : at + wide].astype(jnp.float32)
                for at in range(0, features, wide)
            ]
        )
        lanes = slice(source * rows, (source + 1) * rows)
        turned[:, lanes] = weighted.T
        numbers[:, lanes] = places_of(received_ref, source, GRADS, rows).astype(jnp.float32)
    number = 0
    for out_ref in out_refs:
        for start in range(0, out_ref.shape[0], BLOCK):
            for expert in range(each):
                spread[expert * hidden : (expert + 1) * hidden, :] = jnp.where(
                    numbers[0:1, :] == number + expert,
                    turned[0:hidden, :],
                    jnp.where(numbers[1:2, :] == number + expert, turned[hidden:, :], 0.0),
                ).astype(jnp.bfloat16)
            number += each
            out_ref[start : start + BLOCK, :] = jnp.dot(
                spread[...], token_rows(received_ref, rows), preferred_element_type=jnp.float32
            ).astype(out_ref.dtype)


def down_partial(received, rows, wide, total_rows, count):
    sources, _, features = received.shape
    total = sources * rows
    return pl.pallas_call(
        functools.partial(down_kernel, rows, wide),
        out_shape=[jax.ShapeDtypeStruct((total_rows // count, features), jnp.bfloat16)] * count,
        scratch_shapes=[
            pltpu.VMEM((wide, total), jnp.float32),
            pltpu.VMEM((2, total), jnp.float32),
            pltpu.VMEM((BLOCK, total), jnp.bfloat16),
        ],
        compiler_params=params(),
        cost_estimate=cost(total_rows, total, features),
    )(received)


def lane_numbers(received_ref, which, rows, wide):
    sources = received_ref.shape[0]
    low = low_half((sources * rows, wide))
    found = [
        columns_of(places_of(received_ref, source, which, rows), wide)
        for source in range(sources)
    ]
    odd = jnp.where(low, 0.0, 1.0)
    return low, *[jnp.concatenate([pair[k] for pair in found]) - odd for k in range(2)]


def join(pieces, piece_refs, full):
    at = start = 0
    for terms in pieces:
        value = piece_refs[at][...]
        for ref in piece_refs[at + 1 : at + terms]:
            value = value + ref[...]
        full[start : start + value.shape[0], :] = value
        at, start = at + terms, start + value.shape[0]


def project_kernel(pieces, received_ref, *refs):
    piece_refs, out_ref, full = refs[:-2], refs[-2], refs[-1]
    pl.when(pl.program_id(0) == 0)(lambda: join(pieces, piece_refs, full))
    sources, rows, wide = out_ref.shape
    low, first, second = lane_numbers(received_ref, DOWN, rows, wide)
    tokens = token_rows(received_ref, rows)
    sums = [jnp.zeros((sources * rows, wide), jnp.float32) for _ in range(2)]
    for start in range(0, full.shape[0], BLOCK):
        product = lax.dot_general(
            tokens,
            full[start : start + BLOCK, :],
            (((1,), (1,)), ((), ())),
            preferred_element_type=jnp.float32,
        )
        for at in range(0, BLOCK, wide):
            part = product[:, at : at + wide]
            number = (start + at) // wide * 2.0
            sums[0] = jnp.where(first == number, part, sums[0])
            sums[1] = jnp.where(second == number, part, sums[1])
    folded = [value + pltpu.roll(value, wide // 2, 1) for value in sums]
    value = jnp.where(low, folded[0], folded[1]).astype(out_ref.dtype)
    out_ref[...] = value.reshape(out_ref.shape)


def project(received, pieces, rows, wide):
    sources, height, features = received.shape
    flat = [term for terms in pieces for term in terms]
    joined = sum(terms[0].shape[0] for terms in pieces)
    return pl.pallas_call(
        functools.partial(project_kernel, [len(terms) for terms in pieces]),
        grid=(sources // 2,),
        in_specs=[
            pl.BlockSpec((2, height, features), lambda i: (i, 0, 0)),
            *[pl.BlockSpec(term.shape, lambda i: (0, 0)) for term in flat],
        ],
        out_specs=pl.BlockSpec((2, rows, wide), lambda i: (i, 0, 0)),
        out_shape=jax.ShapeDtypeStruct((sources, rows, wide), jnp.bfloat16),
        scratch_shapes=[pltpu.VMEM((joined, features), jnp.bfloat16)],
        compiler_params=params(),
        cost_estimate=cost(sources * rows, features, joined),
    )(received, *flat)


def hidden_kernel(parts_ref, activation_ref, scaled_ref, hidden_ref, gate_ref):
    projected = parts_ref[0].astype(jnp.float32)
    for source in range(1, parts_ref.shape[0]):
        projected = projected + parts_ref[source].astype(jnp.float32)
    wide = projected.shape[1]
    half = lax.broadcasted_iota(jnp.int32, (8, wide), 1) // (wide // 2)
    wanted = lax.broadcasted_iota(jnp.int32, (8, wide), 0)
    sums = lax.dot_general(
        jnp.where(wanted == half, 1.0, 0.0),
        activation_ref[...] * projected,
        (((1,), (1,)), ((), ())),
        precision=lax.Precision.HIGHEST,
        preferred_element_type=jnp.float32,
    )
    gate_ref[...] = sums[0:2, :].astype(gate_ref.dtype)
    hidden = (projected * scaled_ref[...]).astype(hidden_ref.dtype)
    for source in range(hidden_ref.shape[0]):
        hidden_ref[source] = hidden


def input_kernel(received_ref, hidden_ref, weight_ref, out_ref, spread):
    sources, rows, wide = hidden_ref.shape
    low, first, second = lane_numbers(received_ref, UP, rows, wide)
    values = hidden_ref[...].reshape(sources * rows, wide).astype(jnp.float32)
    swapped = pltpu.roll(values, wide // 2, 1)
    one = jnp.where(low, values, swapped)
    two = jnp.where(low, swapped, values)
    for start in range(0, weight_ref.shape[0], wide):
        number = start // wide * 2.0
        spread[:, start : start + wide] = jnp.where(
            first == number, one, jnp.where(second == number, two, 0.0)
        ).astype(jnp.bfloat16)
    out_ref[...] = (
        jnp.dot(spread[...], weight_ref[...], preferred_element_type=jnp.float32)
        .astype(out_ref.dtype)
        .reshape(out_ref.shape)
    )


def input_rows(received, hidden_grad, weight):
    sources, rows, wide = hidden_grad.shape
    features = weight.shape[1]
    return pl.pallas_call(
        input_kernel,
        grid=(sources // 2,),
        in_specs=[
            pl.BlockSpec((2, received.shape[1], features), lambda i: (i, 0, 0)),
            pl.BlockSpec((2, rows, wide), lambda i: (i, 0, 0)),
            pl.BlockSpec(weight.shape, lambda i: (0, 0)),
        ],
        out_specs=pl.BlockSpec((2, rows, features), lambda i: (i, 0, 0)),
        out_shape=jax.ShapeDtypeStruct((sources, rows, features), jnp.bfloat16),
        scratch_shapes=[pltpu.VMEM((2 * rows, weight.shape[0]), jnp.bfloat16)],
        compiler_params=params(),
        cost_estimate=cost(sources * rows, weight.shape[0], features),
    )(received, hidden_grad, weight)


def exchange(value, axes):
    return lax.all_to_all(value, axes, split_axis=0, concat_axis=0, tiled=True)


def chain_gather(mine):
    beside = lax.ppermute(mine, "far", SIDES)
    across = lax.ppermute(mine, "far", MIDDLE)
    across_far = lax.ppermute(beside, "far", MIDDLE)
    second = lax.ppermute(across, "far", OUTWARD)
    third = lax.ppermute(across_far, "far", OUTWARD)
    return [(mine,), (beside,), (across, second), (across_far, third)]


def add(*terms):
    return sum(term.astype(jnp.float32) for term in terms).astype(jnp.bfloat16)


def chain_scatter(own, beside, second, third):
    third = add(third, lax.ppermute(third, "far", INWARD))
    second = add(second, lax.ppermute(second, "far", INWARD))
    beside = add(beside, lax.ppermute(third, "far", MIDDLE))
    across = lax.ppermute(second, "far", MIDDLE)
    return add(own, across, lax.ppermute(beside, "far", SIDES))


def body(token_grads, router_gates, expert_ids, saved_hidden, up_weight, down_weight):
    tok_count = token_grads.shape[0]
    local_experts, hidden, width = up_weight.shape
    members, far_count = lax.axis_size(GROUP), lax.axis_size("far")
    wide, features = 2 * hidden, width // NEAR
    own_rows = local_experts * hidden
    near = lax.axis_index("near")
    chained = far_count == len(CHAIN)

    def halves(weight):
        flat = weight.reshape(own_rows, width)
        own = lax.dynamic_slice_in_dim(flat, near * features, features, axis=1)
        other = lax.dynamic_slice_in_dim(flat, (1 - near) * features, features, axis=1)
        return own, lax.ppermute(other, "near", SWAP)

    down_halves, up_halves = halves(down_weight), halves(up_weight)
    if chained:
        down_pieces = [terms for half in down_halves for terms in chain_gather(half)]
        far_places = jnp.asarray(CHAIN, jnp.int32)[lax.axis_index("far")]
    else:
        down_pieces = [(lax.all_gather(half, "far", tiled=True),) for half in down_halves]
        far_places = jnp.arange(far_count, dtype=jnp.int32)
    up_full = lax.all_gather(jnp.concatenate(up_halves), "far", tiled=True)
    packed, activation, scaled = pack_tokens(
        far_places, expert_ids.T, router_gates.T, saved_hidden, token_grads, members, local_experts
    )
    received = exchange(packed, GROUP)

    partial_value = down_partial(
        received, tok_count, wide, own_rows * NEAR * far_count, far_count if chained else 1
    )
    if chained:
        sums = chain_scatter(*partial_value)
    else:
        sums = lax.psum_scatter(partial_value[0], "far", scatter_dimension=0, tiled=True)
    kept, passed = sums[:own_rows], lax.ppermute(sums[own_rows:], "near", SWAP)
    down_grads = jnp.concatenate(
        [jnp.where(near == 0, kept, passed), jnp.where(near == 0, passed, kept)], axis=1
    ).reshape(down_weight.shape)

    parts = exchange(project(received, down_pieces, tok_count, wide), GROUP)
    hidden_grad, gate_grads = pl.pallas_call(
        hidden_kernel,
        out_shape=(
            jax.ShapeDtypeStruct((members, tok_count, wide), jnp.bfloat16),
            jax.ShapeDtypeStruct((2, tok_count), jnp.bfloat16),
        ),
        compiler_params=params(),
    )(parts, activation, scaled)
    hidden_grad = exchange(hidden_grad, GROUP)
    input_grads = unpack_tokens(exchange(input_rows(received, hidden_grad, up_full), GROUP))
    return (input_grads, gate_grads.T, down_grads)


def solution(mesh):
    sizes = [mesh.shape[name] for name in ("expert", "inner", "outer")]
    split = Mesh(
        mesh.devices.reshape(sizes[0] // NEAR, NEAR, *sizes[1:]),
        ("far", "near", "inner", "outer"),
    )
    rows = P(("far", "near", "inner", "outer"), None)
    weights = P(("far", "near"), None, ("inner", "outer"))
    return jax.shard_map(
        body,
        mesh=split,
        in_specs=(rows, rows, rows, rows, weights, weights),
        out_specs=(rows, rows, weights),
        check_vma=False,
    )
```

```python
import functools
import jax
import jax.numpy as jnp
from jax import lax
from jax.experimental import pallas as pl
from jax.experimental.pallas import tpu as pltpu
from jax.sharding import Mesh, PartitionSpec as P

root_half = 0.7071067811865476
inv_root_tau = 0.3989422804014327
GROUP = ("inner", "outer", "near")
NEAR = 2
BLOCK = 256
TILE = 16
MIB = 1 << 20
CHAIN = ((0, 1, 2, 3), (1, 0, 2, 3), (3, 2, 0, 1), (3, 2, 1, 0))
SIDES = ((0, 1), (1, 0), (2, 3), (3, 2))
MIDDLE = ((1, 2), (2, 1))
OUTWARD = ((1, 0), (2, 3))
SWAP = ((0, 1), (1, 0))
DOWN, UP = 0, 2


def gelu_parts(preact):
    cumulative = 0.5 * (1.0 + lax.erf(preact * root_half))
    density = inv_root_tau * jnp.exp(-0.5 * preact * preact)
    return (preact * cumulative, cumulative + preact * density)


def params():
    return pltpu.CompilerParams(vmem_limit_bytes=40 * MIB)


def cost(rows, inner, columns):
    return pl.CostEstimate(
        flops=2 * rows * inner * columns,
        bytes_accessed=2 * (rows * inner + inner * columns + rows * columns),
        transcendentals=0,
    )


def low_half(shape):
    return lax.broadcasted_iota(jnp.int32, shape, len(shape) - 1) < shape[-1] // 2


def columns_of(pair, wide):
    wanted = lax.broadcasted_iota(jnp.int32, (2, wide), 0)
    return [
        lax.dot_general(
            pair.astype(jnp.bfloat16),
            jnp.where(wanted == k, 1.0, 0.0).astype(jnp.bfloat16),
            (((0,), (0,)), ((), ())),
            preferred_element_type=jnp.float32,
        )
        for k in range(2)
    ]


def pack_kernel(
    local_experts, far_ref, ids_ref, gates_ref, preact_ref, tokens_ref, *refs
):
    out_ref, activation_ref, scaled_ref, weighted = refs[-4:]
    blocks, height, features = out_ref.shape
    rows, wide = preact_ref.shape
    far_count = far_ref.shape[0]
    taken = rows * wide // features

    @pl.when(pl.program_id(0) == 0)
    def _():
        activation, slope = gelu_parts(preact_ref[...].astype(jnp.float32))
        gates = jnp.where(low_half((rows, wide)), *columns_of(gates_ref[...], wide))
        activation_ref[...] = activation
        scaled_ref[...] = gates * slope
        weighted[...] = (gates * activation).astype(jnp.bfloat16)

    ids = ids_ref[...]
    local = lax.rem(ids, local_experts)
    line = lax.div(ids, local_experts)
    far, near = lax.div(line, NEAR), lax.rem(line, NEAR)
    far_place = jnp.zeros_like(far)
    for at in range(far_count):
        far_place = jnp.where(far == at, far_ref[at], far_place)
    for block in range(blocks):
        side = lax.rem(near + block, NEAR)
        places = (
            (far_place * NEAR + side) * local_experts + local,
            (far * NEAR + side) * local_experts + local,
        )
        out_ref[block, 0:rows, :] = tokens_ref[:, block * features : (block + 1) * features]
        for at in range(0, features, wide):
            start = at // wide * taken
            out_ref[block, rows : rows + taken, at : at + wide] = weighted[start : start + taken, :]
        last = height - TILE
        out_ref[block, last:, :] = jnp.zeros((TILE, features), jnp.bfloat16)
        for at, place in zip((DOWN, UP), places):
            out_ref[block, last + at : last + at + 2, 0:rows] = place.astype(jnp.bfloat16)


def pack_tokens(far_places, ids, gates, preact, tokens, members, local_experts, before):
    rows, width = tokens.shape
    features = width // members
    each = members // 4
    height = rows + preact.size // features + TILE
    small = jax.ShapeDtypeStruct(preact.shape, jnp.float32)
    whole = [pl.BlockSpec(array.shape, lambda i: (0, 0)) for array in (ids, gates, preact)]
    return pl.pallas_call(
        functools.partial(pack_kernel, local_experts),
        grid=(4,),
        in_specs=[
            pl.BlockSpec(memory_space=pltpu.SMEM),
            *whole,
            pl.BlockSpec((rows, each * features), lambda i: (0, i)),
            *[pl.BlockSpec(memory_space=pl.ANY) for _ in before],
        ],
        out_specs=(pl.BlockSpec((each, height, features), lambda i: (i, 0, 0)), whole[2], whole[2]),
        out_shape=(
            jax.ShapeDtypeStruct((members, height, features), jnp.bfloat16), small, small,
        ),
        scratch_shapes=[pltpu.VMEM(preact.shape, jnp.bfloat16)],
        compiler_params=params(),
    )(far_places, ids, gates, preact, tokens, *before)


def unpack_kernel(parts_ref, out_ref):
    blocks, _, features = parts_ref.shape
    for block in range(blocks):
        out_ref[:, block * features : (block + 1) * features] = parts_ref[block]


def unpack_tokens(parts):
    members, rows, features = parts.shape
    each = members // 4
    return pl.pallas_call(
        unpack_kernel,
        grid=(4,),
        in_specs=[pl.BlockSpec((each, rows, features), lambda i: (i, 0, 0))],
        out_specs=pl.BlockSpec((rows, each * features), lambda i: (0, i)),
        out_shape=jax.ShapeDtypeStruct((rows, members * features), jnp.bfloat16),
        compiler_params=params(),
    )(parts)


def places_of(received_ref, source, which, rows):
    at = received_ref.shape[1] - TILE + which
    return received_ref[source, at : at + 2, 0:rows]


def token_rows(received_ref, rows):
    sources, _, features = received_ref.shape
    return received_ref[:, 0:rows, :].reshape(sources * rows, features)


def down_kernel(rows, wide, received_ref, *refs):
    out_ref, turned, numbers, spread = refs[-4:]
    sources, _, features = received_ref.shape
    hidden, each = wide // 2, BLOCK // (wide // 2)
    taken = rows * wide // features
    for source in range(sources):
        weighted = jnp.concatenate(
            [
                received_ref[source, rows : rows + taken, at : at + wide].astype(jnp.float32)
                for at in range(0, features, wide)
            ]
        )
        lanes = slice(source * rows, (source + 1) * rows)
        turned[:, lanes] = weighted.T
        numbers[:, lanes] = places_of(received_ref, source, UP, rows).astype(jnp.float32)
    for start in range(0, out_ref.shape[0], BLOCK):
        for expert in range(each):
            number = start // hidden + expert
            spread[expert * hidden : (expert + 1) * hidden, :] = jnp.where(
                numbers[0:1, :] == number,
                turned[0:hidden, :],
                jnp.where(numbers[1:2, :] == number, turned[hidden:, :], 0.0),
            ).astype(jnp.bfloat16)
        out_ref[start : start + BLOCK, :] = jnp.dot(
            spread[...], token_rows(received_ref, rows), preferred_element_type=jnp.float32
        ).astype(out_ref.dtype)


def down_partial(received, rows, wide, total_rows, before):
    sources, _, features = received.shape
    total = sources * rows
    return pl.pallas_call(
        functools.partial(down_kernel, rows, wide),
        in_specs=[
            pl.BlockSpec(memory_space=pltpu.VMEM),
            *[pl.BlockSpec(memory_space=pl.ANY) for _ in before],
        ],
        out_shape=jax.ShapeDtypeStruct((total_rows, features), jnp.bfloat16),
        scratch_shapes=[
            pltpu.VMEM((wide, total), jnp.float32),
            pltpu.VMEM((2, total), jnp.float32),
            pltpu.VMEM((BLOCK, total), jnp.bfloat16),
        ],
        compiler_params=params(),
        cost_estimate=cost(total_rows, total, features),
    )(received, *before)


def lane_numbers(received_ref, which, rows, wide):
    sources = received_ref.shape[0]
    low = low_half((sources * rows, wide))
    found = [
        columns_of(places_of(received_ref, source, which, rows), wide)
        for source in range(sources)
    ]
    odd = jnp.where(low, 0.0, 1.0)
    return low, *[jnp.concatenate([pair[k] for pair in found]) - odd for k in range(2)]


def join(pieces, piece_refs, full):
    at = start = 0
    for terms in pieces:
        value = piece_refs[at][...]
        for ref in piece_refs[at + 1 : at + terms]:
            value = value + ref[...]
        full[start : start + value.shape[0], :] = value
        at, start = at + terms, start + value.shape[0]


def project_kernel(pieces, received_ref, *refs):
    piece_refs, out_ref, full = refs[:-2], refs[-2], refs[-1]
    pl.when(pl.program_id(0) == 0)(lambda: join(pieces, piece_refs, full))
    sources, rows, wide = out_ref.shape
    low, first, second = lane_numbers(received_ref, DOWN, rows, wide)
    tokens = token_rows(received_ref, rows)
    sums = [jnp.zeros((sources * rows, wide), jnp.float32) for _ in range(2)]
    for start in range(0, full.shape[0], BLOCK):
        product = lax.dot_general(
            tokens,
            full[start : start + BLOCK, :],
            (((1,), (1,)), ((), ())),
            preferred_element_type=jnp.float32,
        )
        for at in range(0, BLOCK, wide):
            part = product[:, at : at + wide]
            number = (start + at) // wide * 2.0
            sums[0] = jnp.where(first == number, part, sums[0])
            sums[1] = jnp.where(second == number, part, sums[1])
    folded = [value + pltpu.roll(value, wide // 2, 1) for value in sums]
    value = jnp.where(low, folded[0], folded[1]).astype(out_ref.dtype)
    out_ref[...] = value.reshape(out_ref.shape)


def project(received, pieces, rows, wide):
    sources, height, features = received.shape
    flat = [term for terms in pieces for term in terms]
    joined = sum(terms[0].shape[0] for terms in pieces)
    return pl.pallas_call(
        functools.partial(project_kernel, [len(terms) for terms in pieces]),
        grid=(sources // 2,),
        in_specs=[
            pl.BlockSpec((2, height, features), lambda i: (i, 0, 0)),
            *[pl.BlockSpec(term.shape, lambda i: (0, 0)) for term in flat],
        ],
        out_specs=pl.BlockSpec((2, rows, wide), lambda i: (i, 0, 0)),
        out_shape=jax.ShapeDtypeStruct((sources, rows, wide), jnp.bfloat16),
        scratch_shapes=[pltpu.VMEM((joined, features), jnp.bfloat16)],
        compiler_params=params(),
        cost_estimate=cost(sources * rows, features, joined),
    )(received, *flat)


def hidden_kernel(parts_ref, activation_ref, scaled_ref, hidden_ref, gate_ref):
    projected = parts_ref[0].astype(jnp.float32)
    for source in range(1, parts_ref.shape[0]):
        projected = projected + parts_ref[source].astype(jnp.float32)
    wide = projected.shape[1]
    half = lax.broadcasted_iota(jnp.int32, (8, wide), 1) // (wide // 2)
    wanted = lax.broadcasted_iota(jnp.int32, (8, wide), 0)
    sums = lax.dot_general(
        jnp.where(wanted == half, 1.0, 0.0),
        activation_ref[...] * projected,
        (((1,), (1,)), ((), ())),
        precision=lax.Precision.HIGHEST,
        preferred_element_type=jnp.float32,
    )
    gate_ref[...] = sums[0:2, :].astype(gate_ref.dtype)
    hidden = (projected * scaled_ref[...]).astype(hidden_ref.dtype)
    for source in range(hidden_ref.shape[0]):
        hidden_ref[source] = hidden


def input_kernel(received_ref, hidden_ref, weight_ref, out_ref, spread):
    sources, rows, wide = hidden_ref.shape
    low, first, second = lane_numbers(received_ref, UP, rows, wide)
    values = hidden_ref[...].reshape(sources * rows, wide).astype(jnp.float32)
    swapped = pltpu.roll(values, wide // 2, 1)
    one = jnp.where(low, values, swapped)
    two = jnp.where(low, swapped, values)
    for start in range(0, weight_ref.shape[0], wide):
        number = start // wide * 2.0
        spread[:, start : start + wide] = jnp.where(
            first == number, one, jnp.where(second == number, two, 0.0)
        ).astype(jnp.bfloat16)
    out_ref[...] = (
        jnp.dot(spread[...], weight_ref[...], preferred_element_type=jnp.float32)
        .astype(out_ref.dtype)
        .reshape(out_ref.shape)
    )


def input_rows(received, hidden_grad, weight):
    sources, rows, wide = hidden_grad.shape
    features = weight.shape[1]
    return pl.pallas_call(
        input_kernel,
        grid=(sources // 2,),
        in_specs=[
            pl.BlockSpec((2, received.shape[1], features), lambda i: (i, 0, 0)),
            pl.BlockSpec((2, rows, wide), lambda i: (i, 0, 0)),
            pl.BlockSpec(weight.shape, lambda i: (0, 0)),
        ],
        out_specs=pl.BlockSpec((2, rows, features), lambda i: (i, 0, 0)),
        out_shape=jax.ShapeDtypeStruct((sources, rows, features), jnp.bfloat16),
        scratch_shapes=[pltpu.VMEM((2 * rows, weight.shape[0]), jnp.bfloat16)],
        compiler_params=params(),
        cost_estimate=cost(sources * rows, weight.shape[0], features),
    )(received, hidden_grad, weight)


def exchange(value, axes):
    return lax.all_to_all(value, axes, split_axis=0, concat_axis=0, tiled=True)


def chain_gather(mine):
    beside = lax.ppermute(mine, "far", SIDES)
    across = lax.ppermute(mine, "far", MIDDLE)
    across_far = lax.ppermute(beside, "far", MIDDLE)
    second = lax.ppermute(across, "far", OUTWARD)
    third = lax.ppermute(across_far, "far", OUTWARD)
    return [(mine,), (beside,), (across, second), (across_far, third)]


def body(token_grads, router_gates, expert_ids, saved_hidden, up_weight, down_weight):
    tok_count = token_grads.shape[0]
    local_experts, hidden, width = up_weight.shape
    members, far_count = lax.axis_size(GROUP), lax.axis_size("far")
    wide, features = 2 * hidden, width // NEAR
    own_rows = local_experts * hidden
    near = lax.axis_index("near")
    chained = far_count == len(CHAIN)

    def halves(weight):
        flat = weight.reshape(own_rows, width)
        own = lax.dynamic_slice_in_dim(flat, near * features, features, axis=1)
        other = lax.dynamic_slice_in_dim(flat, (1 - near) * features, features, axis=1)
        return jnp.concatenate([own, lax.ppermute(other, "near", SWAP)])

    down_own, up_own = halves(down_weight), halves(up_weight)
    if far_count == len(CHAIN):
        down_pieces = chain_gather(down_own)
        far_places = jnp.asarray(CHAIN, jnp.int32)[lax.axis_index("far")]
    else:
        down_pieces = [(lax.all_gather(down_own, "far", tiled=True),)]
        far_places = jnp.arange(far_count, dtype=jnp.int32)
    up_full = lax.all_gather(up_own, "far", tiled=True)
    packed, activation, scaled = pack_tokens(
        far_places, expert_ids.T, router_gates.T, saved_hidden, token_grads, members,
        local_experts, (down_own, up_own),
    )
    received = exchange(packed, GROUP)

    projected = project(received, down_pieces, tok_count, wide)
    parts = exchange(projected, GROUP)
    hidden_grad, gate_grads = pl.pallas_call(
        hidden_kernel,
        out_shape=(
            jax.ShapeDtypeStruct((members, tok_count, wide), jnp.bfloat16),
            jax.ShapeDtypeStruct((2, tok_count), jnp.bfloat16),
        ),
        compiler_params=params(),
    )(parts, activation, scaled)
    hidden_grad = exchange(hidden_grad, GROUP)
    input_grads = unpack_tokens(exchange(input_rows(received, hidden_grad, up_full), GROUP))

    partial_value = down_partial(
        received, tok_count, wide, up_full.shape[0], (up_full, projected)
    )
    sums = lax.psum_scatter(partial_value, "far", scatter_dimension=0, tiled=True)
    kept, passed = sums[:own_rows], lax.ppermute(sums[own_rows:], "near", SWAP)
    down_grads = jnp.concatenate(
        [jnp.where(near == 0, kept, passed), jnp.where(near == 0, passed, kept)], axis=1
    ).reshape(down_weight.shape)
    return (input_grads, gate_grads.T, down_grads)


def solution(mesh):
    sizes = [mesh.shape[name] for name in ("expert", "inner", "outer")]
    split = Mesh(
        mesh.devices.reshape(sizes[0] // NEAR, NEAR, *sizes[1:]),
        ("far", "near", "inner", "outer"),
    )
    rows = P(("far", "near", "inner", "outer"), None)
    weights = P(("far", "near"), None, ("inner", "outer"))
    return jax.shard_map(
        body,
        mesh=split,
        in_specs=(rows, rows, rows, rows, weights, weights),
        out_specs=(rows, rows, weights),
        check_vma=False,
    )
```

```python
import functools
import jax
import jax.numpy as jnp
from jax import lax
from jax.experimental import pallas as pl
from jax.experimental.pallas import tpu as pltpu
from jax.sharding import Mesh, PartitionSpec as P

root_half = 0.7071067811865476
inv_root_tau = 0.3989422804014327
GROUP = ("inner", "outer", "near")
NEAR = 2
BLOCK = 256
TILE = 16
MIB = 1 << 20
CHAIN = ((0, 1, 2, 3), (1, 0, 2, 3), (3, 2, 0, 1), (3, 2, 1, 0))
SIDES = ((0, 1), (1, 0), (2, 3), (3, 2))
MIDDLE = ((1, 2), (2, 1))
OUTWARD = ((1, 0), (2, 3))
INWARD = ((0, 1), (3, 2))
SWAP = ((0, 1), (1, 0))
DOWN, UP = 0, 2


def gelu_parts(preact):
    cumulative = 0.5 * (1.0 + lax.erf(preact * root_half))
    density = inv_root_tau * jnp.exp(-0.5 * preact * preact)
    return (preact * cumulative, cumulative + preact * density)


def params(grant=40):
    return pltpu.CompilerParams(vmem_limit_bytes=grant * MIB)


def cost(rows, inner, columns):
    return pl.CostEstimate(
        flops=2 * rows * inner * columns,
        bytes_accessed=2 * (rows * inner + inner * columns + rows * columns),
        transcendentals=0,
    )


def low_half(shape):
    return lax.broadcasted_iota(jnp.int32, shape, len(shape) - 1) < shape[-1] // 2


def columns_of(pair, wide):
    wanted = lax.broadcasted_iota(jnp.int32, (2, wide), 0)
    return [
        lax.dot_general(
            pair.astype(jnp.bfloat16),
            jnp.where(wanted == k, 1.0, 0.0).astype(jnp.bfloat16),
            (((0,), (0,)), ((), ())),
            preferred_element_type=jnp.float32,
        )
        for k in range(2)
    ]


def stack_kernel(own_ref, other_ref, *refs):
    rows = own_ref.shape[0]
    refs[-1][0:rows, :] = own_ref[...]
    refs[-1][rows:, :] = other_ref[...]


def stack(own, other, before):
    return pl.pallas_call(
        stack_kernel,
        in_specs=[
            *[pl.BlockSpec(memory_space=pltpu.VMEM)] * 2,
            *[pl.BlockSpec(memory_space=pl.ANY) for _ in before],
        ],
        out_shape=jax.ShapeDtypeStruct((2 * own.shape[0], own.shape[1]), own.dtype),
        compiler_params=params(),
    )(own, other, *before)


def pack_kernel(
    local_experts, far_ref, ids_ref, gates_ref, preact_ref, tokens_ref, *refs
):
    out_ref, activation_ref, scaled_ref, weighted = refs[-4:]
    blocks, height, features = out_ref.shape
    rows, wide = preact_ref.shape
    far_count = far_ref.shape[0]
    taken = rows * wide // features

    @pl.when(pl.program_id(0) == 0)
    def _():
        activation, slope = gelu_parts(preact_ref[...].astype(jnp.float32))
        gates = jnp.where(low_half((rows, wide)), *columns_of(gates_ref[...], wide))
        activation_ref[...] = activation
        scaled_ref[...] = gates * slope
        weighted[...] = (gates * activation).astype(jnp.bfloat16)

    ids = ids_ref[...]
    local = lax.rem(ids, local_experts)
    line = lax.div(ids, local_experts)
    far, near = lax.div(line, NEAR), lax.rem(line, NEAR)
    far_place = jnp.zeros_like(far)
    for at in range(far_count):
        far_place = jnp.where(far == at, far_ref[at], far_place)
    for block in range(blocks):
        side = lax.rem(near + block, NEAR)
        places = (
            (side * far_count + far) * local_experts + local,
            (far_place * NEAR + side) * local_experts + local,
        )
        out_ref[block, 0:rows, :] = tokens_ref[:, block * features : (block + 1) * features]
        for at in range(0, features, wide):
            start = at // wide * taken
            out_ref[block, rows : rows + taken, at : at + wide] = weighted[start : start + taken, :]
        last = height - TILE
        out_ref[block, last:, :] = jnp.zeros((TILE, features), jnp.bfloat16)
        for at, place in zip((DOWN, UP), places):
            out_ref[block, last + at : last + at + 2, 0:rows] = place.astype(jnp.bfloat16)


def pack_tokens(far_places, ids, gates, preact, tokens, members, local_experts, before):
    rows, width = tokens.shape
    features = width // members
    each = members // 4
    height = rows + preact.size // features + TILE
    small = jax.ShapeDtypeStruct(preact.shape, jnp.float32)
    whole = [pl.BlockSpec(array.shape, lambda i: (0, 0)) for array in (ids, gates, preact)]
    return pl.pallas_call(
        functools.partial(pack_kernel, local_experts),
        grid=(4,),
        in_specs=[
            pl.BlockSpec(memory_space=pltpu.SMEM),
            *whole,
            pl.BlockSpec((rows, each * features), lambda i: (0, i)),
            *[pl.BlockSpec(memory_space=pl.ANY) for _ in before],
        ],
        out_specs=(pl.BlockSpec((each, height, features), lambda i: (i, 0, 0)), whole[2], whole[2]),
        out_shape=(
            jax.ShapeDtypeStruct((members, height, features), jnp.bfloat16), small, small,
        ),
        scratch_shapes=[pltpu.VMEM(preact.shape, jnp.bfloat16)],
        compiler_params=params(),
    )(far_places, ids, gates, preact, tokens, *before)


def unpack_kernel(parts_ref, out_ref):
    blocks, _, features = parts_ref.shape
    for block in range(blocks):
        out_ref[:, block * features : (block + 1) * features] = parts_ref[block]


def unpack_tokens(parts):
    members, rows, features = parts.shape
    each = members // 4
    return pl.pallas_call(
        unpack_kernel,
        grid=(4,),
        in_specs=[pl.BlockSpec((each, rows, features), lambda i: (i, 0, 0))],
        out_specs=pl.BlockSpec((rows, each * features), lambda i: (0, i)),
        out_shape=jax.ShapeDtypeStruct((rows, members * features), jnp.bfloat16),
        compiler_params=params(),
    )(parts)


def places_of(received_ref, source, which, rows):
    at = received_ref.shape[1] - TILE + which
    return received_ref[source, at : at + 2, 0:rows]


def token_rows(received_ref, rows):
    sources, _, features = received_ref.shape
    return received_ref[:, 0:rows, :].reshape(sources * rows, features)


def down_kernel(rows, wide, count, received_ref, *refs):
    out_refs, (turned, numbers, spread) = refs[-3 - count : -3], refs[-3:]
    sources, _, features = received_ref.shape
    hidden, each = wide // 2, BLOCK // (wide // 2)
    taken = rows * wide // features
    for source in range(sources):
        weighted = jnp.concatenate(
            [
                received_ref[source, rows : rows + taken, at : at + wide].astype(jnp.float32)
                for at in range(0, features, wide)
            ]
        )
        lanes = slice(source * rows, (source + 1) * rows)
        turned[:, lanes] = weighted.T
        numbers[:, lanes] = places_of(received_ref, source, UP, rows).astype(jnp.float32)
    number = 0
    for out_ref in out_refs:
        for start in range(0, out_ref.shape[0], BLOCK):
            for expert in range(each):
                spread[expert * hidden : (expert + 1) * hidden, :] = jnp.where(
                    numbers[0:1, :] == number + expert,
                    turned[0:hidden, :],
                    jnp.where(numbers[1:2, :] == number + expert, turned[hidden:, :], 0.0),
                ).astype(jnp.bfloat16)
            number += each
            out_ref[start : start + BLOCK, :] = jnp.dot(
                spread[...], token_rows(received_ref, rows), preferred_element_type=jnp.float32
            ).astype(out_ref.dtype)


def down_partial(received, rows, wide, total_rows, count, before):
    sources, _, features = received.shape
    total = sources * rows
    return pl.pallas_call(
        functools.partial(down_kernel, rows, wide, count),
        in_specs=[
            pl.BlockSpec(memory_space=pltpu.VMEM),
            *[pl.BlockSpec(memory_space=pl.ANY) for _ in before],
        ],
        out_shape=[jax.ShapeDtypeStruct((total_rows // count, features), jnp.bfloat16)] * count,
        scratch_shapes=[
            pltpu.VMEM((wide, total), jnp.float32),
            pltpu.VMEM((2, total), jnp.float32),
            pltpu.VMEM((BLOCK, total), jnp.bfloat16),
        ],
        compiler_params=params(),
        cost_estimate=cost(total_rows, total, features),
    )(received, *before)


def lane_numbers(received_ref, which, rows, wide):
    sources = received_ref.shape[0]
    low = low_half((sources * rows, wide))
    found = [
        columns_of(places_of(received_ref, source, which, rows), wide)
        for source in range(sources)
    ]
    odd = jnp.where(low, 0.0, 1.0)
    return low, *[jnp.concatenate([pair[k] for pair in found]) - odd for k in range(2)]


def join(pieces, piece_refs, full):
    at = start = 0
    for terms in pieces:
        value = piece_refs[at][...]
        for ref in piece_refs[at + 1 : at + terms]:
            value = value + ref[...]
        full[start : start + value.shape[0], :] = value
        at, start = at + terms, start + value.shape[0]


def project_kernel(received_ref, *refs):
    weight_refs, out_ref = refs[:-1], refs[-1]
    sources, rows, wide = out_ref.shape
    low, first, second = lane_numbers(received_ref, DOWN, rows, wide)
    tokens = token_rows(received_ref, rows)
    sums = [jnp.zeros((sources * rows, wide), jnp.float32) for _ in range(2)]
    number = 0.0
    for weight_ref, start in [
        (ref, at) for ref in weight_refs for at in range(0, ref.shape[0], BLOCK)
    ]:
        product = lax.dot_general(
            tokens,
            weight_ref[start : start + BLOCK, :],
            (((1,), (1,)), ((), ())),
            preferred_element_type=jnp.float32,
        )
        for at in range(0, BLOCK, wide):
            part = product[:, at : at + wide]
            sums[0] = jnp.where(first == number, part, sums[0])
            sums[1] = jnp.where(second == number, part, sums[1])
            number += 2.0
    folded = [value + pltpu.roll(value, wide // 2, 1) for value in sums]
    value = jnp.where(low, folded[0], folded[1]).astype(out_ref.dtype)
    out_ref[...] = value.reshape(out_ref.shape)


def project(received, weights, rows, wide):
    sources, height, features = received.shape
    return pl.pallas_call(
        project_kernel,
        grid=(sources // 2,),
        in_specs=[
            pl.BlockSpec((2, height, features), lambda i: (i, 0, 0)),
            *[pl.BlockSpec(weight.shape, lambda i: (0, 0)) for weight in weights],
        ],
        out_specs=pl.BlockSpec((2, rows, wide), lambda i: (i, 0, 0)),
        out_shape=jax.ShapeDtypeStruct((sources, rows, wide), jnp.bfloat16),
        compiler_params=params(),
        cost_estimate=cost(sources * rows, features, sum(w.shape[0] for w in weights)),
    )(received, *weights)


def hidden_kernel(parts_ref, activation_ref, scaled_ref, hidden_ref, gate_ref):
    projected = parts_ref[0].astype(jnp.float32)
    for source in range(1, parts_ref.shape[0]):
        projected = projected + parts_ref[source].astype(jnp.float32)
    wide = projected.shape[1]
    half = lax.broadcasted_iota(jnp.int32, (8, wide), 1) // (wide // 2)
    wanted = lax.broadcasted_iota(jnp.int32, (8, wide), 0)
    sums = lax.dot_general(
        jnp.where(wanted == half, 1.0, 0.0),
        activation_ref[...] * projected,
        (((1,), (1,)), ((), ())),
        precision=lax.Precision.HIGHEST,
        preferred_element_type=jnp.float32,
    )
    gate_ref[...] = sums[0:2, :].astype(gate_ref.dtype)
    hidden = (projected * scaled_ref[...]).astype(hidden_ref.dtype)
    for source in range(hidden_ref.shape[0]):
        hidden_ref[source] = hidden


def input_kernel(pieces, received_ref, hidden_ref, *refs):
    piece_refs, out_ref, full, spread = refs[:-3], refs[-3], refs[-2], refs[-1]
    pl.when(pl.program_id(0) == 0)(lambda: join(pieces, piece_refs, full))
    sources, rows, wide = hidden_ref.shape
    low, first, second = lane_numbers(received_ref, UP, rows, wide)
    values = hidden_ref[...].reshape(sources * rows, wide).astype(jnp.float32)
    swapped = pltpu.roll(values, wide // 2, 1)
    one = jnp.where(low, values, swapped)
    two = jnp.where(low, swapped, values)
    for start in range(0, full.shape[0], wide):
        number = start // wide * 2.0
        spread[:, start : start + wide] = jnp.where(
            first == number, one, jnp.where(second == number, two, 0.0)
        ).astype(jnp.bfloat16)
    out_ref[...] = (
        jnp.dot(spread[...], full[...], preferred_element_type=jnp.float32)
        .astype(out_ref.dtype)
        .reshape(out_ref.shape)
    )


def input_rows(received, hidden_grad, pieces):
    sources, rows, wide = hidden_grad.shape
    flat = [term for terms in pieces for term in terms]
    joined, features = sum(terms[0].shape[0] for terms in pieces), flat[0].shape[1]
    return pl.pallas_call(
        functools.partial(input_kernel, [len(terms) for terms in pieces]),
        grid=(sources // 2,),
        in_specs=[
            pl.BlockSpec((2, received.shape[1], features), lambda i: (i, 0, 0)),
            pl.BlockSpec((2, rows, wide), lambda i: (i, 0, 0)),
            *[pl.BlockSpec(term.shape, lambda i: (0, 0)) for term in flat],
        ],
        out_specs=pl.BlockSpec((2, rows, features), lambda i: (i, 0, 0)),
        out_shape=jax.ShapeDtypeStruct((sources, rows, features), jnp.bfloat16),
        scratch_shapes=[
            pltpu.VMEM((joined, features), jnp.bfloat16),
            pltpu.VMEM((2 * rows, joined), jnp.bfloat16),
        ],
        compiler_params=params(),
        cost_estimate=cost(sources * rows, joined, features),
    )(received, hidden_grad, *flat)


def exchange(value, axes):
    return lax.all_to_all(value, axes, split_axis=0, concat_axis=0, tiled=True)


def chain_gather(mine):
    beside = lax.ppermute(mine, "far", SIDES)
    across = lax.ppermute(mine, "far", MIDDLE)
    across_far = lax.ppermute(beside, "far", MIDDLE)
    second = lax.ppermute(across, "far", OUTWARD)
    third = lax.ppermute(across_far, "far", OUTWARD)
    return [(mine,), (beside,), (across, second), (across_far, third)]


def add(*terms):
    return sum(term.astype(jnp.float32) for term in terms).astype(jnp.bfloat16)


def chain_scatter(own, beside, second, third):
    third = add(third, lax.ppermute(third, "far", INWARD))
    second = add(second, lax.ppermute(second, "far", INWARD))
    beside = add(beside, lax.ppermute(third, "far", MIDDLE))
    across = lax.ppermute(second, "far", MIDDLE)
    return add(own, across, lax.ppermute(beside, "far", SIDES))


def body(token_grads, router_gates, expert_ids, saved_hidden, up_weight, down_weight):
    tok_count = token_grads.shape[0]
    local_experts, hidden, width = up_weight.shape
    members, far_count = lax.axis_size(GROUP), lax.axis_size("far")
    wide, features = 2 * hidden, width // NEAR
    own_rows = local_experts * hidden
    near = lax.axis_index("near")
    chained = far_count == len(CHAIN)

    chained = far_count == len(CHAIN)

    def halves(weight):
        flat = weight.reshape(own_rows, width)
        own = lax.dynamic_slice_in_dim(flat, near * features, features, axis=1)
        other = lax.dynamic_slice_in_dim(flat, (1 - near) * features, features, axis=1)
        return own, lax.ppermute(other, "near", SWAP)

    down_halves, up_halves = halves(down_weight), halves(up_weight)
    down_full = [lax.all_gather(half, "far", tiled=True) for half in down_halves]
    up_own = stack(*up_halves, down_full)
    if chained:
        up_pieces = chain_gather(up_own)
        far_places = jnp.asarray(CHAIN, jnp.int32)[lax.axis_index("far")]
    else:
        up_pieces = [(lax.all_gather(up_own, "far", tiled=True),)]
        far_places = jnp.arange(far_count, dtype=jnp.int32)
    packed, activation, scaled = pack_tokens(
        far_places, expert_ids.T, router_gates.T, saved_hidden, token_grads, members,
        local_experts, (down_halves[1], up_halves[1]),
    )
    received = exchange(packed, GROUP)

    projected = project(received, down_full, tok_count, wide)
    parts = exchange(projected, GROUP)
    hidden_grad, gate_grads = pl.pallas_call(
        hidden_kernel,
        out_shape=(
            jax.ShapeDtypeStruct((members, tok_count, wide), jnp.bfloat16),
            jax.ShapeDtypeStruct((2, tok_count), jnp.bfloat16),
        ),
        compiler_params=params(),
    )(parts, activation, scaled)
    hidden_grad = exchange(hidden_grad, GROUP)
    input_grads = unpack_tokens(exchange(input_rows(received, hidden_grad, up_pieces), GROUP))

    partial_value = down_partial(
        received, tok_count, wide, own_rows * NEAR * far_count, far_count if chained else 1,
        (projected,),
    )
    if chained:
        sums = chain_scatter(*partial_value)
    else:
        sums = lax.psum_scatter(partial_value[0], "far", scatter_dimension=0, tiled=True)
    kept, passed = sums[:own_rows], lax.ppermute(sums[own_rows:], "near", SWAP)
    down_grads = jnp.concatenate(
        [jnp.where(near == 0, kept, passed), jnp.where(near == 0, passed, kept)], axis=1
    ).reshape(down_weight.shape)
    return (input_grads, gate_grads.T, down_grads)


def solution(mesh):
    sizes = [mesh.shape[name] for name in ("expert", "inner", "outer")]
    split = Mesh(
        mesh.devices.reshape(sizes[0] // NEAR, NEAR, *sizes[1:]),
        ("far", "near", "inner", "outer"),
    )
    rows = P(("far", "near", "inner", "outer"), None)
    weights = P(("far", "near"), None, ("inner", "outer"))
    return jax.shard_map(
        body,
        mesh=split,
        in_specs=(rows, rows, rows, rows, weights, weights),
        out_specs=(rows, rows, weights),
        check_vma=False,
    )
```

```python
import functools
import jax
import jax.numpy as jnp
from jax import lax
from jax.experimental import pallas as pl
from jax.experimental.pallas import tpu as pltpu
from jax.sharding import Mesh, PartitionSpec as P

root_half = 0.7071067811865476
inv_root_tau = 0.3989422804014327
GROUP = ("inner", "outer", "near")
NEAR = 2
BLOCK = 256
TILE = 16
MIB = 1 << 20
CHAIN = ((0, 1, 2, 3), (1, 0, 2, 3), (3, 2, 0, 1), (3, 2, 1, 0))
SIDES = ((0, 1), (1, 0), (2, 3), (3, 2))
MIDDLE = ((1, 2), (2, 1))
OUTWARD = ((1, 0), (2, 3))
INWARD = ((0, 1), (3, 2))
SWAP = ((0, 1), (1, 0))


def gelu_parts(preact):
    cumulative = 0.5 * (1.0 + lax.erf(preact * root_half))
    density = inv_root_tau * jnp.exp(-0.5 * preact * preact)
    return (preact * cumulative, cumulative + preact * density)


def params(grant=20):
    return pltpu.CompilerParams(vmem_limit_bytes=grant * MIB)


def cost(rows, inner, columns):
    return pl.CostEstimate(
        flops=2 * rows * inner * columns,
        bytes_accessed=2 * (rows * inner + inner * columns + rows * columns),
        transcendentals=0,
    )


def low_half(shape):
    return lax.broadcasted_iota(jnp.int32, shape, len(shape) - 1) < shape[-1] // 2


def columns_of(pair, wide):
    wanted = lax.broadcasted_iota(jnp.int32, (2, wide), 0)
    return [
        lax.dot_general(
            pair.astype(jnp.bfloat16),
            jnp.where(wanted == k, 1.0, 0.0).astype(jnp.bfloat16),
            (((0,), (0,)), ((), ())),
            preferred_element_type=jnp.float32,
        )
        for k in range(2)
    ]


def stack_kernel(own_ref, other_ref, *refs):
    rows = own_ref.shape[0]
    refs[-1][0:rows, :] = own_ref[...]
    refs[-1][rows:, :] = other_ref[...]


def stack(own, other, before):
    return pl.pallas_call(
        stack_kernel,
        in_specs=[
            *[pl.BlockSpec(memory_space=pltpu.VMEM)] * 2,
            *[pl.BlockSpec(memory_space=pl.ANY) for _ in before],
        ],
        out_shape=jax.ShapeDtypeStruct((2 * own.shape[0], own.shape[1]), own.dtype),
        compiler_params=params(),
    )(own, other, *before)


def pass_on(value, before):
    anywhere = pl.BlockSpec(memory_space=pl.ANY)
    return pl.pallas_call(
        lambda *refs: None,
        in_specs=[anywhere] * (1 + len(before)),
        out_specs=anywhere,
        out_shape=jax.ShapeDtypeStruct(value.shape, value.dtype),
        input_output_aliases={0: 0},
        compiler_params=params(),
    )(value, *before)


def add_kernel(count, *refs):
    terms, out_refs = refs[: 2 * count], refs[-count:]
    for at in range(count):
        left, right = terms[2 * at][...], terms[2 * at + 1][...]
        total = left.astype(jnp.float32) + right.astype(jnp.float32)
        out_refs[at][...] = total.astype(out_refs[at].dtype)


def add_pairs(pairs, before):
    flat = [term for pair in pairs for term in pair]
    return pl.pallas_call(
        functools.partial(add_kernel, len(pairs)),
        in_specs=[
            *[pl.BlockSpec(memory_space=pltpu.VMEM) for _ in flat],
            *[pl.BlockSpec(memory_space=pl.ANY) for _ in before],
        ],
        out_shape=[jax.ShapeDtypeStruct(pair[0].shape, pair[0].dtype) for pair in pairs],
        compiler_params=params(),
    )(*flat, *before)


def pack_kernel(
    local_experts, far_ref, ids_ref, gates_ref, preact_ref, tokens_ref, *refs
):
    out_ref, activation_ref, scaled_ref, weighted = refs[-4:]
    blocks, height, features = out_ref.shape
    rows, wide = preact_ref.shape
    far_count = far_ref.shape[0]
    taken = rows * wide // features

    @pl.when(pl.program_id(0) == 0)
    def _():
        activation, slope = gelu_parts(preact_ref[...].astype(jnp.float32))
        gates = jnp.where(low_half((rows, wide)), *columns_of(gates_ref[...], wide))
        activation_ref[...] = activation
        scaled_ref[...] = gates * slope
        weighted[...] = (gates * activation).astype(jnp.bfloat16)

    ids = ids_ref[...]
    local = lax.rem(ids, local_experts)
    line = lax.div(ids, local_experts)
    far, near = lax.div(line, NEAR), lax.rem(line, NEAR)
    far_place = jnp.zeros_like(far)
    for at in range(far_count):
        far_place = jnp.where(far == at, far_ref[at], far_place)
    for block in range(blocks):
        side = lax.rem(near + block, NEAR)
        place = (far_place * NEAR + side) * local_experts + local
        out_ref[block, 0:rows, :] = tokens_ref[:, block * features : (block + 1) * features]
        for at in range(0, features, wide):
            start = at // wide * taken
            out_ref[block, rows : rows + taken, at : at + wide] = weighted[start : start + taken, :]
        last = height - TILE
        out_ref[block, last:, :] = jnp.zeros((TILE, features), jnp.bfloat16)
        out_ref[block, last : last + 2, 0:rows] = place.astype(jnp.bfloat16)


def pack_tokens(far_places, ids, gates, preact, tokens, members, local_experts, before):
    rows, width = tokens.shape
    features = width // members
    each = members // 4
    height = rows + preact.size // features + TILE
    small = jax.ShapeDtypeStruct(preact.shape, jnp.float32)
    whole = [pl.BlockSpec(array.shape, lambda i: (0, 0)) for array in (ids, gates, preact)]
    return pl.pallas_call(
        functools.partial(pack_kernel, local_experts),
        grid=(4,),
        in_specs=[
            pl.BlockSpec(memory_space=pltpu.SMEM),
            *whole,
            pl.BlockSpec((rows, each * features), lambda i: (0, i)),
            *[pl.BlockSpec(memory_space=pl.ANY) for _ in before],
        ],
        out_specs=(pl.BlockSpec((each, height, features), lambda i: (i, 0, 0)), whole[2], whole[2]),
        out_shape=(
            jax.ShapeDtypeStruct((members, height, features), jnp.bfloat16), small, small,
        ),
        scratch_shapes=[pltpu.VMEM(preact.shape, jnp.bfloat16)],
        compiler_params=params(),
    )(far_places, ids, gates, preact, tokens, *before)


def unpack_kernel(parts_ref, out_ref):
    blocks, _, features = parts_ref.shape
    for block in range(blocks):
        out_ref[:, block * features : (block + 1) * features] = parts_ref[block]


def unpack_tokens(parts):
    members, rows, features = parts.shape
    each = members // 4
    return pl.pallas_call(
        unpack_kernel,
        grid=(4,),
        in_specs=[pl.BlockSpec((each, rows, features), lambda i: (i, 0, 0))],
        out_specs=pl.BlockSpec((rows, each * features), lambda i: (0, i)),
        out_shape=jax.ShapeDtypeStruct((rows, members * features), jnp.bfloat16),
        compiler_params=params(),
    )(parts)


def places_of(received_ref, source, rows):
    at = received_ref.shape[1] - TILE
    return received_ref[source, at : at + 2, 0:rows]


def token_rows(received_ref, rows):
    sources, _, features = received_ref.shape
    return received_ref[:, 0:rows, :].reshape(sources * rows, features)


def down_kernel(rows, wide, count, received_ref, *refs):
    out_refs, (turned, numbers, spread) = refs[-3 - count : -3], refs[-3:]
    sources, _, features = received_ref.shape
    hidden, each = wide // 2, BLOCK // (wide // 2)
    taken = rows * wide // features
    for source in range(sources):
        weighted = jnp.concatenate(
            [
                received_ref[source, rows : rows + taken, at : at + wide].astype(jnp.float32)
                for at in range(0, features, wide)
            ]
        )
        lanes = slice(source * rows, (source + 1) * rows)
        turned[:, lanes] = weighted.T
        numbers[:, lanes] = places_of(received_ref, source, rows).astype(jnp.float32)
    number = 0
    for out_ref in out_refs:
        for start in range(0, out_ref.shape[0], BLOCK):
            for expert in range(each):
                spread[expert * hidden : (expert + 1) * hidden, :] = jnp.where(
                    numbers[0:1, :] == number + expert,
                    turned[0:hidden, :],
                    jnp.where(numbers[1:2, :] == number + expert, turned[hidden:, :], 0.0),
                ).astype(jnp.bfloat16)
            number += each
            out_ref[start : start + BLOCK, :] = jnp.dot(
                spread[...], token_rows(received_ref, rows), preferred_element_type=jnp.float32
            ).astype(out_ref.dtype)


def down_partial(received, rows, wide, total_rows, count, before):
    sources, _, features = received.shape
    total = sources * rows
    return pl.pallas_call(
        functools.partial(down_kernel, rows, wide, count),
        in_specs=[
            pl.BlockSpec(memory_space=pltpu.VMEM),
            *[pl.BlockSpec(memory_space=pl.ANY) for _ in before],
        ],
        out_shape=[jax.ShapeDtypeStruct((total_rows // count, features), jnp.bfloat16)] * count,
        scratch_shapes=[
            pltpu.VMEM((wide, total), jnp.float32),
            pltpu.VMEM((2, total), jnp.float32),
            pltpu.VMEM((BLOCK, total), jnp.bfloat16),
        ],
        compiler_params=params(),
        cost_estimate=cost(total_rows, total, features),
    )(received, *before)


def lane_numbers(received_ref, rows, wide):
    sources = received_ref.shape[0]
    low = low_half((sources * rows, wide))
    found = [
        columns_of(places_of(received_ref, source, rows), wide)
        for source in range(sources)
    ]
    odd = jnp.where(low, 0.0, 1.0)
    return low, *[jnp.concatenate([pair[k] for pair in found]) - odd for k in range(2)]


def join(pieces, piece_refs, full):
    at = start = 0
    for terms in pieces:
        value = piece_refs[at][...]
        for ref in piece_refs[at + 1 : at + terms]:
            value = value + ref[...]
        full[start : start + value.shape[0], :] = value
        at, start = at + terms, start + value.shape[0]


def project_kernel(pieces, received_ref, *refs):
    piece_refs, out_ref, full = refs[:-2], refs[-2], refs[-1]
    pl.when(pl.program_id(0) == 0)(lambda: join(pieces, piece_refs, full))
    sources, rows, wide = out_ref.shape
    low, first, second = lane_numbers(received_ref, rows, wide)
    tokens = token_rows(received_ref, rows)
    sums = [jnp.zeros((sources * rows, wide), jnp.float32) for _ in range(2)]
    number = 0.0
    for start in range(0, full.shape[0], BLOCK):
        product = lax.dot_general(
            tokens,
            full[start : start + BLOCK, :],
            (((1,), (1,)), ((), ())),
            preferred_element_type=jnp.float32,
        )
        for at in range(0, BLOCK, wide):
            part = product[:, at : at + wide]
            sums[0] = jnp.where(first == number, part, sums[0])
            sums[1] = jnp.where(second == number, part, sums[1])
            number += 2.0
    folded = [value + pltpu.roll(value, wide // 2, 1) for value in sums]
    value = jnp.where(low, folded[0], folded[1]).astype(out_ref.dtype)
    out_ref[...] = value.reshape(out_ref.shape)


def project(received, pieces, rows, wide):
    sources, height, features = received.shape
    flat = [term for terms in pieces for term in terms]
    joined = sum(terms[0].shape[0] for terms in pieces)
    return pl.pallas_call(
        functools.partial(project_kernel, [len(terms) for terms in pieces]),
        grid=(sources // 2,),
        in_specs=[
            pl.BlockSpec((2, height, features), lambda i: (i, 0, 0)),
            *[pl.BlockSpec(term.shape, lambda i: (0, 0)) for term in flat],
        ],
        out_specs=pl.BlockSpec((2, rows, wide), lambda i: (i, 0, 0)),
        out_shape=jax.ShapeDtypeStruct((sources, rows, wide), jnp.bfloat16),
        scratch_shapes=[pltpu.VMEM((joined, features), jnp.bfloat16)],
        compiler_params=params(),
        cost_estimate=cost(sources * rows, features, joined),
    )(received, *flat)


def hidden_kernel(parts_ref, activation_ref, scaled_ref, hidden_ref, gate_ref):
    projected = parts_ref[0].astype(jnp.float32)
    for source in range(1, parts_ref.shape[0]):
        projected = projected + parts_ref[source].astype(jnp.float32)
    wide = projected.shape[1]
    half = lax.broadcasted_iota(jnp.int32, (8, wide), 1) // (wide // 2)
    wanted = lax.broadcasted_iota(jnp.int32, (8, wide), 0)
    sums = lax.dot_general(
        jnp.where(wanted == half, 1.0, 0.0),
        activation_ref[...] * projected,
        (((1,), (1,)), ((), ())),
        precision=lax.Precision.HIGHEST,
        preferred_element_type=jnp.float32,
    )
    gate_ref[...] = sums[0:2, :].astype(gate_ref.dtype)
    hidden = (projected * scaled_ref[...]).astype(hidden_ref.dtype)
    for source in range(hidden_ref.shape[0]):
        hidden_ref[source] = hidden


def input_kernel(pieces, received_ref, hidden_ref, *refs):
    piece_refs, out_ref, full, spread = refs[:-3], refs[-3], refs[-2], refs[-1]
    pl.when(pl.program_id(0) == 0)(lambda: join(pieces, piece_refs, full))
    sources, rows, wide = hidden_ref.shape
    low, first, second = lane_numbers(received_ref, rows, wide)
    values = hidden_ref[...].reshape(sources * rows, wide).astype(jnp.float32)
    swapped = pltpu.roll(values, wide // 2, 1)
    one = jnp.where(low, values, swapped)
    two = jnp.where(low, swapped, values)
    for start in range(0, full.shape[0], wide):
        number = start // wide * 2.0
        spread[:, start : start + wide] = jnp.where(
            first == number, one, jnp.where(second == number, two, 0.0)
        ).astype(jnp.bfloat16)
    out_ref[...] = (
        jnp.dot(spread[...], full[...], preferred_element_type=jnp.float32)
        .astype(out_ref.dtype)
        .reshape(out_ref.shape)
    )


def input_rows(received, hidden_grad, pieces):
    sources, rows, wide = hidden_grad.shape
    flat = [term for terms in pieces for term in terms]
    joined, features = sum(terms[0].shape[0] for terms in pieces), flat[0].shape[1]
    return pl.pallas_call(
        functools.partial(input_kernel, [len(terms) for terms in pieces]),
        grid=(sources // 2,),
        in_specs=[
            pl.BlockSpec((2, received.shape[1], features), lambda i: (i, 0, 0)),
            pl.BlockSpec((2, rows, wide), lambda i: (i, 0, 0)),
            *[pl.BlockSpec(term.shape, lambda i: (0, 0)) for term in flat],
        ],
        out_specs=pl.BlockSpec((2, rows, features), lambda i: (i, 0, 0)),
        out_shape=jax.ShapeDtypeStruct((sources, rows, features), jnp.bfloat16),
        scratch_shapes=[
            pltpu.VMEM((joined, features), jnp.bfloat16),
            pltpu.VMEM((2 * rows, joined), jnp.bfloat16),
        ],
        compiler_params=params(),
        cost_estimate=cost(sources * rows, joined, features),
    )(received, hidden_grad, *flat)


def exchange(value, axes):
    return lax.all_to_all(value, axes, split_axis=0, concat_axis=0, tiled=True)


def chain_gather(mine):
    beside = lax.ppermute(mine, "far", SIDES)
    across = lax.ppermute(mine, "far", MIDDLE)
    return beside, across, lax.ppermute(beside, "far", MIDDLE)


def chain_finish(mine, beside, across, across_far):
    second = lax.ppermute(across, "far", OUTWARD)
    third = lax.ppermute(across_far, "far", OUTWARD)
    return [(mine,), (beside,), (across, second), (across_far, third)]


def add(*terms):
    return sum(term.astype(jnp.float32) for term in terms).astype(jnp.bfloat16)


def chain_scatter(blocks, before_second, before_third):
    own, beside, second, third = blocks
    second, third = add_pairs(
        [(block, lax.ppermute(block, "far", INWARD)) for block in (second, third)], before_second
    )
    across = lax.ppermute(second, "far", MIDDLE)
    (beside,) = add_pairs([(beside, lax.ppermute(third, "far", MIDDLE))], before_third)
    return add(own, across, lax.ppermute(beside, "far", SIDES))


def body(token_grads, router_gates, expert_ids, saved_hidden, up_weight, down_weight):
    tok_count = token_grads.shape[0]
    local_experts, hidden, width = up_weight.shape
    members, far_count = lax.axis_size(GROUP), lax.axis_size("far")
    wide, features = 2 * hidden, width // NEAR
    own_rows = local_experts * hidden
    near = lax.axis_index("near")
    chained = far_count == len(CHAIN)

    chained = far_count == len(CHAIN)

    def halves(weight):
        flat = weight.reshape(own_rows, width)
        own = lax.dynamic_slice_in_dim(flat, near * features, features, axis=1)
        other = lax.dynamic_slice_in_dim(flat, (1 - near) * features, features, axis=1)
        return own, lax.ppermute(other, "near", SWAP)

    down_halves, up_halves = halves(down_weight), halves(up_weight)
    down_own = stack(*down_halves, ())
    if chained:
        far_places = jnp.asarray(CHAIN, jnp.int32)[lax.axis_index("far")]
        reached = chain_gather(down_own)
        down_pieces = chain_finish(down_own, *reached)
        up_own = stack(*up_halves, reached[2:])
        up_reached = chain_gather(up_own)
    else:
        far_places = jnp.arange(far_count, dtype=jnp.int32)
        down_pieces = [(lax.all_gather(down_own, "far", tiled=True),)]
        up_own = stack(*up_halves, ())
    packed, activation, scaled = pack_tokens(
        far_places, expert_ids.T, router_gates.T, saved_hidden, token_grads, members,
        local_experts, (down_halves[1], up_halves[1]),
    )
    received = exchange(packed, GROUP)

    projected = project(received, down_pieces, tok_count, wide)
    if chained:
        beside, across, across_far = up_reached
        up_pieces = chain_finish(up_own, beside, across, pass_on(across_far, (projected,)))
    else:
        up_pieces = [(lax.all_gather(up_own, "far", tiled=True),)]
    partial_value = down_partial(
        received, tok_count, wide, own_rows * NEAR * far_count, far_count if chained else 1,
        (projected,),
    )
    parts = exchange(projected, GROUP)
    hidden_grad, gate_grads = pl.pallas_call(
        hidden_kernel,
        out_shape=(
            jax.ShapeDtypeStruct((members, tok_count, wide), jnp.bfloat16),
            jax.ShapeDtypeStruct((2, tok_count), jnp.bfloat16),
        ),
        compiler_params=params(),
    )(parts, activation, scaled)
    rows_back = input_rows(received, exchange(hidden_grad, GROUP), up_pieces)
    input_grads = unpack_tokens(exchange(rows_back, GROUP))
    if chained:
        sums = chain_scatter(partial_value, (hidden_grad,), (rows_back,))
    else:
        sums = lax.psum_scatter(partial_value[0], "far", scatter_dimension=0, tiled=True)
    kept, passed = sums[:own_rows], lax.ppermute(sums[own_rows:], "near", SWAP)
    down_grads = jnp.concatenate(
        [jnp.where(near == 0, kept, passed), jnp.where(near == 0, passed, kept)], axis=1
    ).reshape(down_weight.shape)
    return (input_grads, gate_grads.T, down_grads)


def solution(mesh):
    sizes = [mesh.shape[name] for name in ("expert", "inner", "outer")]
    split = Mesh(
        mesh.devices.reshape(sizes[0] // NEAR, NEAR, *sizes[1:]),
        ("far", "near", "inner", "outer"),
    )
    rows = P(("far", "near", "inner", "outer"), None)
    weights = P(("far", "near"), None, ("inner", "outer"))
    return jax.shard_map(
        body,
        mesh=split,
        in_specs=(rows, rows, rows, rows, weights, weights),
        out_specs=(rows, rows, weights),
        check_vma=False,
    )
```

```python
import functools
import jax
import jax.numpy as jnp
from jax import lax
from jax.experimental import pallas as pl
from jax.experimental.pallas import tpu as pltpu
from jax.sharding import Mesh, PartitionSpec as P

root_half = 0.7071067811865476
inv_root_tau = 0.3989422804014327
GROUP = ("inner", "outer", "near")
FAR = ("high", "low")
PAIR = 2
BLOCK = 256
TILE = 16
MIB = 1 << 20
SWAP = ((0, 1), (1, 0))


def gelu_parts(preact):
    cumulative = 0.5 * (1.0 + lax.erf(preact * root_half))
    density = inv_root_tau * jnp.exp(-0.5 * preact * preact)
    return (preact * cumulative, cumulative + preact * density)


def params(grant=20):
    return pltpu.CompilerParams(vmem_limit_bytes=grant * MIB)


def cost(rows, inner, columns):
    return pl.CostEstimate(
        flops=2 * rows * inner * columns,
        bytes_accessed=2 * (rows * inner + inner * columns + rows * columns),
        transcendentals=0,
    )


def low_half(shape):
    return lax.broadcasted_iota(jnp.int32, shape, len(shape) - 1) < shape[-1] // 2


def columns_of(pair, wide):
    wanted = lax.broadcasted_iota(jnp.int32, (2, wide), 0)
    return [
        lax.dot_general(
            pair.astype(jnp.bfloat16),
            jnp.where(wanted == k, 1.0, 0.0).astype(jnp.bfloat16),
            (((0,), (0,)), ((), ())),
            preferred_element_type=jnp.float32,
        )
        for k in range(2)
    ]


def stack_kernel(own_ref, other_ref, *refs):
    rows = own_ref.shape[0]
    refs[-1][0:rows, :] = own_ref[...]
    refs[-1][rows:, :] = other_ref[...]


def stack(own, other, before):
    return pl.pallas_call(
        stack_kernel,
        in_specs=[
            *[pl.BlockSpec(memory_space=pltpu.VMEM)] * 2,
            *[pl.BlockSpec(memory_space=pl.ANY) for _ in before],
        ],
        out_shape=jax.ShapeDtypeStruct((2 * own.shape[0], own.shape[1]), own.dtype),
        compiler_params=params(),
    )(own, other, *before)


def add_kernel(count, *refs):
    terms, out_refs = refs[: 2 * count], refs[-count:]
    for at in range(count):
        left, right = terms[2 * at][...], terms[2 * at + 1][...]
        total = left.astype(jnp.float32) + right.astype(jnp.float32)
        out_refs[at][...] = total.astype(out_refs[at].dtype)


def add_pairs(pairs, before):
    flat = [term for pair in pairs for term in pair]
    return pl.pallas_call(
        functools.partial(add_kernel, len(pairs)),
        in_specs=[
            *[pl.BlockSpec(memory_space=pltpu.VMEM) for _ in flat],
            *[pl.BlockSpec(memory_space=pl.ANY) for _ in before],
        ],
        out_shape=[jax.ShapeDtypeStruct(pair[0].shape, pair[0].dtype) for pair in pairs],
        compiler_params=params(),
    )(*flat, *before)


def pack_kernel(
    local_experts, far_ref, ids_ref, gates_ref, preact_ref, tokens_ref, *refs
):
    out_ref, activation_ref, scaled_ref, weighted = refs[-4:]
    blocks, height, features = out_ref.shape
    rows, wide = preact_ref.shape
    far_count = far_ref.shape[0]
    taken = rows * wide // features

    @pl.when(pl.program_id(0) == 0)
    def _():
        activation, slope = gelu_parts(preact_ref[...].astype(jnp.float32))
        gates = jnp.where(low_half((rows, wide)), *columns_of(gates_ref[...], wide))
        activation_ref[...] = activation
        scaled_ref[...] = gates * slope
        weighted[...] = (gates * activation).astype(jnp.bfloat16)

    ids = ids_ref[...]
    local = lax.rem(ids, local_experts)
    line = lax.div(ids, local_experts)
    near = lax.rem(lax.div(line, PAIR), PAIR)
    far = lax.div(line, PAIR * PAIR) * PAIR + lax.rem(line, PAIR)
    far_place = jnp.zeros_like(far)
    for at in range(far_count):
        far_place = jnp.where(far == at, far_ref[at], far_place)
    for block in range(blocks):
        side = lax.rem(near + block, PAIR)
        place = (far_place * PAIR + side) * local_experts + local
        out_ref[block, 0:rows, :] = tokens_ref[:, block * features : (block + 1) * features]
        for at in range(0, features, wide):
            start = at // wide * taken
            out_ref[block, rows : rows + taken, at : at + wide] = weighted[start : start + taken, :]
        last = height - TILE
        out_ref[block, last:, :] = jnp.zeros((TILE, features), jnp.bfloat16)
        out_ref[block, last : last + 2, 0:rows] = place.astype(jnp.bfloat16)


def pack_tokens(far_places, ids, gates, preact, tokens, members, local_experts, before):
    rows, width = tokens.shape
    features = width // members
    each = members // 4
    height = rows + preact.size // features + TILE
    small = jax.ShapeDtypeStruct(preact.shape, jnp.float32)
    whole = [pl.BlockSpec(array.shape, lambda i: (0, 0)) for array in (ids, gates, preact)]
    return pl.pallas_call(
        functools.partial(pack_kernel, local_experts),
        grid=(4,),
        in_specs=[
            pl.BlockSpec(memory_space=pltpu.SMEM),
            *whole,
            pl.BlockSpec((rows, each * features), lambda i: (0, i)),
            *[pl.BlockSpec(memory_space=pl.ANY) for _ in before],
        ],
        out_specs=(pl.BlockSpec((each, height, features), lambda i: (i, 0, 0)), whole[2], whole[2]),
        out_shape=(
            jax.ShapeDtypeStruct((members, height, features), jnp.bfloat16), small, small,
        ),
        scratch_shapes=[pltpu.VMEM(preact.shape, jnp.bfloat16)],
        compiler_params=params(),
    )(far_places, ids, gates, preact, tokens, *before)


def unpack_kernel(parts_ref, out_ref):
    blocks, _, features = parts_ref.shape
    for block in range(blocks):
        out_ref[:, block * features : (block + 1) * features] = parts_ref[block]


def unpack_tokens(parts):
    members, rows, features = parts.shape
    each = members // 4
    return pl.pallas_call(
        unpack_kernel,
        grid=(4,),
        in_specs=[pl.BlockSpec((each, rows, features), lambda i: (i, 0, 0))],
        out_specs=pl.BlockSpec((rows, each * features), lambda i: (0, i)),
        out_shape=jax.ShapeDtypeStruct((rows, members * features), jnp.bfloat16),
        compiler_params=params(),
    )(parts)


def places_of(received_ref, source, rows):
    at = received_ref.shape[1] - TILE
    return received_ref[source, at : at + 2, 0:rows]


def token_rows(received_ref, rows):
    sources, _, features = received_ref.shape
    return received_ref[:, 0:rows, :].reshape(sources * rows, features)


def down_kernel(rows, wide, count, received_ref, *refs):
    out_refs, (turned, numbers, spread) = refs[-3 - count : -3], refs[-3:]
    sources, _, features = received_ref.shape
    hidden, each = wide // 2, BLOCK // (wide // 2)
    taken = rows * wide // features
    for source in range(sources):
        weighted = jnp.concatenate(
            [
                received_ref[source, rows : rows + taken, at : at + wide].astype(jnp.float32)
                for at in range(0, features, wide)
            ]
        )
        lanes = slice(source * rows, (source + 1) * rows)
        turned[:, lanes] = weighted.T
        numbers[:, lanes] = places_of(received_ref, source, rows).astype(jnp.float32)
    number = 0
    for out_ref in out_refs:
        for start in range(0, out_ref.shape[0], BLOCK):
            for expert in range(each):
                spread[expert * hidden : (expert + 1) * hidden, :] = jnp.where(
                    numbers[0:1, :] == number + expert,
                    turned[0:hidden, :],
                    jnp.where(numbers[1:2, :] == number + expert, turned[hidden:, :], 0.0),
                ).astype(jnp.bfloat16)
            number += each
            out_ref[start : start + BLOCK, :] = jnp.dot(
                spread[...], token_rows(received_ref, rows), preferred_element_type=jnp.float32
            ).astype(out_ref.dtype)


def down_partial(received, rows, wide, total_rows, count, before):
    sources, _, features = received.shape
    total = sources * rows
    return pl.pallas_call(
        functools.partial(down_kernel, rows, wide, count),
        in_specs=[
            pl.BlockSpec(memory_space=pltpu.VMEM),
            *[pl.BlockSpec(memory_space=pl.ANY) for _ in before],
        ],
        out_shape=[jax.ShapeDtypeStruct((total_rows // count, features), jnp.bfloat16)] * count,
        scratch_shapes=[
            pltpu.VMEM((wide, total), jnp.float32),
            pltpu.VMEM((2, total), jnp.float32),
            pltpu.VMEM((BLOCK, total), jnp.bfloat16),
        ],
        compiler_params=params(),
        cost_estimate=cost(total_rows, total, features),
    )(received, *before)


def lane_numbers(received_ref, rows, wide):
    sources = received_ref.shape[0]
    low = low_half((sources * rows, wide))
    found = [
        columns_of(places_of(received_ref, source, rows), wide)
        for source in range(sources)
    ]
    odd = jnp.where(low, 0.0, 1.0)
    return low, *[jnp.concatenate([pair[k] for pair in found]) - odd for k in range(2)]


def join(piece_refs, full):
    start = 0
    for ref in piece_refs:
        full[start : start + ref.shape[0], :] = ref[...]
        start += ref.shape[0]


def project_kernel(received_ref, *refs):
    piece_refs, out_ref = refs[:-1], refs[-1]
    sources, rows, wide = out_ref.shape
    low, first, second = lane_numbers(received_ref, rows, wide)
    tokens = token_rows(received_ref, rows)
    sums = [jnp.zeros((sources * rows, wide), jnp.float32) for _ in range(2)]
    number = 0.0
    for ref, start in [(ref, at) for ref in piece_refs for at in range(0, ref.shape[0], BLOCK)]:
        product = lax.dot_general(
            tokens,
            ref[start : start + BLOCK, :],
            (((1,), (1,)), ((), ())),
            preferred_element_type=jnp.float32,
        )
        for at in range(0, BLOCK, wide):
            part = product[:, at : at + wide]
            sums[0] = jnp.where(first == number, part, sums[0])
            sums[1] = jnp.where(second == number, part, sums[1])
            number += 2.0
    folded = [value + pltpu.roll(value, wide // 2, 1) for value in sums]
    value = jnp.where(low, folded[0], folded[1]).astype(out_ref.dtype)
    out_ref[...] = value.reshape(out_ref.shape)


def project(received, pieces, rows, wide):
    sources, height, features = received.shape
    return pl.pallas_call(
        project_kernel,
        grid=(sources // 2,),
        in_specs=[
            pl.BlockSpec((2, height, features), lambda i: (i, 0, 0)),
            *[pl.BlockSpec(piece.shape, lambda i: (0, 0)) for piece in pieces],
        ],
        out_specs=pl.BlockSpec((2, rows, wide), lambda i: (i, 0, 0)),
        out_shape=jax.ShapeDtypeStruct((sources, rows, wide), jnp.bfloat16),
        compiler_params=params(),
        cost_estimate=cost(sources * rows, features, sum(p.shape[0] for p in pieces)),
    )(received, *pieces)


def hidden_kernel(parts_ref, activation_ref, scaled_ref, hidden_ref, gate_ref):
    projected = parts_ref[0].astype(jnp.float32)
    for source in range(1, parts_ref.shape[0]):
        projected = projected + parts_ref[source].astype(jnp.float32)
    wide = projected.shape[1]
    half = lax.broadcasted_iota(jnp.int32, (8, wide), 1) // (wide // 2)
    wanted = lax.broadcasted_iota(jnp.int32, (8, wide), 0)
    sums = lax.dot_general(
        jnp.where(wanted == half, 1.0, 0.0),
        activation_ref[...] * projected,
        (((1,), (1,)), ((), ())),
        precision=lax.Precision.HIGHEST,
        preferred_element_type=jnp.float32,
    )
    gate_ref[...] = sums[0:2, :].astype(gate_ref.dtype)
    hidden = (projected * scaled_ref[...]).astype(hidden_ref.dtype)
    for source in range(hidden_ref.shape[0]):
        hidden_ref[source] = hidden


def input_kernel(received_ref, hidden_ref, *refs):
    piece_refs, out_ref, full, spread = refs[:-3], refs[-3], refs[-2], refs[-1]
    pl.when(pl.program_id(0) == 0)(lambda: join(piece_refs, full))
    sources, rows, wide = hidden_ref.shape
    low, first, second = lane_numbers(received_ref, rows, wide)
    values = hidden_ref[...].reshape(sources * rows, wide).astype(jnp.float32)
    swapped = pltpu.roll(values, wide // 2, 1)
    one = jnp.where(low, values, swapped)
    two = jnp.where(low, swapped, values)
    for start in range(0, full.shape[0], wide):
        number = start // wide * 2.0
        spread[:, start : start + wide] = jnp.where(
            first == number, one, jnp.where(second == number, two, 0.0)
        ).astype(jnp.bfloat16)
    out_ref[...] = (
        jnp.dot(spread[...], full[...], preferred_element_type=jnp.float32)
        .astype(out_ref.dtype)
        .reshape(out_ref.shape)
    )


def input_rows(received, hidden_grad, pieces):
    sources, rows, wide = hidden_grad.shape
    joined, features = sum(piece.shape[0] for piece in pieces), pieces[0].shape[1]
    return pl.pallas_call(
        input_kernel,
        grid=(sources // 2,),
        in_specs=[
            pl.BlockSpec((2, received.shape[1], features), lambda i: (i, 0, 0)),
            pl.BlockSpec((2, rows, wide), lambda i: (i, 0, 0)),
            *[pl.BlockSpec(piece.shape, lambda i: (0, 0)) for piece in pieces],
        ],
        out_specs=pl.BlockSpec((2, rows, features), lambda i: (i, 0, 0)),
        out_shape=jax.ShapeDtypeStruct((sources, rows, features), jnp.bfloat16),
        scratch_shapes=[
            pltpu.VMEM((joined, features), jnp.bfloat16),
            pltpu.VMEM((2 * rows, joined), jnp.bfloat16),
        ],
        compiler_params=params(),
        cost_estimate=cost(sources * rows, joined, features),
    )(received, hidden_grad, *pieces)


def exchange(value, axes):
    return lax.all_to_all(value, axes, split_axis=0, concat_axis=0, tiled=True)


def swap(value, axis):
    return lax.ppermute(value, axis, SWAP)


def add(*terms):
    return sum(term.astype(jnp.float32) for term in terms).astype(jnp.bfloat16)


def body(token_grads, router_gates, expert_ids, saved_hidden, up_weight, down_weight):
    tok_count = token_grads.shape[0]
    local_experts, hidden, width = up_weight.shape
    members, far_count = lax.axis_size(GROUP), lax.axis_size(FAR)
    wide, features = 2 * hidden, width // PAIR
    own_rows = local_experts * hidden
    near = lax.axis_index("near")
    paired = lax.axis_size("high") == PAIR

    def halves(weight):
        flat = weight.reshape(own_rows, width)
        own = lax.dynamic_slice_in_dim(flat, near * features, features, axis=1)
        other = lax.dynamic_slice_in_dim(flat, (1 - near) * features, features, axis=1)
        return own, swap(other, "near")

    down_halves, up_halves = halves(down_weight), halves(up_weight)
    down_own = stack(*down_halves, ())
    far_places = jnp.arange(far_count, dtype=jnp.int32)
    if paired:
        high_place = far_places // PAIR ^ lax.axis_index("high")
        far_places = (far_places % PAIR ^ lax.axis_index("low")) * PAIR + high_place
        beside = swap(down_own, "high")
        down_pieces = [down_own, beside, swap(down_own, "low"), swap(beside, "low")]
        up_own = stack(*up_halves, (beside,))
        up_beside = swap(up_own, "high")
        up_low = swap(stack(*up_halves, down_pieces[2:]), "low")
        up_pieces = [up_own, up_beside, up_low, swap(up_beside, "low")]
    else:
        down_pieces = [lax.all_gather(down_own, FAR, tiled=True)]
        up_pieces = [lax.all_gather(stack(*up_halves, ()), FAR, tiled=True)]
    packed, activation, scaled = pack_tokens(
        far_places, expert_ids.T, router_gates.T, saved_hidden, token_grads, members,
        local_experts, (down_halves[1], up_halves[1]),
    )
    received = exchange(packed, GROUP)

    projected = project(received, down_pieces, tok_count, wide)
    partial_value = down_partial(
        received, tok_count, wide, own_rows * PAIR * far_count, far_count if paired else 1,
        (projected,),
    )
    parts = exchange(projected, GROUP)
    hidden_grad, gate_grads = pl.pallas_call(
        hidden_kernel,
        out_shape=(
            jax.ShapeDtypeStruct((members, tok_count, wide), jnp.bfloat16),
            jax.ShapeDtypeStruct((2, tok_count), jnp.bfloat16),
        ),
        compiler_params=params(),
    )(parts, activation, scaled)
    rows_back = input_rows(received, exchange(hidden_grad, GROUP), up_pieces)
    input_grads = unpack_tokens(exchange(rows_back, GROUP))

    if paired:
        own, beside, low, low_beside = partial_value
        (beside,) = add_pairs([(beside, swap(low_beside, "low"))], (hidden_grad,))
        sums = add(own, swap(low, "low"), swap(beside, "high"))
    else:
        sums = lax.psum_scatter(partial_value[0], FAR, scatter_dimension=0, tiled=True)
    kept, passed = sums[:own_rows], swap(sums[own_rows:], "near")
    down_grads = jnp.concatenate(
        [jnp.where(near == 0, kept, passed), jnp.where(near == 0, passed, kept)], axis=1
    ).reshape(down_weight.shape)
    return (input_grads, gate_grads.T, down_grads)


def solution(mesh):
    sizes = [mesh.shape[name] for name in ("expert", "inner", "outer")]
    expert = ("high", "near", "low")
    split = Mesh(
        mesh.devices.reshape(sizes[0] // PAIR**2, PAIR, PAIR, *sizes[1:]),
        (*expert, "inner", "outer"),
    )
    rows = P((*expert, "inner", "outer"), None)
    weights = P(expert, None, ("inner", "outer"))
    return jax.shard_map(
        body,
        mesh=split,
        in_specs=(rows, rows, rows, rows, weights, weights),
        out_specs=(rows, rows, weights),
        check_vma=False,
    )
```

```python
import functools
import jax
import jax.numpy as jnp
from jax import lax
from jax.experimental import pallas as pl
from jax.experimental.pallas import tpu as pltpu
from jax.sharding import Mesh, PartitionSpec as P

root_half = 0.7071067811865476
inv_root_tau = 0.3989422804014327
GROUP = ("inner", "outer", "near")
FAR = ("high", "low")
PAIR = 2
BLOCK = 256
TILE = 16
MIB = 1 << 20
SWAP = ((0, 1), (1, 0))


def gelu_parts(preact):
    cumulative = 0.5 * (1.0 + lax.erf(preact * root_half))
    density = inv_root_tau * jnp.exp(-0.5 * preact * preact)
    return (preact * cumulative, cumulative + preact * density)


def params(grant=20):
    return pltpu.CompilerParams(vmem_limit_bytes=grant * MIB)


def cost(rows, inner, columns):
    return pl.CostEstimate(
        flops=2 * rows * inner * columns,
        bytes_accessed=2 * (rows * inner + inner * columns + rows * columns),
        transcendentals=0,
    )


def low_half(shape):
    return lax.broadcasted_iota(jnp.int32, shape, len(shape) - 1) < shape[-1] // 2


def columns_of(pair, wide):
    wanted = lax.broadcasted_iota(jnp.int32, (2, wide), 0)
    return [
        lax.dot_general(
            pair.astype(jnp.bfloat16),
            jnp.where(wanted == k, 1.0, 0.0).astype(jnp.bfloat16),
            (((0,), (0,)), ((), ())),
            preferred_element_type=jnp.float32,
        )
        for k in range(2)
    ]


def stack_kernel(own_ref, other_ref, *refs):
    rows = own_ref.shape[0]
    refs[-1][0:rows, :] = own_ref[...]
    refs[-1][rows:, :] = other_ref[...]


def stack(own, other, before):
    return pl.pallas_call(
        stack_kernel,
        in_specs=[
            *[pl.BlockSpec(memory_space=pltpu.VMEM)] * 2,
            *[pl.BlockSpec(memory_space=pl.ANY) for _ in before],
        ],
        out_shape=jax.ShapeDtypeStruct((2 * own.shape[0], own.shape[1]), own.dtype),
        compiler_params=params(),
    )(own, other, *before)


def add_kernel(count, *refs):
    terms, out_refs = refs[: 2 * count], refs[-count:]
    for at in range(count):
        left, right = terms[2 * at][...], terms[2 * at + 1][...]
        total = left.astype(jnp.float32) + right.astype(jnp.float32)
        out_refs[at][...] = total.astype(out_refs[at].dtype)


def add_pairs(pairs, before):
    flat = [term for pair in pairs for term in pair]
    return pl.pallas_call(
        functools.partial(add_kernel, len(pairs)),
        in_specs=[
            *[pl.BlockSpec(memory_space=pltpu.VMEM) for _ in flat],
            *[pl.BlockSpec(memory_space=pl.ANY) for _ in before],
        ],
        out_shape=[jax.ShapeDtypeStruct(pair[0].shape, pair[0].dtype) for pair in pairs],
        compiler_params=params(),
    )(*flat, *before)


def pack_kernel(
    local_experts, far_ref, ids_ref, gates_ref, preact_ref, tokens_ref, *refs
):
    out_ref, activation_ref, scaled_ref, weighted = refs[-4:]
    blocks, height, features = out_ref.shape
    rows, wide = preact_ref.shape
    far_count = far_ref.shape[0]
    taken = rows * wide // features

    @pl.when(pl.program_id(0) == 0)
    def _():
        activation, slope = gelu_parts(preact_ref[...].astype(jnp.float32))
        gates = jnp.where(low_half((rows, wide)), *columns_of(gates_ref[...], wide))
        activation_ref[...] = activation
        scaled_ref[...] = gates * slope
        weighted[...] = (gates * activation).astype(jnp.bfloat16)

    ids = ids_ref[...]
    local = lax.rem(ids, local_experts)
    line = lax.div(ids, local_experts)
    near = lax.rem(lax.div(line, PAIR), PAIR)
    far = lax.div(line, PAIR * PAIR) * PAIR + lax.rem(line, PAIR)
    far_place = jnp.zeros_like(far)
    for at in range(far_count):
        far_place = jnp.where(far == at, far_ref[at], far_place)
    for block in range(blocks):
        side = lax.rem(near + block, PAIR)
        place = (far_place * PAIR + side) * local_experts + local
        out_ref[block, 0:rows, :] = tokens_ref[:, block * features : (block + 1) * features]
        for at in range(0, features, wide):
            start = at // wide * taken
            out_ref[block, rows : rows + taken, at : at + wide] = weighted[start : start + taken, :]
        last = height - TILE
        out_ref[block, last:, :] = jnp.zeros((TILE, features), jnp.bfloat16)
        out_ref[block, last : last + 2, 0:rows] = place.astype(jnp.bfloat16)


def pack_tokens(far_places, ids, gates, preact, tokens, members, local_experts, before):
    rows, width = tokens.shape
    features = width // members
    each = members // 4
    height = rows + preact.size // features + TILE
    small = jax.ShapeDtypeStruct(preact.shape, jnp.float32)
    whole = [pl.BlockSpec(array.shape, lambda i: (0, 0)) for array in (ids, gates, preact)]
    return pl.pallas_call(
        functools.partial(pack_kernel, local_experts),
        grid=(4,),
        in_specs=[
            pl.BlockSpec(memory_space=pltpu.SMEM),
            *whole,
            pl.BlockSpec((rows, each * features), lambda i: (0, i)),
            *[pl.BlockSpec(memory_space=pl.ANY) for _ in before],
        ],
        out_specs=(pl.BlockSpec((each, height, features), lambda i: (i, 0, 0)), whole[2], whole[2]),
        out_shape=(
            jax.ShapeDtypeStruct((members, height, features), jnp.bfloat16), small, small,
        ),
        scratch_shapes=[pltpu.VMEM(preact.shape, jnp.bfloat16)],
        compiler_params=params(),
    )(far_places, ids, gates, preact, tokens, *before)


def unpack_kernel(parts_ref, out_ref):
    blocks, _, features = parts_ref.shape
    for block in range(blocks):
        out_ref[:, block * features : (block + 1) * features] = parts_ref[block]


def unpack_tokens(parts):
    members, rows, features = parts.shape
    each = members // 4
    return pl.pallas_call(
        unpack_kernel,
        grid=(4,),
        in_specs=[pl.BlockSpec((each, rows, features), lambda i: (i, 0, 0))],
        out_specs=pl.BlockSpec((rows, each * features), lambda i: (0, i)),
        out_shape=jax.ShapeDtypeStruct((rows, members * features), jnp.bfloat16),
        compiler_params=params(),
    )(parts)


def places_of(received_ref, source, rows):
    at = received_ref.shape[1] - TILE
    return received_ref[source, at : at + 2, 0:rows]


def token_rows(received_ref, rows):
    sources, _, features = received_ref.shape
    return received_ref[:, 0:rows, :].reshape(sources * rows, features)


def down_kernel(rows, wide, count, received_ref, *refs):
    out_refs, (turned, numbers, spread) = refs[-3 - count : -3], refs[-3:]
    sources, _, features = received_ref.shape
    hidden, each = wide // 2, BLOCK // (wide // 2)
    taken = rows * wide // features
    for source in range(sources):
        weighted = jnp.concatenate(
            [
                received_ref[source, rows : rows + taken, at : at + wide].astype(jnp.float32)
                for at in range(0, features, wide)
            ]
        )
        lanes = slice(source * rows, (source + 1) * rows)
        turned[:, lanes] = weighted.T
        numbers[:, lanes] = places_of(received_ref, source, rows).astype(jnp.float32)
    number = 0
    for out_ref in out_refs:
        for start in range(0, out_ref.shape[0], BLOCK):
            for expert in range(each):
                spread[expert * hidden : (expert + 1) * hidden, :] = jnp.where(
                    numbers[0:1, :] == number + expert,
                    turned[0:hidden, :],
                    jnp.where(numbers[1:2, :] == number + expert, turned[hidden:, :], 0.0),
                ).astype(jnp.bfloat16)
            number += each
            out_ref[start : start + BLOCK, :] = jnp.dot(
                spread[...], token_rows(received_ref, rows), preferred_element_type=jnp.float32
            ).astype(out_ref.dtype)


def down_partial(received, rows, wide, total_rows, count, before):
    sources, _, features = received.shape
    total = sources * rows
    return pl.pallas_call(
        functools.partial(down_kernel, rows, wide, count),
        in_specs=[
            pl.BlockSpec(memory_space=pltpu.VMEM),
            *[pl.BlockSpec(memory_space=pl.ANY) for _ in before],
        ],
        out_shape=[jax.ShapeDtypeStruct((total_rows // count, features), jnp.bfloat16)] * count,
        scratch_shapes=[
            pltpu.VMEM((wide, total), jnp.float32),
            pltpu.VMEM((2, total), jnp.float32),
            pltpu.VMEM((BLOCK, total), jnp.bfloat16),
        ],
        compiler_params=params(),
        cost_estimate=cost(total_rows, total, features),
    )(received, *before)


def lane_numbers(received_ref, rows, wide):
    sources = received_ref.shape[0]
    low = low_half((sources * rows, wide))
    found = [
        columns_of(places_of(received_ref, source, rows), wide)
        for source in range(sources)
    ]
    odd = jnp.where(low, 0.0, 1.0)
    return low, *[jnp.concatenate([pair[k] for pair in found]) - odd for k in range(2)]


def join(piece_refs, full):
    start = 0
    for ref in piece_refs:
        full[start : start + ref.shape[0], :] = ref[...]
        start += ref.shape[0]


def project_kernel(received_ref, *refs):
    piece_refs, out_ref = refs[:-1], refs[-1]
    sources, rows, wide = out_ref.shape
    low, first, second = lane_numbers(received_ref, rows, wide)
    tokens = token_rows(received_ref, rows)
    sums = [jnp.zeros((sources * rows, wide), jnp.float32) for _ in range(2)]
    number = 0.0
    for ref, start in [(ref, at) for ref in piece_refs for at in range(0, ref.shape[0], BLOCK)]:
        product = lax.dot_general(
            tokens,
            ref[start : start + BLOCK, :],
            (((1,), (1,)), ((), ())),
            preferred_element_type=jnp.float32,
        )
        for at in range(0, BLOCK, wide):
            part = product[:, at : at + wide]
            sums[0] = jnp.where(first == number, part, sums[0])
            sums[1] = jnp.where(second == number, part, sums[1])
            number += 2.0
    folded = [value + pltpu.roll(value, wide // 2, 1) for value in sums]
    value = jnp.where(low, folded[0], folded[1]).astype(out_ref.dtype)
    out_ref[...] = value.reshape(out_ref.shape)


def project(received, pieces, rows, wide):
    sources, height, features = received.shape
    return pl.pallas_call(
        project_kernel,
        grid=(sources // 2,),
        in_specs=[
            pl.BlockSpec((2, height, features), lambda i: (i, 0, 0)),
            *[pl.BlockSpec(piece.shape, lambda i: (0, 0)) for piece in pieces],
        ],
        out_specs=pl.BlockSpec((2, rows, wide), lambda i: (i, 0, 0)),
        out_shape=jax.ShapeDtypeStruct((sources, rows, wide), jnp.bfloat16),
        compiler_params=params(),
        cost_estimate=cost(sources * rows, features, sum(p.shape[0] for p in pieces)),
    )(received, *pieces)


def hidden_kernel(parts_ref, activation_ref, scaled_ref, *refs):
    hidden_ref, gate_ref = refs[-2:]
    projected = parts_ref[0].astype(jnp.float32)
    for source in range(1, parts_ref.shape[0]):
        projected = projected + parts_ref[source].astype(jnp.float32)
    wide = projected.shape[1]
    half = lax.broadcasted_iota(jnp.int32, (8, wide), 1) // (wide // 2)
    wanted = lax.broadcasted_iota(jnp.int32, (8, wide), 0)
    sums = lax.dot_general(
        jnp.where(wanted == half, 1.0, 0.0),
        activation_ref[...] * projected,
        (((1,), (1,)), ((), ())),
        precision=lax.Precision.HIGHEST,
        preferred_element_type=jnp.float32,
    )
    gate_ref[...] = sums[0:2, :].astype(gate_ref.dtype)
    hidden = (projected * scaled_ref[...]).astype(hidden_ref.dtype)
    for source in range(hidden_ref.shape[0]):
        hidden_ref[source] = hidden


def input_kernel(count, received_ref, hidden_ref, *refs):
    piece_refs, (out_ref, full, spread) = refs[:count], refs[-3:]
    pl.when(pl.program_id(0) == 0)(lambda: join(piece_refs, full))
    sources, rows, wide = hidden_ref.shape
    low, first, second = lane_numbers(received_ref, rows, wide)
    values = hidden_ref[...].reshape(sources * rows, wide).astype(jnp.float32)
    swapped = pltpu.roll(values, wide // 2, 1)
    one = jnp.where(low, values, swapped)
    two = jnp.where(low, swapped, values)
    for start in range(0, full.shape[0], wide):
        number = start // wide * 2.0
        spread[:, start : start + wide] = jnp.where(
            first == number, one, jnp.where(second == number, two, 0.0)
        ).astype(jnp.bfloat16)
    out_ref[...] = (
        jnp.dot(spread[...], full[...], preferred_element_type=jnp.float32)
        .astype(out_ref.dtype)
        .reshape(out_ref.shape)
    )


def input_rows(received, hidden_grad, pieces, before):
    sources, rows, wide = hidden_grad.shape
    joined, features = sum(piece.shape[0] for piece in pieces), pieces[0].shape[1]
    return pl.pallas_call(
        functools.partial(input_kernel, len(pieces)),
        grid=(sources // 2,),
        in_specs=[
            pl.BlockSpec((2, received.shape[1], features), lambda i: (i, 0, 0)),
            pl.BlockSpec((2, rows, wide), lambda i: (i, 0, 0)),
            *[pl.BlockSpec(piece.shape, lambda i: (0, 0)) for piece in pieces],
            *[pl.BlockSpec(memory_space=pl.ANY) for _ in before],
        ],
        out_specs=pl.BlockSpec((2, rows, features), lambda i: (i, 0, 0)),
        out_shape=jax.ShapeDtypeStruct((sources, rows, features), jnp.bfloat16),
        scratch_shapes=[
            pltpu.VMEM((joined, features), jnp.bfloat16),
            pltpu.VMEM((2 * rows, joined), jnp.bfloat16),
        ],
        compiler_params=params(),
        cost_estimate=cost(sources * rows, joined, features),
    )(received, hidden_grad, *pieces, *before)


def exchange(value, axes):
    return lax.all_to_all(value, axes, split_axis=0, concat_axis=0, tiled=True)


def swap(value, axis):
    return lax.ppermute(value, axis, SWAP)


def add(*terms):
    return sum(term.astype(jnp.float32) for term in terms).astype(jnp.bfloat16)


def body(token_grads, router_gates, expert_ids, saved_hidden, up_weight, down_weight):
    tok_count = token_grads.shape[0]
    local_experts, hidden, width = up_weight.shape
    members, far_count = lax.axis_size(GROUP), lax.axis_size(FAR)
    wide, features = 2 * hidden, width // PAIR
    own_rows = local_experts * hidden
    near = lax.axis_index("near")
    paired = lax.axis_size("high") == PAIR

    def halves(weight):
        flat = weight.reshape(own_rows, width)
        own = lax.dynamic_slice_in_dim(flat, near * features, features, axis=1)
        other = lax.dynamic_slice_in_dim(flat, (1 - near) * features, features, axis=1)
        return own, swap(other, "near")

    down_halves, up_halves = halves(down_weight), halves(up_weight)
    down_own = stack(*down_halves, ())
    first = [down_halves[1], up_halves[1]]
    far_places = jnp.arange(far_count, dtype=jnp.int32)
    if paired:
        high_place = far_places // PAIR ^ lax.axis_index("high")
        far_places = (far_places % PAIR ^ lax.axis_index("low")) * PAIR + high_place
        beside = swap(down_own, "high")
        down_pieces = [down_own, beside, swap(down_own, "low"), swap(beside, "low")]
        first += [down_pieces[2]]
        up_own = stack(*up_halves, (beside,))
        up_beside = swap(up_own, "high")
        up_low = swap(stack(*up_halves, down_pieces[2:]), "low")
        up_pieces = [up_own, up_beside, up_low, swap(up_beside, "low")]
    else:
        down_pieces = [lax.all_gather(down_own, FAR, tiled=True)]
        up_pieces = [lax.all_gather(stack(*up_halves, ()), FAR, tiled=True)]
    packed, activation, scaled = pack_tokens(
        far_places, expert_ids.T, router_gates.T, saved_hidden, token_grads, members,
        local_experts, first,
    )
    received = exchange(packed, GROUP)

    projected = project(received, down_pieces, tok_count, wide)
    partial_value = down_partial(
        received, tok_count, wide, own_rows * PAIR * far_count, far_count if paired else 1,
        (projected,),
    )
    parts = exchange(projected, GROUP)
    hidden_grad, gate_grads = pl.pallas_call(
        hidden_kernel,
        in_specs=[
            *[pl.BlockSpec(memory_space=pltpu.VMEM) for _ in range(3)],
            *[pl.BlockSpec(memory_space=pl.ANY) for _ in partial_value],
        ],
        out_shape=(
            jax.ShapeDtypeStruct((members, tok_count, wide), jnp.bfloat16),
            jax.ShapeDtypeStruct((2, tok_count), jnp.bfloat16),
        ),
        compiler_params=params(),
    )(parts, activation, scaled, *partial_value)
    if paired:
        own, beside, low, low_beside = partial_value
        before = add_pairs([(beside, swap(low_beside, "low"))], ())
        sums = add(own, swap(low, "low"), swap(before[0], "high"))
    else:
        before = ()
        sums = lax.psum_scatter(partial_value[0], FAR, scatter_dimension=0, tiled=True)
    rows_back = input_rows(received, exchange(hidden_grad, GROUP), up_pieces, before)
    input_grads = unpack_tokens(exchange(rows_back, GROUP))

    kept, passed = sums[:own_rows], swap(sums[own_rows:], "near")
    down_grads = jnp.concatenate(
        [jnp.where(near == 0, kept, passed), jnp.where(near == 0, passed, kept)], axis=1
    ).reshape(down_weight.shape)
    return (input_grads, gate_grads.T, down_grads)


def solution(mesh):
    sizes = [mesh.shape[name] for name in ("expert", "inner", "outer")]
    expert = ("high", "near", "low")
    split = Mesh(
        mesh.devices.reshape(sizes[0] // PAIR**2, PAIR, PAIR, *sizes[1:]),
        (*expert, "inner", "outer"),
    )
    rows = P((*expert, "inner", "outer"), None)
    weights = P(expert, None, ("inner", "outer"))
    return jax.shard_map(
        body,
        mesh=split,
        in_specs=(rows, rows, rows, rows, weights, weights),
        out_specs=(rows, rows, weights),
        check_vma=False,
    )
```

```python
import functools
import jax
import jax.numpy as jnp
from jax import lax
from jax.experimental import pallas as pl
from jax.experimental.pallas import tpu as pltpu
from jax.sharding import Mesh, PartitionSpec as P

root_half = 0.7071067811865476
inv_root_tau = 0.3989422804014327
GROUP = ("inner", "outer", "near")
FAR = ("high", "low")
PAIR = 2
BLOCK = 256
TILE = 16
MIB = 1 << 20
SWAP = ((0, 1), (1, 0))


def gelu_parts(preact):
    cumulative = 0.5 * (1.0 + lax.erf(preact * root_half))
    density = inv_root_tau * jnp.exp(-0.5 * preact * preact)
    return (preact * cumulative, cumulative + preact * density)


def params(grant=20):
    return pltpu.CompilerParams(vmem_limit_bytes=grant * MIB)


def cost(rows, inner, columns):
    return pl.CostEstimate(
        flops=2 * rows * inner * columns,
        bytes_accessed=2 * (rows * inner + inner * columns + rows * columns),
        transcendentals=0,
    )


def low_half(shape):
    return lax.broadcasted_iota(jnp.int32, shape, len(shape) - 1) < shape[-1] // 2


def columns_of(pair, wide):
    wanted = lax.broadcasted_iota(jnp.int32, (2, wide), 0)
    return [
        lax.dot_general(
            pair.astype(jnp.bfloat16),
            jnp.where(wanted == k, 1.0, 0.0).astype(jnp.bfloat16),
            (((0,), (0,)), ((), ())),
            preferred_element_type=jnp.float32,
        )
        for k in range(2)
    ]


def stack_kernel(own_ref, other_ref, *refs):
    rows = own_ref.shape[0]
    refs[-1][0:rows, :] = own_ref[...]
    refs[-1][rows:, :] = other_ref[...]


def stack(own, other, before):
    return pl.pallas_call(
        stack_kernel,
        in_specs=[
            *[pl.BlockSpec(memory_space=pltpu.VMEM)] * 2,
            *[pl.BlockSpec(memory_space=pl.ANY) for _ in before],
        ],
        out_shape=jax.ShapeDtypeStruct((2 * own.shape[0], own.shape[1]), own.dtype),
        compiler_params=params(),
    )(own, other, *before)


def add_kernel(count, *refs):
    terms, out_refs = refs[: 2 * count], refs[-count:]
    for at in range(count):
        left, right = terms[2 * at][...], terms[2 * at + 1][...]
        total = left.astype(jnp.float32) + right.astype(jnp.float32)
        out_refs[at][...] = total.astype(out_refs[at].dtype)


def add_pairs(pairs, before):
    flat = [term for pair in pairs for term in pair]
    return pl.pallas_call(
        functools.partial(add_kernel, len(pairs)),
        in_specs=[
            *[pl.BlockSpec(memory_space=pltpu.VMEM) for _ in flat],
            *[pl.BlockSpec(memory_space=pl.ANY) for _ in before],
        ],
        out_shape=[jax.ShapeDtypeStruct(pair[0].shape, pair[0].dtype) for pair in pairs],
        compiler_params=params(),
    )(*flat, *before)


def pack_kernel(
    local_experts, far_ref, ids_ref, gates_ref, preact_ref, tokens_ref, *refs
):
    out_ref, activation_ref, scaled_ref, weighted = refs[-4:]
    blocks, height, features = out_ref.shape
    rows, wide = preact_ref.shape
    far_count = far_ref.shape[0]
    taken = rows * wide // features

    @pl.when(pl.program_id(0) == 0)
    def _():
        activation, slope = gelu_parts(preact_ref[...].astype(jnp.float32))
        gates = jnp.where(low_half((rows, wide)), *columns_of(gates_ref[...], wide))
        activation_ref[...] = activation
        scaled_ref[...] = gates * slope
        weighted[...] = (gates * activation).astype(jnp.bfloat16)

    ids = ids_ref[...]
    local = lax.rem(ids, local_experts)
    line = lax.div(ids, local_experts)
    far, near = lax.div(line, PAIR), lax.rem(line, PAIR)
    far_place = jnp.zeros_like(far)
    for at in range(far_count):
        far_place = jnp.where(far == at, far_ref[at], far_place)
    for block in range(blocks):
        side = lax.rem(near + block, PAIR)
        place = (far_place * PAIR + side) * local_experts + local
        out_ref[block, 0:rows, :] = tokens_ref[:, block * features : (block + 1) * features]
        for at in range(0, features, wide):
            start = at // wide * taken
            out_ref[block, rows : rows + taken, at : at + wide] = weighted[start : start + taken, :]
        last = height - TILE
        out_ref[block, last:, :] = jnp.zeros((TILE, features), jnp.bfloat16)
        out_ref[block, last : last + 2, 0:rows] = place.astype(jnp.bfloat16)


def pack_tokens(far_places, ids, gates, preact, tokens, members, local_experts, before):
    rows, width = tokens.shape
    features = width // members
    each = members // 4
    height = rows + preact.size // features + TILE
    small = jax.ShapeDtypeStruct(preact.shape, jnp.float32)
    whole = [pl.BlockSpec(array.shape, lambda i: (0, 0)) for array in (ids, gates, preact)]
    return pl.pallas_call(
        functools.partial(pack_kernel, local_experts),
        grid=(4,),
        in_specs=[
            pl.BlockSpec(memory_space=pltpu.SMEM),
            *whole,
            pl.BlockSpec((rows, each * features), lambda i: (0, i)),
            *[pl.BlockSpec(memory_space=pl.ANY) for _ in before],
        ],
        out_specs=(pl.BlockSpec((each, height, features), lambda i: (i, 0, 0)), whole[2], whole[2]),
        out_shape=(
            jax.ShapeDtypeStruct((members, height, features), jnp.bfloat16), small, small,
        ),
        scratch_shapes=[pltpu.VMEM(preact.shape, jnp.bfloat16)],
        compiler_params=params(),
    )(far_places, ids, gates, preact, tokens, *before)


def unpack_kernel(parts_ref, out_ref):
    blocks, _, features = parts_ref.shape
    for block in range(blocks):
        out_ref[:, block * features : (block + 1) * features] = parts_ref[block]


def unpack_tokens(parts):
    members, rows, features = parts.shape
    each = members // 4
    return pl.pallas_call(
        unpack_kernel,
        grid=(4,),
        in_specs=[pl.BlockSpec((each, rows, features), lambda i: (i, 0, 0))],
        out_specs=pl.BlockSpec((rows, each * features), lambda i: (0, i)),
        out_shape=jax.ShapeDtypeStruct((rows, members * features), jnp.bfloat16),
        compiler_params=params(),
    )(parts)


def places_of(received_ref, source, rows):
    at = received_ref.shape[1] - TILE
    return received_ref[source, at : at + 2, 0:rows]


def token_rows(received_ref, rows):
    sources, _, features = received_ref.shape
    return received_ref[:, 0:rows, :].reshape(sources * rows, features)


def down_kernel(rows, wide, count, received_ref, *refs):
    out_refs, (turned, numbers, spread) = refs[-3 - count : -3], refs[-3:]
    sources, _, features = received_ref.shape
    hidden, each = wide // 2, BLOCK // (wide // 2)
    taken = rows * wide // features
    for source in range(sources):
        weighted = jnp.concatenate(
            [
                received_ref[source, rows : rows + taken, at : at + wide].astype(jnp.float32)
                for at in range(0, features, wide)
            ]
        )
        lanes = slice(source * rows, (source + 1) * rows)
        turned[:, lanes] = weighted.T
        numbers[:, lanes] = places_of(received_ref, source, rows).astype(jnp.float32)
    number = 0
    for out_ref in out_refs:
        for start in range(0, out_ref.shape[0], BLOCK):
            for expert in range(each):
                spread[expert * hidden : (expert + 1) * hidden, :] = jnp.where(
                    numbers[0:1, :] == number + expert,
                    turned[0:hidden, :],
                    jnp.where(numbers[1:2, :] == number + expert, turned[hidden:, :], 0.0),
                ).astype(jnp.bfloat16)
            number += each
            out_ref[start : start + BLOCK, :] = jnp.dot(
                spread[...], token_rows(received_ref, rows), preferred_element_type=jnp.float32
            ).astype(out_ref.dtype)


def down_partial(received, rows, wide, total_rows, count, before):
    sources, _, features = received.shape
    total = sources * rows
    return pl.pallas_call(
        functools.partial(down_kernel, rows, wide, count),
        in_specs=[
            pl.BlockSpec(memory_space=pltpu.VMEM),
            *[pl.BlockSpec(memory_space=pl.ANY) for _ in before],
        ],
        out_shape=[jax.ShapeDtypeStruct((total_rows // count, features), jnp.bfloat16)] * count,
        scratch_shapes=[
            pltpu.VMEM((wide, total), jnp.float32),
            pltpu.VMEM((2, total), jnp.float32),
            pltpu.VMEM((BLOCK, total), jnp.bfloat16),
        ],
        compiler_params=params(),
        cost_estimate=cost(total_rows, total, features),
    )(received, *before)


def lane_numbers(received_ref, rows, wide):
    sources = received_ref.shape[0]
    low = low_half((sources * rows, wide))
    found = [
        columns_of(places_of(received_ref, source, rows), wide)
        for source in range(sources)
    ]
    odd = jnp.where(low, 0.0, 1.0)
    return low, *[jnp.concatenate([pair[k] for pair in found]) - odd for k in range(2)]


def join(piece_refs, full):
    start = 0
    for ref in piece_refs:
        full[start : start + ref.shape[0], :] = ref[...]
        start += ref.shape[0]


def project_kernel(received_ref, *refs):
    piece_refs, (out_ref, full) = refs[:-2], refs[-2:]
    pl.when(pl.program_id(0) == 0)(lambda: join(piece_refs, full))
    sources, rows, wide = out_ref.shape
    low, first, second = lane_numbers(received_ref, rows, wide)
    tokens = token_rows(received_ref, rows)
    sums = [jnp.zeros((sources * rows, wide), jnp.float32) for _ in range(2)]
    number = 0.0
    for start in range(0, full.shape[0], BLOCK):
        product = lax.dot_general(
            tokens,
            full[start : start + BLOCK, :],
            (((1,), (1,)), ((), ())),
            preferred_element_type=jnp.float32,
        )
        for at in range(0, BLOCK, wide):
            part = product[:, at : at + wide]
            sums[0] = jnp.where(first == number, part, sums[0])
            sums[1] = jnp.where(second == number, part, sums[1])
            number += 2.0
    folded = [value + pltpu.roll(value, wide // 2, 1) for value in sums]
    value = jnp.where(low, folded[0], folded[1]).astype(out_ref.dtype)
    out_ref[...] = value.reshape(out_ref.shape)


def project(received, pieces, rows, wide):
    sources, height, features = received.shape
    joined = sum(piece.shape[0] for piece in pieces)
    return pl.pallas_call(
        project_kernel,
        grid=(sources // 2,),
        in_specs=[
            pl.BlockSpec((2, height, features), lambda i: (i, 0, 0)),
            *[pl.BlockSpec(piece.shape, lambda i: (0, 0)) for piece in pieces],
        ],
        out_specs=pl.BlockSpec((2, rows, wide), lambda i: (i, 0, 0)),
        out_shape=jax.ShapeDtypeStruct((sources, rows, wide), jnp.bfloat16),
        scratch_shapes=[pltpu.VMEM((joined, features), jnp.bfloat16)],
        compiler_params=params(),
        cost_estimate=cost(sources * rows, features, joined),
    )(received, *pieces)


def hidden_kernel(parts_ref, activation_ref, scaled_ref, hidden_ref, gate_ref):
    projected = parts_ref[0].astype(jnp.float32)
    for source in range(1, parts_ref.shape[0]):
        projected = projected + parts_ref[source].astype(jnp.float32)
    wide = projected.shape[1]
    half = lax.broadcasted_iota(jnp.int32, (8, wide), 1) // (wide // 2)
    wanted = lax.broadcasted_iota(jnp.int32, (8, wide), 0)
    sums = lax.dot_general(
        jnp.where(wanted == half, 1.0, 0.0),
        activation_ref[...] * projected,
        (((1,), (1,)), ((), ())),
        precision=lax.Precision.HIGHEST,
        preferred_element_type=jnp.float32,
    )
    gate_ref[...] = sums[0:2, :].astype(gate_ref.dtype)
    hidden = (projected * scaled_ref[...]).astype(hidden_ref.dtype)
    for source in range(hidden_ref.shape[0]):
        hidden_ref[source] = hidden


def input_kernel(count, received_ref, hidden_ref, *refs):
    piece_refs, (out_ref, full, spread) = refs[:count], refs[-3:]
    pl.when(pl.program_id(0) == 0)(lambda: join(piece_refs, full))
    sources, rows, wide = hidden_ref.shape
    low, first, second = lane_numbers(received_ref, rows, wide)
    values = hidden_ref[...].reshape(sources * rows, wide).astype(jnp.float32)
    swapped = pltpu.roll(values, wide // 2, 1)
    one = jnp.where(low, values, swapped)
    two = jnp.where(low, swapped, values)
    for start in range(0, full.shape[0], wide):
        number = start // wide * 2.0
        spread[:, start : start + wide] = jnp.where(
            first == number, one, jnp.where(second == number, two, 0.0)
        ).astype(jnp.bfloat16)
    out_ref[...] = (
        jnp.dot(spread[...], full[...], preferred_element_type=jnp.float32)
        .astype(out_ref.dtype)
        .reshape(out_ref.shape)
    )


def input_rows(received, hidden_grad, pieces, before):
    sources, rows, wide = hidden_grad.shape
    joined, features = sum(piece.shape[0] for piece in pieces), pieces[0].shape[1]
    return pl.pallas_call(
        functools.partial(input_kernel, len(pieces)),
        grid=(sources // 2,),
        in_specs=[
            pl.BlockSpec((2, received.shape[1], features), lambda i: (i, 0, 0)),
            pl.BlockSpec((2, rows, wide), lambda i: (i, 0, 0)),
            *[pl.BlockSpec(piece.shape, lambda i: (0, 0)) for piece in pieces],
            *[pl.BlockSpec(memory_space=pl.ANY) for _ in before],
        ],
        out_specs=pl.BlockSpec((2, rows, features), lambda i: (i, 0, 0)),
        out_shape=jax.ShapeDtypeStruct((sources, rows, features), jnp.bfloat16),
        scratch_shapes=[
            pltpu.VMEM((joined, features), jnp.bfloat16),
            pltpu.VMEM((2 * rows, joined), jnp.bfloat16),
        ],
        compiler_params=params(),
        cost_estimate=cost(sources * rows, joined, features),
    )(received, hidden_grad, *pieces, *before)


def exchange(value, axes):
    return lax.all_to_all(value, axes, split_axis=0, concat_axis=0, tiled=True)


def swap(value, axis):
    return lax.ppermute(value, axis, SWAP)


def add(*terms):
    return sum(term.astype(jnp.float32) for term in terms).astype(jnp.bfloat16)


def body(token_grads, router_gates, expert_ids, saved_hidden, up_weight, down_weight):
    tok_count = token_grads.shape[0]
    local_experts, hidden, width = up_weight.shape
    members, far_count = lax.axis_size(GROUP), lax.axis_size(FAR)
    wide, features = 2 * hidden, width // PAIR
    own_rows = local_experts * hidden
    near = lax.axis_index("near")
    paired = lax.axis_size("high") == PAIR

    def halves(weight):
        flat = weight.reshape(own_rows, width)
        own = lax.dynamic_slice_in_dim(flat, near * features, features, axis=1)
        other = lax.dynamic_slice_in_dim(flat, (1 - near) * features, features, axis=1)
        return own, swap(other, "near")

    down_halves, up_halves = halves(down_weight), halves(up_weight)
    first = [down_halves[1], up_halves[1]]
    far_places = jnp.arange(far_count, dtype=jnp.int32)
    if paired:
        high_place = far_places // PAIR ^ lax.axis_index("high")
        far_places = (far_places % PAIR ^ lax.axis_index("low")) * PAIR + high_place
        beside = [swap(half, "high") for half in down_halves]
        low = [swap(half, "low") for half in down_halves]
        low_beside = [swap(half, "low") for half in beside]
        down_pieces = [*down_halves, *beside, *low, *low_beside]
        first += beside[:1]
        up_own = stack(*up_halves, beside[1:])
        up_beside = swap(up_own, "high")
        up_low = swap(stack(*up_halves, low_beside), "low")
        up_pieces = [up_own, up_beside, up_low, swap(up_beside, "low")]
    else:
        down_pieces = [lax.all_gather(stack(*down_halves, ()), FAR, tiled=True)]
        up_pieces = [lax.all_gather(stack(*up_halves, ()), FAR, tiled=True)]
    packed, activation, scaled = pack_tokens(
        far_places, expert_ids.T, router_gates.T, saved_hidden, token_grads, members,
        local_experts, first,
    )
    received = exchange(packed, GROUP)

    projected = project(received, down_pieces, tok_count, wide)
    partial_value = down_partial(
        received, tok_count, wide, own_rows * PAIR * far_count, far_count if paired else 1,
        (projected,),
    )
    parts = exchange(projected, GROUP)
    hidden_grad, gate_grads = pl.pallas_call(
        hidden_kernel,
        out_shape=(
            jax.ShapeDtypeStruct((members, tok_count, wide), jnp.bfloat16),
            jax.ShapeDtypeStruct((2, tok_count), jnp.bfloat16),
        ),
        compiler_params=params(),
    )(parts, activation, scaled)
    if paired:
        own, beside, low, low_beside = partial_value
        before = add_pairs([(beside, swap(low_beside, "low"))], ())
        sums = add(own, swap(low, "low"), swap(before[0], "high"))
    else:
        before = ()
        sums = lax.psum_scatter(partial_value[0], FAR, scatter_dimension=0, tiled=True)
    rows_back = input_rows(received, exchange(hidden_grad, GROUP), up_pieces, before)
    input_grads = unpack_tokens(exchange(rows_back, GROUP))

    kept, passed = sums[:own_rows], swap(sums[own_rows:], "near")
    down_grads = jnp.concatenate(
        [jnp.where(near == 0, kept, passed), jnp.where(near == 0, passed, kept)], axis=1
    ).reshape(down_weight.shape)
    return (input_grads, gate_grads.T, down_grads)


def solution(mesh):
    sizes = [mesh.shape[name] for name in ("expert", "inner", "outer")]
    expert = ("high", "low", "near")
    split = Mesh(
        mesh.devices.reshape(sizes[0] // PAIR**2, PAIR, PAIR, *sizes[1:]),
        (*expert, "inner", "outer"),
    )
    rows = P((*expert, "inner", "outer"), None)
    weights = P(expert, None, ("inner", "outer"))
    return jax.shard_map(
        body,
        mesh=split,
        in_specs=(rows, rows, rows, rows, weights, weights),
        out_specs=(rows, rows, weights),
        check_vma=False,
    )
```

```python
import functools
import jax
import jax.numpy as jnp
from jax import lax
from jax.experimental import pallas as pl
from jax.experimental.pallas import tpu as pltpu
from jax.sharding import Mesh, PartitionSpec as P

root_half = 0.7071067811865476
inv_root_tau = 0.3989422804014327
GROUP = ("inner", "outer", "near")
FAR = ("high", "low")
PAIR = 2
BLOCK = 256
TILE = 16
MIB = 1 << 20
SWAP = ((0, 1), (1, 0))


def gelu_parts(preact):
    cumulative = 0.5 * (1.0 + lax.erf(preact * root_half))
    density = inv_root_tau * jnp.exp(-0.5 * preact * preact)
    return (preact * cumulative, cumulative + preact * density)


def params(grant=20):
    return pltpu.CompilerParams(vmem_limit_bytes=grant * MIB)


def cost(rows, inner, columns):
    return pl.CostEstimate(
        flops=2 * rows * inner * columns,
        bytes_accessed=2 * (rows * inner + inner * columns + rows * columns),
        transcendentals=0,
    )


def low_half(shape):
    return lax.broadcasted_iota(jnp.int32, shape, len(shape) - 1) < shape[-1] // 2


def columns_of(pair, wide):
    wanted = lax.broadcasted_iota(jnp.int32, (2, wide), 0)
    return [
        lax.dot_general(
            pair.astype(jnp.bfloat16),
            jnp.where(wanted == k, 1.0, 0.0).astype(jnp.bfloat16),
            (((0,), (0,)), ((), ())),
            preferred_element_type=jnp.float32,
        )
        for k in range(2)
    ]


def in_hbm(*arrays):
    return [pltpu.with_memory_space_constraint(array, pltpu.HBM) for array in arrays]


def stack_kernel(own_ref, other_ref, *refs):
    rows = own_ref.shape[0]
    refs[-1][0:rows, :] = own_ref[...]
    refs[-1][rows:, :] = other_ref[...]


def stack(own, other, before):
    return pl.pallas_call(
        stack_kernel,
        in_specs=[
            *[pl.BlockSpec(memory_space=pltpu.VMEM)] * 2,
            *[pl.BlockSpec(memory_space=pl.ANY) for _ in before],
        ],
        out_shape=jax.ShapeDtypeStruct((2 * own.shape[0], own.shape[1]), own.dtype),
        compiler_params=params(),
    )(own, other, *in_hbm(*before))


def add_kernel(count, *refs):
    terms, out_refs = refs[: 2 * count], refs[-count:]
    for at in range(count):
        left, right = terms[2 * at][...], terms[2 * at + 1][...]
        total = left.astype(jnp.float32) + right.astype(jnp.float32)
        out_refs[at][...] = total.astype(out_refs[at].dtype)


def add_pairs(pairs, before):
    flat = [term for pair in pairs for term in pair]
    return pl.pallas_call(
        functools.partial(add_kernel, len(pairs)),
        in_specs=[
            *[pl.BlockSpec(memory_space=pltpu.VMEM) for _ in flat],
            *[pl.BlockSpec(memory_space=pl.ANY) for _ in before],
        ],
        out_shape=[jax.ShapeDtypeStruct(pair[0].shape, pair[0].dtype) for pair in pairs],
        compiler_params=params(),
    )(*flat, *in_hbm(*before))


def pack_kernel(
    local_experts, far_ref, ids_ref, gates_ref, preact_ref, tokens_ref, *refs
):
    out_ref, activation_ref, scaled_ref, weighted = refs[-4:]
    blocks, height, features = out_ref.shape
    rows, wide = preact_ref.shape
    far_count = far_ref.shape[0]
    taken = rows * wide // features

    @pl.when(pl.program_id(0) == 0)
    def _():
        activation, slope = gelu_parts(preact_ref[...].astype(jnp.float32))
        gates = jnp.where(low_half((rows, wide)), *columns_of(gates_ref[...], wide))
        activation_ref[...] = activation
        scaled_ref[...] = gates * slope
        weighted[...] = (gates * activation).astype(jnp.bfloat16)

    ids = ids_ref[...]
    local = lax.rem(ids, local_experts)
    line = lax.div(ids, local_experts)
    far, near = lax.div(line, PAIR), lax.rem(line, PAIR)
    far_place = jnp.zeros_like(far)
    for at in range(far_count):
        far_place = jnp.where(far == at, far_ref[at], far_place)
    for block in range(blocks):
        side = lax.rem(near + block, PAIR)
        place = (far_place * PAIR + side) * local_experts + local
        out_ref[block, 0:rows, :] = tokens_ref[:, block * features : (block + 1) * features]
        for at in range(0, features, wide):
            start = at // wide * taken
            out_ref[block, rows : rows + taken, at : at + wide] = weighted[start : start + taken, :]
        last = height - TILE
        out_ref[block, last:, :] = jnp.zeros((TILE, features), jnp.bfloat16)
        out_ref[block, last : last + 2, 0:rows] = place.astype(jnp.bfloat16)


def pack_tokens(far_places, ids, gates, preact, tokens, members, local_experts, before):
    rows, width = tokens.shape
    features = width // members
    each = members // 4
    height = rows + preact.size // features + TILE
    small = jax.ShapeDtypeStruct(preact.shape, jnp.float32)
    whole = [pl.BlockSpec(array.shape, lambda i: (0, 0)) for array in (ids, gates, preact)]
    return pl.pallas_call(
        functools.partial(pack_kernel, local_experts),
        grid=(4,),
        in_specs=[
            pl.BlockSpec(memory_space=pltpu.SMEM),
            *whole,
            pl.BlockSpec((rows, each * features), lambda i: (0, i)),
            *[pl.BlockSpec(memory_space=pl.ANY) for _ in before],
        ],
        out_specs=(pl.BlockSpec((each, height, features), lambda i: (i, 0, 0)), whole[2], whole[2]),
        out_shape=(
            pltpu.HBM((members, height, features), jnp.bfloat16), small, small,
        ),
        scratch_shapes=[pltpu.VMEM(preact.shape, jnp.bfloat16)],
        compiler_params=params(),
    )(far_places, ids, gates, preact, tokens, *in_hbm(*before))


def unpack_kernel(parts_ref, out_ref):
    blocks, _, features = parts_ref.shape
    for block in range(blocks):
        out_ref[:, block * features : (block + 1) * features] = parts_ref[block]


def unpack_tokens(parts):
    members, rows, features = parts.shape
    each = members // 4
    return pl.pallas_call(
        unpack_kernel,
        grid=(4,),
        in_specs=[pl.BlockSpec((each, rows, features), lambda i: (i, 0, 0))],
        out_specs=pl.BlockSpec((rows, each * features), lambda i: (0, i)),
        out_shape=jax.ShapeDtypeStruct((rows, members * features), jnp.bfloat16),
        compiler_params=params(),
    )(parts)


def places_of(received_ref, source, rows):
    at = received_ref.shape[1] - TILE
    return received_ref[source, at : at + 2, 0:rows]


def token_rows(received_ref, rows):
    sources, _, features = received_ref.shape
    return received_ref[:, 0:rows, :].reshape(sources * rows, features)


def down_kernel(rows, wide, count, received_ref, *refs):
    out_refs, (turned, numbers, spread) = refs[-3 - count : -3], refs[-3:]
    sources, _, features = received_ref.shape
    hidden, each = wide // 2, BLOCK // (wide // 2)
    taken = rows * wide // features
    for source in range(sources):
        weighted = jnp.concatenate(
            [
                received_ref[source, rows : rows + taken, at : at + wide].astype(jnp.float32)
                for at in range(0, features, wide)
            ]
        )
        lanes = slice(source * rows, (source + 1) * rows)
        turned[:, lanes] = weighted.T
        numbers[:, lanes] = places_of(received_ref, source, rows).astype(jnp.float32)
    number = 0
    for out_ref in out_refs:
        for start in range(0, out_ref.shape[0], BLOCK):
            for expert in range(each):
                spread[expert * hidden : (expert + 1) * hidden, :] = jnp.where(
                    numbers[0:1, :] == number + expert,
                    turned[0:hidden, :],
                    jnp.where(numbers[1:2, :] == number + expert, turned[hidden:, :], 0.0),
                ).astype(jnp.bfloat16)
            number += each
            out_ref[start : start + BLOCK, :] = jnp.dot(
                spread[...], token_rows(received_ref, rows), preferred_element_type=jnp.float32
            ).astype(out_ref.dtype)


def down_partial(received, rows, wide, total_rows, count, before):
    sources, _, features = received.shape
    total = sources * rows
    return pl.pallas_call(
        functools.partial(down_kernel, rows, wide, count),
        in_specs=[
            pl.BlockSpec(memory_space=pltpu.VMEM),
            *[pl.BlockSpec(memory_space=pl.ANY) for _ in before],
        ],
        out_shape=[jax.ShapeDtypeStruct((total_rows // count, features), jnp.bfloat16)] * count,
        scratch_shapes=[
            pltpu.VMEM((wide, total), jnp.float32),
            pltpu.VMEM((2, total), jnp.float32),
            pltpu.VMEM((BLOCK, total), jnp.bfloat16),
        ],
        compiler_params=params(),
        cost_estimate=cost(total_rows, total, features),
    )(received, *in_hbm(*before))


def lane_numbers(received_ref, rows, wide):
    sources = received_ref.shape[0]
    low = low_half((sources * rows, wide))
    found = [
        columns_of(places_of(received_ref, source, rows), wide)
        for source in range(sources)
    ]
    odd = jnp.where(low, 0.0, 1.0)
    return low, *[jnp.concatenate([pair[k] for pair in found]) - odd for k in range(2)]


def join(piece_refs, full):
    start = 0
    for ref in piece_refs:
        full[start : start + ref.shape[0], :] = ref[...]
        start += ref.shape[0]


def project_kernel(count, received_ref, *refs):
    piece_refs, (out_ref, full) = refs[:count], refs[-2:]
    pl.when(pl.program_id(0) == 0)(lambda: join(piece_refs, full))
    sources, rows, wide = out_ref.shape
    low, first, second = lane_numbers(received_ref, rows, wide)
    tokens = token_rows(received_ref, rows)
    sums = [jnp.zeros((sources * rows, wide), jnp.float32) for _ in range(2)]
    number = 0.0
    for start in range(0, full.shape[0], BLOCK):
        product = lax.dot_general(
            tokens,
            full[start : start + BLOCK, :],
            (((1,), (1,)), ((), ())),
            preferred_element_type=jnp.float32,
        )
        for at in range(0, BLOCK, wide):
            part = product[:, at : at + wide]
            sums[0] = jnp.where(first == number, part, sums[0])
            sums[1] = jnp.where(second == number, part, sums[1])
            number += 2.0
    folded = [value + pltpu.roll(value, wide // 2, 1) for value in sums]
    value = jnp.where(low, folded[0], folded[1]).astype(out_ref.dtype)
    out_ref[...] = value.reshape(out_ref.shape)


def project(received, pieces, rows, wide, before):
    sources, height, features = received.shape
    joined = sum(piece.shape[0] for piece in pieces)
    return pl.pallas_call(
        functools.partial(project_kernel, len(pieces)),
        grid=(sources // 2,),
        in_specs=[
            pl.BlockSpec((2, height, features), lambda i: (i, 0, 0)),
            *[pl.BlockSpec(piece.shape, lambda i: (0, 0)) for piece in pieces],
            *[pl.BlockSpec(memory_space=pl.ANY) for _ in before],
        ],
        out_specs=pl.BlockSpec((2, rows, wide), lambda i: (i, 0, 0)),
        out_shape=jax.ShapeDtypeStruct((sources, rows, wide), jnp.bfloat16),
        scratch_shapes=[pltpu.VMEM((joined, features), jnp.bfloat16)],
        compiler_params=params(),
        cost_estimate=cost(sources * rows, features, joined),
    )(received, *in_hbm(*pieces, *before))


def hidden_kernel(parts_ref, activation_ref, scaled_ref, hidden_ref, gate_ref):
    projected = parts_ref[0].astype(jnp.float32)
    for source in range(1, parts_ref.shape[0]):
        projected = projected + parts_ref[source].astype(jnp.float32)
    wide = projected.shape[1]
    half = lax.broadcasted_iota(jnp.int32, (8, wide), 1) // (wide // 2)
    wanted = lax.broadcasted_iota(jnp.int32, (8, wide), 0)
    sums = lax.dot_general(
        jnp.where(wanted == half, 1.0, 0.0),
        activation_ref[...] * projected,
        (((1,), (1,)), ((), ())),
        precision=lax.Precision.HIGHEST,
        preferred_element_type=jnp.float32,
    )
    gate_ref[...] = sums[0:2, :].astype(gate_ref.dtype)
    hidden = (projected * scaled_ref[...]).astype(hidden_ref.dtype)
    for source in range(hidden_ref.shape[0]):
        hidden_ref[source] = hidden


def input_kernel(count, received_ref, hidden_ref, *refs):
    piece_refs, (out_ref, full, spread) = refs[:count], refs[-3:]
    pl.when(pl.program_id(0) == 0)(lambda: join(piece_refs, full))
    sources, rows, wide = hidden_ref.shape
    low, first, second = lane_numbers(received_ref, rows, wide)
    values = hidden_ref[...].reshape(sources * rows, wide).astype(jnp.float32)
    swapped = pltpu.roll(values, wide // 2, 1)
    one = jnp.where(low, values, swapped)
    two = jnp.where(low, swapped, values)
    for start in range(0, full.shape[0], wide):
        number = start // wide * 2.0
        spread[:, start : start + wide] = jnp.where(
            first == number, one, jnp.where(second == number, two, 0.0)
        ).astype(jnp.bfloat16)
    out_ref[...] = (
        jnp.dot(spread[...], full[...], preferred_element_type=jnp.float32)
        .astype(out_ref.dtype)
        .reshape(out_ref.shape)
    )


def input_rows(received, hidden_grad, pieces, before):
    sources, rows, wide = hidden_grad.shape
    joined, features = sum(piece.shape[0] for piece in pieces), pieces[0].shape[1]
    return pl.pallas_call(
        functools.partial(input_kernel, len(pieces)),
        grid=(sources // 2,),
        in_specs=[
            pl.BlockSpec((2, received.shape[1], features), lambda i: (i, 0, 0)),
            pl.BlockSpec((2, rows, wide), lambda i: (i, 0, 0)),
            *[pl.BlockSpec(piece.shape, lambda i: (0, 0)) for piece in pieces],
            *[pl.BlockSpec(memory_space=pl.ANY) for _ in before],
        ],
        out_specs=pl.BlockSpec((2, rows, features), lambda i: (i, 0, 0)),
        out_shape=jax.ShapeDtypeStruct((sources, rows, features), jnp.bfloat16),
        scratch_shapes=[
            pltpu.VMEM((joined, features), jnp.bfloat16),
            pltpu.VMEM((2 * rows, joined), jnp.bfloat16),
        ],
        compiler_params=params(),
        cost_estimate=cost(sources * rows, joined, features),
    )(received, hidden_grad, *in_hbm(*pieces, *before))


def exchange(value, axes):
    return lax.all_to_all(value, axes, split_axis=0, concat_axis=0, tiled=True)


def swap(value, axis):
    return lax.ppermute(value, axis, SWAP)


def add(*terms):
    return sum(term.astype(jnp.float32) for term in terms).astype(jnp.bfloat16)


def body(token_grads, router_gates, expert_ids, saved_hidden, up_weight, down_weight):
    tok_count = token_grads.shape[0]
    local_experts, hidden, width = up_weight.shape
    members, far_count = lax.axis_size(GROUP), lax.axis_size(FAR)
    wide, features = 2 * hidden, width // PAIR
    own_rows = local_experts * hidden
    near = lax.axis_index("near")
    paired = lax.axis_size("high") == PAIR

    def halves(weight):
        flat = weight.reshape(own_rows, width)
        own = lax.dynamic_slice_in_dim(flat, near * features, features, axis=1)
        other = lax.dynamic_slice_in_dim(flat, (1 - near) * features, features, axis=1)
        return own, swap(other, "near")

    down_halves, up_halves = halves(down_weight), halves(up_weight)
    first = [down_halves[1], up_halves[1]]
    far_places = jnp.arange(far_count, dtype=jnp.int32)
    if paired:
        high_place = far_places // PAIR ^ lax.axis_index("high")
        far_places = (far_places % PAIR ^ lax.axis_index("low")) * PAIR + high_place
        beside = [swap(half, "high") for half in down_halves]
        low = [swap(half, "low") for half in down_halves]
        low_beside = [swap(half, "low") for half in beside]
        down_pieces = [*down_halves, *beside, *low, *low_beside]
        first += [beside[0], *low]
        up_own = stack(*up_halves, beside[1:])
        up_beside = swap(up_own, "high")
        up_low = swap(up_own, "low")
        up_pieces = [up_own, up_beside, up_low, swap(up_beside, "low")]
    else:
        down_pieces = [lax.all_gather(stack(*down_halves, ()), FAR, tiled=True)]
        up_pieces = [lax.all_gather(stack(*up_halves, ()), FAR, tiled=True)]
    packed, activation, scaled = pack_tokens(
        far_places, expert_ids.T, router_gates.T, saved_hidden, token_grads, members,
        local_experts, first,
    )
    received = exchange(packed, GROUP)

    partial_value = down_partial(
        received, tok_count, wide, own_rows * PAIR * far_count, far_count if paired else 1, ()
    )
    projected = project(received, down_pieces, tok_count, wide, partial_value[:1])
    parts = exchange(projected, GROUP)
    hidden_grad, gate_grads = pl.pallas_call(
        hidden_kernel,
        out_shape=(
            jax.ShapeDtypeStruct((members, tok_count, wide), jnp.bfloat16),
            jax.ShapeDtypeStruct((2, tok_count), jnp.bfloat16),
        ),
        compiler_params=params(),
    )(parts, activation, scaled)
    if paired:
        own, beside, low, low_beside = partial_value
        before = add_pairs([(beside, swap(low_beside, "low"))], ())
        sums = add(own, swap(low, "low"), swap(before[0], "high"))
    else:
        before = ()
        sums = lax.psum_scatter(partial_value[0], FAR, scatter_dimension=0, tiled=True)
    rows_back = input_rows(received, exchange(hidden_grad, GROUP), up_pieces, before)
    input_grads = unpack_tokens(exchange(rows_back, GROUP))

    kept, passed = sums[:own_rows], swap(sums[own_rows:], "near")
    down_grads = jnp.concatenate(
        [jnp.where(near == 0, kept, passed), jnp.where(near == 0, passed, kept)], axis=1
    ).reshape(down_weight.shape)
    return (input_grads, gate_grads.T, down_grads)


def solution(mesh):
    sizes = [mesh.shape[name] for name in ("expert", "inner", "outer")]
    expert = ("high", "low", "near")
    split = Mesh(
        mesh.devices.reshape(sizes[0] // PAIR**2, PAIR, PAIR, *sizes[1:]),
        (*expert, "inner", "outer"),
    )
    rows = P((*expert, "inner", "outer"), None)
    weights = P(expert, None, ("inner", "outer"))
    return jax.shard_map(
        body,
        mesh=split,
        in_specs=(rows, rows, rows, rows, weights, weights),
        out_specs=(rows, rows, weights),
        check_vma=False,
    )
```

```python
import functools
import jax
import jax.numpy as jnp
from jax import lax
from jax.experimental import pallas as pl
from jax.experimental.pallas import tpu as pltpu
from jax.sharding import Mesh, PartitionSpec as P

root_half = 0.7071067811865476
inv_root_tau = 0.3989422804014327
GROUP = ("inner", "outer", "near")
FAR = ("high", "low")
PAIR = 2
BLOCK = 256
TILE = 16
MIB = 1 << 20
SWAP = ((0, 1), (1, 0))


def gelu_parts(preact):
    cumulative = 0.5 * (1.0 + lax.erf(preact * root_half))
    density = inv_root_tau * jnp.exp(-0.5 * preact * preact)
    return (preact * cumulative, cumulative + preact * density)


def params(grant=20):
    return pltpu.CompilerParams(vmem_limit_bytes=grant * MIB)


def cost(rows, inner, columns):
    return pl.CostEstimate(
        flops=2 * rows * inner * columns,
        bytes_accessed=2 * (rows * inner + inner * columns + rows * columns),
        transcendentals=0,
    )


def low_half(shape):
    return lax.broadcasted_iota(jnp.int32, shape, len(shape) - 1) < shape[-1] // 2


def columns_of(pair, wide):
    wanted = lax.broadcasted_iota(jnp.int32, (2, wide), 0)
    return [
        lax.dot_general(
            pair.astype(jnp.bfloat16),
            jnp.where(wanted == k, 1.0, 0.0).astype(jnp.bfloat16),
            (((0,), (0,)), ((), ())),
            preferred_element_type=jnp.float32,
        )
        for k in range(2)
    ]


def in_hbm(*arrays):
    return [pltpu.with_memory_space_constraint(array, pltpu.HBM) for array in arrays]


def stack_kernel(own_ref, other_ref, *refs):
    rows = own_ref.shape[0]
    refs[-1][0:rows, :] = own_ref[...]
    refs[-1][rows:, :] = other_ref[...]


def stack(own, other, before):
    return pl.pallas_call(
        stack_kernel,
        in_specs=[
            *[pl.BlockSpec(memory_space=pltpu.VMEM)] * 2,
            *[pl.BlockSpec(memory_space=pl.ANY) for _ in before],
        ],
        out_shape=jax.ShapeDtypeStruct((2 * own.shape[0], own.shape[1]), own.dtype),
        compiler_params=params(),
    )(own, other, *in_hbm(*before))


def pass_on(value, before):
    anywhere = pl.BlockSpec(memory_space=pl.ANY)
    return pl.pallas_call(
        lambda *refs: None,
        in_specs=[anywhere] * (1 + len(before)),
        out_specs=anywhere,
        out_shape=jax.ShapeDtypeStruct(value.shape, value.dtype),
        input_output_aliases={0: 0},
        compiler_params=params(),
    )(value, *before)


def place_kernel(near_ref, kept_ref, passed_ref, before_ref, out_ref):
    features = kept_ref.shape[1]
    first = near_ref[0] == 0
    kept, passed = kept_ref[...], passed_ref[...]
    out_ref[:, 0:features] = jnp.where(first, kept, passed)
    out_ref[:, features:] = jnp.where(first, passed, kept)


def place_halves(near, kept, passed, before):
    rows, features = kept.shape
    return pl.pallas_call(
        place_kernel,
        in_specs=[
            pl.BlockSpec(memory_space=pltpu.SMEM),
            *[pl.BlockSpec(memory_space=pltpu.VMEM)] * 2,
            pl.BlockSpec(memory_space=pl.ANY),
        ],
        out_shape=jax.ShapeDtypeStruct((rows, PAIR * features), kept.dtype),
        compiler_params=params(),
    )(near[None], kept, passed, *in_hbm(before))


def add_kernel(count, *refs):
    terms, out_refs = refs[: 2 * count], refs[-count:]
    for at in range(count):
        left, right = terms[2 * at][...], terms[2 * at + 1][...]
        total = left.astype(jnp.float32) + right.astype(jnp.float32)
        out_refs[at][...] = total.astype(out_refs[at].dtype)


def add_pairs(pairs, before):
    flat = [term for pair in pairs for term in pair]
    return pl.pallas_call(
        functools.partial(add_kernel, len(pairs)),
        in_specs=[
            *[pl.BlockSpec(memory_space=pltpu.VMEM) for _ in flat],
            *[pl.BlockSpec(memory_space=pl.ANY) for _ in before],
        ],
        out_shape=[jax.ShapeDtypeStruct(pair[0].shape, pair[0].dtype) for pair in pairs],
        compiler_params=params(),
    )(*flat, *in_hbm(*before))


def pack_kernel(
    local_experts, far_ref, ids_ref, gates_ref, preact_ref, tokens_ref, *refs
):
    out_ref, activation_ref, scaled_ref, weighted = refs[-4:]
    blocks, height, features = out_ref.shape
    rows, wide = preact_ref.shape
    far_count = far_ref.shape[0]
    taken = rows * wide // features

    @pl.when(pl.program_id(0) == 0)
    def _():
        activation, slope = gelu_parts(preact_ref[...].astype(jnp.float32))
        gates = jnp.where(low_half((rows, wide)), *columns_of(gates_ref[...], wide))
        activation_ref[...] = activation
        scaled_ref[...] = gates * slope
        weighted[...] = (gates * activation).astype(jnp.bfloat16)

    ids = ids_ref[...]
    local = lax.rem(ids, local_experts)
    line = lax.div(ids, local_experts)
    far, near = lax.div(line, PAIR), lax.rem(line, PAIR)
    far_place = jnp.zeros_like(far)
    for at in range(far_count):
        far_place = jnp.where(far == at, far_ref[at], far_place)
    for block in range(blocks):
        side = lax.rem(near + block, PAIR)
        place = (far_place * PAIR + side) * local_experts + local
        out_ref[block, 0:rows, :] = tokens_ref[:, block * features : (block + 1) * features]
        for at in range(0, features, wide):
            start = at // wide * taken
            out_ref[block, rows : rows + taken, at : at + wide] = weighted[start : start + taken, :]
        last = height - TILE
        out_ref[block, last:, :] = jnp.zeros((TILE, features), jnp.bfloat16)
        out_ref[block, last : last + 2, 0:rows] = place.astype(jnp.bfloat16)


def pack_tokens(far_places, ids, gates, preact, tokens, members, local_experts, before):
    rows, width = tokens.shape
    features = width // members
    each = members // 4
    height = rows + preact.size // features + TILE
    small = jax.ShapeDtypeStruct(preact.shape, jnp.float32)
    whole = [pl.BlockSpec(array.shape, lambda i: (0, 0)) for array in (ids, gates, preact)]
    return pl.pallas_call(
        functools.partial(pack_kernel, local_experts),
        grid=(4,),
        in_specs=[
            pl.BlockSpec(memory_space=pltpu.SMEM),
            *whole,
            pl.BlockSpec((rows, each * features), lambda i: (0, i)),
            *[pl.BlockSpec(memory_space=pl.ANY) for _ in before],
        ],
        out_specs=(pl.BlockSpec((each, height, features), lambda i: (i, 0, 0)), whole[2], whole[2]),
        out_shape=(
            pltpu.HBM((members, height, features), jnp.bfloat16), small, small,
        ),
        scratch_shapes=[pltpu.VMEM(preact.shape, jnp.bfloat16)],
        compiler_params=params(),
    )(far_places, ids, gates, preact, tokens, *in_hbm(*before))


def unpack_kernel(parts_ref, out_ref):
    blocks, _, features = parts_ref.shape
    for block in range(blocks):
        out_ref[:, block * features : (block + 1) * features] = parts_ref[block]


def unpack_tokens(parts):
    members, rows, features = parts.shape
    each = members // 4
    return pl.pallas_call(
        unpack_kernel,
        grid=(4,),
        in_specs=[pl.BlockSpec((each, rows, features), lambda i: (i, 0, 0))],
        out_specs=pl.BlockSpec((rows, each * features), lambda i: (0, i)),
        out_shape=jax.ShapeDtypeStruct((rows, members * features), jnp.bfloat16),
        compiler_params=params(),
    )(parts)


def places_of(received_ref, source, rows):
    at = received_ref.shape[1] - TILE
    return received_ref[source, at : at + 2, 0:rows]


def token_rows(received_ref, rows):
    sources, _, features = received_ref.shape
    return received_ref[:, 0:rows, :].reshape(sources * rows, features)


def down_kernel(rows, wide, count, received_ref, *refs):
    out_refs, (turned, numbers, spread) = refs[-3 - count : -3], refs[-3:]
    sources, _, features = received_ref.shape
    hidden, each = wide // 2, BLOCK // (wide // 2)
    taken = rows * wide // features
    for source in range(sources):
        weighted = jnp.concatenate(
            [
                received_ref[source, rows : rows + taken, at : at + wide].astype(jnp.float32)
                for at in range(0, features, wide)
            ]
        )
        lanes = slice(source * rows, (source + 1) * rows)
        turned[:, lanes] = weighted.T
        numbers[:, lanes] = places_of(received_ref, source, rows).astype(jnp.float32)
    number = 0
    for out_ref in out_refs:
        for start in range(0, out_ref.shape[0], BLOCK):
            for expert in range(each):
                spread[expert * hidden : (expert + 1) * hidden, :] = jnp.where(
                    numbers[0:1, :] == number + expert,
                    turned[0:hidden, :],
                    jnp.where(numbers[1:2, :] == number + expert, turned[hidden:, :], 0.0),
                ).astype(jnp.bfloat16)
            number += each
            out_ref[start : start + BLOCK, :] = jnp.dot(
                spread[...], token_rows(received_ref, rows), preferred_element_type=jnp.float32
            ).astype(out_ref.dtype)


def down_partial(received, rows, wide, total_rows, count, before):
    sources, _, features = received.shape
    total = sources * rows
    return pl.pallas_call(
        functools.partial(down_kernel, rows, wide, count),
        in_specs=[
            pl.BlockSpec(memory_space=pltpu.VMEM),
            *[pl.BlockSpec(memory_space=pl.ANY) for _ in before],
        ],
        out_shape=[jax.ShapeDtypeStruct((total_rows // count, features), jnp.bfloat16)] * count,
        scratch_shapes=[
            pltpu.VMEM((wide, total), jnp.float32),
            pltpu.VMEM((2, total), jnp.float32),
            pltpu.VMEM((BLOCK, total), jnp.bfloat16),
        ],
        compiler_params=params(),
        cost_estimate=cost(total_rows, total, features),
    )(received, *in_hbm(*before))


def lane_numbers(received_ref, rows, wide):
    sources = received_ref.shape[0]
    low = low_half((sources * rows, wide))
    found = [
        columns_of(places_of(received_ref, source, rows), wide)
        for source in range(sources)
    ]
    odd = jnp.where(low, 0.0, 1.0)
    return low, *[jnp.concatenate([pair[k] for pair in found]) - odd for k in range(2)]


def join(piece_refs, full):
    start = 0
    for ref in piece_refs:
        full[start : start + ref.shape[0], :] = ref[...]
        start += ref.shape[0]


def project_kernel(count, received_ref, *refs):
    piece_refs, (out_ref, full) = refs[:count], refs[-2:]
    pl.when(pl.program_id(0) == 0)(lambda: join(piece_refs, full))
    sources, rows, wide = out_ref.shape
    low, first, second = lane_numbers(received_ref, rows, wide)
    tokens = token_rows(received_ref, rows)
    sums = [jnp.zeros((sources * rows, wide), jnp.float32) for _ in range(2)]
    number = 0.0
    for start in range(0, full.shape[0], BLOCK):
        product = lax.dot_general(
            tokens,
            full[start : start + BLOCK, :],
            (((1,), (1,)), ((), ())),
            preferred_element_type=jnp.float32,
        )
        for at in range(0, BLOCK, wide):
            part = product[:, at : at + wide]
            sums[0] = jnp.where(first == number, part, sums[0])
            sums[1] = jnp.where(second == number, part, sums[1])
            number += 2.0
    folded = [value + pltpu.roll(value, wide // 2, 1) for value in sums]
    value = jnp.where(low, folded[0], folded[1]).astype(out_ref.dtype)
    out_ref[...] = value.reshape(out_ref.shape)


def project(received, pieces, rows, wide, before):
    sources, height, features = received.shape
    joined = sum(piece.shape[0] for piece in pieces)
    return pl.pallas_call(
        functools.partial(project_kernel, len(pieces)),
        grid=(sources // 2,),
        in_specs=[
            pl.BlockSpec((2, height, features), lambda i: (i, 0, 0)),
            *[pl.BlockSpec(piece.shape, lambda i: (0, 0)) for piece in pieces],
            *[pl.BlockSpec(memory_space=pl.ANY) for _ in before],
        ],
        out_specs=pl.BlockSpec((2, rows, wide), lambda i: (i, 0, 0)),
        out_shape=pltpu.HBM((sources, rows, wide), jnp.bfloat16),
        scratch_shapes=[pltpu.VMEM((joined, features), jnp.bfloat16)],
        compiler_params=params(),
        cost_estimate=cost(sources * rows, features, joined),
    )(received, *in_hbm(*pieces), *before)


def hidden_kernel(parts_ref, activation_ref, scaled_ref, hidden_ref, gate_ref):
    projected = parts_ref[0].astype(jnp.float32)
    for source in range(1, parts_ref.shape[0]):
        projected = projected + parts_ref[source].astype(jnp.float32)
    wide = projected.shape[1]
    half = lax.broadcasted_iota(jnp.int32, (8, wide), 1) // (wide // 2)
    wanted = lax.broadcasted_iota(jnp.int32, (8, wide), 0)
    sums = lax.dot_general(
        jnp.where(wanted == half, 1.0, 0.0),
        activation_ref[...] * projected,
        (((1,), (1,)), ((), ())),
        precision=lax.Precision.HIGHEST,
        preferred_element_type=jnp.float32,
    )
    gate_ref[...] = sums[0:2, :].astype(gate_ref.dtype)
    hidden = (projected * scaled_ref[...]).astype(hidden_ref.dtype)
    for source in range(hidden_ref.shape[0]):
        hidden_ref[source] = hidden


def input_kernel(count, received_ref, hidden_ref, *refs):
    piece_refs, (out_ref, full, spread) = refs[:count], refs[-3:]
    pl.when(pl.program_id(0) == 0)(lambda: join(piece_refs, full))
    sources, rows, wide = hidden_ref.shape
    low, first, second = lane_numbers(received_ref, rows, wide)
    values = hidden_ref[...].reshape(sources * rows, wide).astype(jnp.float32)
    swapped = pltpu.roll(values, wide // 2, 1)
    one = jnp.where(low, values, swapped)
    two = jnp.where(low, swapped, values)
    for start in range(0, full.shape[0], wide):
        number = start // wide * 2.0
        spread[:, start : start + wide] = jnp.where(
            first == number, one, jnp.where(second == number, two, 0.0)
        ).astype(jnp.bfloat16)
    out_ref[...] = (
        jnp.dot(spread[...], full[...], preferred_element_type=jnp.float32)
        .astype(out_ref.dtype)
        .reshape(out_ref.shape)
    )


def input_rows(received, hidden_grad, pieces, before):
    sources, rows, wide = hidden_grad.shape
    joined, features = sum(piece.shape[0] for piece in pieces), pieces[0].shape[1]
    return pl.pallas_call(
        functools.partial(input_kernel, len(pieces)),
        grid=(sources // 2,),
        in_specs=[
            pl.BlockSpec((2, received.shape[1], features), lambda i: (i, 0, 0)),
            pl.BlockSpec((2, rows, wide), lambda i: (i, 0, 0)),
            *[pl.BlockSpec(piece.shape, lambda i: (0, 0)) for piece in pieces],
            *[pl.BlockSpec(memory_space=pl.ANY) for _ in before],
        ],
        out_specs=pl.BlockSpec((2, rows, features), lambda i: (i, 0, 0)),
        out_shape=pltpu.HBM((sources, rows, features), jnp.bfloat16),
        scratch_shapes=[
            pltpu.VMEM((joined, features), jnp.bfloat16),
            pltpu.VMEM((2 * rows, joined), jnp.bfloat16),
        ],
        compiler_params=params(),
        cost_estimate=cost(sources * rows, joined, features),
    )(received, hidden_grad, *in_hbm(*pieces, *before))


def exchange(value, axes):
    return lax.all_to_all(value, axes, split_axis=0, concat_axis=0, tiled=True)


def swap(value, axis):
    return lax.ppermute(value, axis, SWAP)


def add(*terms):
    return sum(term.astype(jnp.float32) for term in terms).astype(jnp.bfloat16)


def body(token_grads, router_gates, expert_ids, saved_hidden, up_weight, down_weight):
    tok_count = token_grads.shape[0]
    local_experts, hidden, width = up_weight.shape
    members, far_count = lax.axis_size(GROUP), lax.axis_size(FAR)
    wide, features = 2 * hidden, width // PAIR
    own_rows = local_experts * hidden
    near = lax.axis_index("near")
    paired = lax.axis_size("high") == PAIR

    def halves(weight):
        flat = weight.reshape(own_rows, width)
        own = lax.dynamic_slice_in_dim(flat, near * features, features, axis=1)
        other = lax.dynamic_slice_in_dim(flat, (1 - near) * features, features, axis=1)
        return own, swap(other, "near")

    down_halves, up_halves = halves(down_weight), halves(up_weight)
    first = [down_halves[1], up_halves[1]]
    far_places = jnp.arange(far_count, dtype=jnp.int32)
    if paired:
        high_place = far_places // PAIR ^ lax.axis_index("high")
        far_places = (far_places % PAIR ^ lax.axis_index("low")) * PAIR + high_place
        beside = [swap(half, "high") for half in down_halves]
        low = [swap(half, "low") for half in down_halves]
        low_beside = [swap(half, "low") for half in beside]
        down_pieces = [*down_halves, *beside, *low, *low_beside]
        first += [beside[0], *low]
        up_own = stack(*up_halves, beside[1:])
        up_beside = swap(up_own, "high")
        up_low = swap(up_own, "low")
    else:
        down_pieces = [lax.all_gather(stack(*down_halves, ()), FAR, tiled=True)]
        up_pieces = [lax.all_gather(stack(*up_halves, ()), FAR, tiled=True)]
    packed, activation, scaled = pack_tokens(
        far_places, expert_ids.T, router_gates.T, saved_hidden, token_grads, members,
        local_experts, first,
    )
    received = exchange(packed, GROUP)

    partial_value = down_partial(
        received, tok_count, wide, own_rows * PAIR * far_count, far_count if paired else 1, ()
    )
    projected = project(received, down_pieces, tok_count, wide, partial_value[:1])
    if paired:
        up_beside = pass_on(up_beside, (projected,))
        up_pieces = [up_own, up_beside, up_low, swap(up_beside, "low")]
    parts = exchange(projected, GROUP)
    hidden_grad, gate_grads = pl.pallas_call(
        hidden_kernel,
        out_shape=(
            jax.ShapeDtypeStruct((members, tok_count, wide), jnp.bfloat16),
            jax.ShapeDtypeStruct((2, tok_count), jnp.bfloat16),
        ),
        compiler_params=params(),
    )(parts, activation, scaled)
    if paired:
        own, beside, low, low_beside = partial_value
        before = add_pairs([(beside, swap(low_beside, "low"))], ())
        low = swap(low, "low")
        passed, kept = [
            add(own[at], low[at], swap(before[0][at], "high"))
            for at in (slice(own_rows, None), slice(0, own_rows))
        ]
    else:
        before = ()
        sums = lax.psum_scatter(partial_value[0], FAR, scatter_dimension=0, tiled=True)
        kept, passed = sums[:own_rows], sums[own_rows:]
    rows_back = input_rows(received, exchange(hidden_grad, GROUP), up_pieces, before)
    input_grads = unpack_tokens(exchange(rows_back, GROUP))

    down_grads = place_halves(near, kept, swap(passed, "near"), input_grads)
    down_grads = down_grads.reshape(down_weight.shape)
    return (input_grads, gate_grads.T, down_grads)


def solution(mesh):
    sizes = [mesh.shape[name] for name in ("expert", "inner", "outer")]
    expert = ("high", "low", "near")
    split = Mesh(
        mesh.devices.reshape(sizes[0] // PAIR**2, PAIR, PAIR, *sizes[1:]),
        (*expert, "inner", "outer"),
    )
    rows = P((*expert, "inner", "outer"), None)
    weights = P(expert, None, ("inner", "outer"))
    return jax.shard_map(
        body,
        mesh=split,
        in_specs=(rows, rows, rows, rows, weights, weights),
        out_specs=(rows, rows, weights),
        check_vma=False,
    )
```

```python
import functools
import jax
import jax.numpy as jnp
from jax import lax
from jax.experimental import pallas as pl
from jax.experimental.pallas import tpu as pltpu
from jax.sharding import Mesh, PartitionSpec as P

root_half = 0.7071067811865476
inv_root_tau = 0.3989422804014327
GROUP = ("inner", "outer", "near")
FAR = ("high", "low")
PAIR = 2
BLOCK = 256
TILE = 16
MIB = 1 << 20
SWAP = ((0, 1), (1, 0))


def gelu_parts(preact):
    cumulative = 0.5 * (1.0 + lax.erf(preact * root_half))
    density = inv_root_tau * jnp.exp(-0.5 * preact * preact)
    return (preact * cumulative, cumulative + preact * density)


def params(grant=20):
    return pltpu.CompilerParams(vmem_limit_bytes=grant * MIB)


def cost(rows, inner, columns):
    return pl.CostEstimate(
        flops=2 * rows * inner * columns,
        bytes_accessed=2 * (rows * inner + inner * columns + rows * columns),
        transcendentals=0,
    )


def low_half(shape):
    return lax.broadcasted_iota(jnp.int32, shape, len(shape) - 1) < shape[-1] // 2


def columns_of(pair, wide):
    wanted = lax.broadcasted_iota(jnp.int32, (2, wide), 0)
    return [
        lax.dot_general(
            pair.astype(jnp.bfloat16),
            jnp.where(wanted == k, 1.0, 0.0).astype(jnp.bfloat16),
            (((0,), (0,)), ((), ())),
            preferred_element_type=jnp.float32,
        )
        for k in range(2)
    ]


def in_hbm(*arrays):
    return [pltpu.with_memory_space_constraint(array, pltpu.HBM) for array in arrays]


def stack_kernel(own_ref, other_ref, *refs):
    rows = own_ref.shape[0]
    refs[-1][0:rows, :] = own_ref[...]
    refs[-1][rows:, :] = other_ref[...]


def stack(own, other, before):
    return pl.pallas_call(
        stack_kernel,
        in_specs=[
            *[pl.BlockSpec(memory_space=pltpu.VMEM)] * 2,
            *[pl.BlockSpec(memory_space=pl.ANY) for _ in before],
        ],
        out_shape=jax.ShapeDtypeStruct((2 * own.shape[0], own.shape[1]), own.dtype),
        compiler_params=params(),
    )(own, other, *in_hbm(*before))


def pass_on(value, before):
    anywhere = pl.BlockSpec(memory_space=pl.ANY)
    return pl.pallas_call(
        lambda *refs: None,
        in_specs=[anywhere] * (1 + len(before)),
        out_specs=anywhere,
        out_shape=pltpu.HBM(value.shape, value.dtype),
        input_output_aliases={0: 0},
        compiler_params=params(),
    )(*in_hbm(value), *before)


def place_kernel(near_ref, kept_ref, passed_ref, before_ref, out_ref):
    features = kept_ref.shape[1]
    first = near_ref[0] == 0
    kept, passed = kept_ref[...], passed_ref[...]
    out_ref[:, 0:features] = jnp.where(first, kept, passed)
    out_ref[:, features:] = jnp.where(first, passed, kept)


def place_halves(near, kept, passed, before):
    rows, features = kept.shape
    return pl.pallas_call(
        place_kernel,
        in_specs=[
            pl.BlockSpec(memory_space=pltpu.SMEM),
            *[pl.BlockSpec(memory_space=pltpu.VMEM)] * 2,
            pl.BlockSpec(memory_space=pl.ANY),
        ],
        out_shape=jax.ShapeDtypeStruct((rows, PAIR * features), kept.dtype),
        compiler_params=params(),
    )(near[None], kept, passed, *in_hbm(before))


def add_kernel(count, *refs):
    terms, out_refs = refs[: 2 * count], refs[-count:]
    for at in range(count):
        left, right = terms[2 * at][...], terms[2 * at + 1][...]
        total = left.astype(jnp.float32) + right.astype(jnp.float32)
        out_refs[at][...] = total.astype(out_refs[at].dtype)


def add_pairs(pairs, before):
    flat = [term for pair in pairs for term in pair]
    return pl.pallas_call(
        functools.partial(add_kernel, len(pairs)),
        in_specs=[
            *[pl.BlockSpec(memory_space=pltpu.VMEM) for _ in flat],
            *[pl.BlockSpec(memory_space=pl.ANY) for _ in before],
        ],
        out_shape=[jax.ShapeDtypeStruct(pair[0].shape, pair[0].dtype) for pair in pairs],
        compiler_params=params(),
    )(*flat, *in_hbm(*before))


def pack_kernel(
    local_experts, far_ref, ids_ref, gates_ref, preact_ref, tokens_ref, *refs
):
    out_ref, activation_ref, scaled_ref, weighted = refs[-4:]
    blocks, height, features = out_ref.shape
    rows, wide = preact_ref.shape
    far_count = far_ref.shape[0]
    taken = rows * wide // features

    @pl.when(pl.program_id(0) == 0)
    def _():
        activation, slope = gelu_parts(preact_ref[...].astype(jnp.float32))
        gates = jnp.where(low_half((rows, wide)), *columns_of(gates_ref[...], wide))
        activation_ref[...] = activation
        scaled_ref[...] = gates * slope
        weighted[...] = (gates * activation).astype(jnp.bfloat16)

    ids = ids_ref[...]
    local = lax.rem(ids, local_experts)
    line = lax.div(ids, local_experts)
    far, near = lax.div(line, PAIR), lax.rem(line, PAIR)
    far_place = jnp.zeros_like(far)
    for at in range(far_count):
        far_place = jnp.where(far == at, far_ref[at], far_place)
    for block in range(blocks):
        side = lax.rem(near + block, PAIR)
        place = (far_place * PAIR + side) * local_experts + local
        out_ref[block, 0:rows, :] = tokens_ref[:, block * features : (block + 1) * features]
        for at in range(0, features, wide):
            start = at // wide * taken
            out_ref[block, rows : rows + taken, at : at + wide] = weighted[start : start + taken, :]
        last = height - TILE
        out_ref[block, last:, :] = jnp.zeros((TILE, features), jnp.bfloat16)
        out_ref[block, last : last + 2, 0:rows] = place.astype(jnp.bfloat16)


def pack_tokens(far_places, ids, gates, preact, tokens, members, local_experts, before):
    rows, width = tokens.shape
    features = width // members
    each = members // 4
    height = rows + preact.size // features + TILE
    small = jax.ShapeDtypeStruct(preact.shape, jnp.float32)
    whole = [pl.BlockSpec(array.shape, lambda i: (0, 0)) for array in (ids, gates, preact)]
    return pl.pallas_call(
        functools.partial(pack_kernel, local_experts),
        grid=(4,),
        in_specs=[
            pl.BlockSpec(memory_space=pltpu.SMEM),
            *whole,
            pl.BlockSpec((rows, each * features), lambda i: (0, i)),
            *[pl.BlockSpec(memory_space=pl.ANY) for _ in before],
        ],
        out_specs=(pl.BlockSpec((each, height, features), lambda i: (i, 0, 0)), whole[2], whole[2]),
        out_shape=(
            pltpu.HBM((members, height, features), jnp.bfloat16), small, small,
        ),
        scratch_shapes=[pltpu.VMEM(preact.shape, jnp.bfloat16)],
        compiler_params=params(),
    )(far_places, ids, gates, preact, tokens, *in_hbm(*before))


def unpack_kernel(parts_ref, out_ref):
    blocks, _, features = parts_ref.shape
    for block in range(blocks):
        out_ref[:, block * features : (block + 1) * features] = parts_ref[block]


def unpack_tokens(parts):
    members, rows, features = parts.shape
    each = members // 4
    return pl.pallas_call(
        unpack_kernel,
        grid=(4,),
        in_specs=[pl.BlockSpec((each, rows, features), lambda i: (i, 0, 0))],
        out_specs=pl.BlockSpec((rows, each * features), lambda i: (0, i)),
        out_shape=jax.ShapeDtypeStruct((rows, members * features), jnp.bfloat16),
        compiler_params=params(),
    )(parts)


def places_of(received_ref, source, rows):
    at = received_ref.shape[1] - TILE
    return received_ref[source, at : at + 2, 0:rows]


def token_rows(received_ref, rows):
    sources, _, features = received_ref.shape
    return received_ref[:, 0:rows, :].reshape(sources * rows, features)


def down_kernel(rows, wide, count, received_ref, *refs):
    out_refs, (turned, numbers, spread) = refs[-3 - count : -3], refs[-3:]
    sources, _, features = received_ref.shape
    hidden, each = wide // 2, BLOCK // (wide // 2)
    taken = rows * wide // features
    for source in range(sources):
        weighted = jnp.concatenate(
            [
                received_ref[source, rows : rows + taken, at : at + wide].astype(jnp.float32)
                for at in range(0, features, wide)
            ]
        )
        lanes = slice(source * rows, (source + 1) * rows)
        turned[:, lanes] = weighted.T
        numbers[:, lanes] = places_of(received_ref, source, rows).astype(jnp.float32)
    number = 0
    for out_ref in out_refs:
        for start in range(0, out_ref.shape[0], BLOCK):
            for expert in range(each):
                spread[expert * hidden : (expert + 1) * hidden, :] = jnp.where(
                    numbers[0:1, :] == number + expert,
                    turned[0:hidden, :],
                    jnp.where(numbers[1:2, :] == number + expert, turned[hidden:, :], 0.0),
                ).astype(jnp.bfloat16)
            number += each
            out_ref[start : start + BLOCK, :] = jnp.dot(
                spread[...], token_rows(received_ref, rows), preferred_element_type=jnp.float32
            ).astype(out_ref.dtype)


def down_partial(received, rows, wide, total_rows, count, before):
    sources, _, features = received.shape
    total = sources * rows
    return pl.pallas_call(
        functools.partial(down_kernel, rows, wide, count),
        in_specs=[
            pl.BlockSpec(memory_space=pltpu.VMEM),
            *[pl.BlockSpec(memory_space=pl.ANY) for _ in before],
        ],
        out_shape=[jax.ShapeDtypeStruct((total_rows // count, features), jnp.bfloat16)] * count,
        scratch_shapes=[
            pltpu.VMEM((wide, total), jnp.float32),
            pltpu.VMEM((2, total), jnp.float32),
            pltpu.VMEM((BLOCK, total), jnp.bfloat16),
        ],
        compiler_params=params(),
        cost_estimate=cost(total_rows, total, features),
    )(received, *in_hbm(*before))


def lane_numbers(received_ref, rows, wide):
    sources = received_ref.shape[0]
    low = low_half((sources * rows, wide))
    found = [
        columns_of(places_of(received_ref, source, rows), wide)
        for source in range(sources)
    ]
    odd = jnp.where(low, 0.0, 1.0)
    return low, *[jnp.concatenate([pair[k] for pair in found]) - odd for k in range(2)]


def join(piece_refs, full):
    start = 0
    for ref in piece_refs:
        full[start : start + ref.shape[0], :] = ref[...]
        start += ref.shape[0]


def project_kernel(count, received_ref, *refs):
    piece_refs, (out_ref, full) = refs[:count], refs[-2:]
    pl.when(pl.program_id(0) == 0)(lambda: join(piece_refs, full))
    sources, rows, wide = out_ref.shape
    low, first, second = lane_numbers(received_ref, rows, wide)
    tokens = token_rows(received_ref, rows)
    sums = [jnp.zeros((sources * rows, wide), jnp.float32) for _ in range(2)]
    number = 0.0
    for start in range(0, full.shape[0], BLOCK):
        product = lax.dot_general(
            tokens,
            full[start : start + BLOCK, :],
            (((1,), (1,)), ((), ())),
            preferred_element_type=jnp.float32,
        )
        for at in range(0, BLOCK, wide):
            part = product[:, at : at + wide]
            sums[0] = jnp.where(first == number, part, sums[0])
            sums[1] = jnp.where(second == number, part, sums[1])
            number += 2.0
    folded = [value + pltpu.roll(value, wide // 2, 1) for value in sums]
    value = jnp.where(low, folded[0], folded[1]).astype(out_ref.dtype)
    out_ref[...] = value.reshape(out_ref.shape)


def project(received, pieces, rows, wide, before):
    sources, height, features = received.shape
    joined = sum(piece.shape[0] for piece in pieces)
    return pl.pallas_call(
        functools.partial(project_kernel, len(pieces)),
        grid=(sources // 2,),
        in_specs=[
            pl.BlockSpec((2, height, features), lambda i: (i, 0, 0)),
            *[pl.BlockSpec(piece.shape, lambda i: (0, 0)) for piece in pieces],
            *[pl.BlockSpec(memory_space=pl.ANY) for _ in before],
        ],
        out_specs=pl.BlockSpec((2, rows, wide), lambda i: (i, 0, 0)),
        out_shape=pltpu.HBM((sources, rows, wide), jnp.bfloat16),
        scratch_shapes=[pltpu.VMEM((joined, features), jnp.bfloat16)],
        compiler_params=params(),
        cost_estimate=cost(sources * rows, features, joined),
    )(received, *in_hbm(*pieces), *before)


def hidden_kernel(parts_ref, activation_ref, scaled_ref, hidden_ref, gate_ref):
    projected = parts_ref[0].astype(jnp.float32)
    for source in range(1, parts_ref.shape[0]):
        projected = projected + parts_ref[source].astype(jnp.float32)
    wide = projected.shape[1]
    half = lax.broadcasted_iota(jnp.int32, (8, wide), 1) // (wide // 2)
    wanted = lax.broadcasted_iota(jnp.int32, (8, wide), 0)
    sums = lax.dot_general(
        jnp.where(wanted == half, 1.0, 0.0),
        activation_ref[...] * projected,
        (((1,), (1,)), ((), ())),
        precision=lax.Precision.HIGHEST,
        preferred_element_type=jnp.float32,
    )
    gate_ref[...] = sums[0:2, :].astype(gate_ref.dtype)
    hidden = (projected * scaled_ref[...]).astype(hidden_ref.dtype)
    for source in range(hidden_ref.shape[0]):
        hidden_ref[source] = hidden


def input_kernel(count, received_ref, hidden_ref, *refs):
    piece_refs, (out_ref, full, spread) = refs[:count], refs[-3:]
    pl.when(pl.program_id(0) == 0)(lambda: join(piece_refs, full))
    sources, rows, wide = hidden_ref.shape
    low, first, second = lane_numbers(received_ref, rows, wide)
    values = hidden_ref[...].reshape(sources * rows, wide).astype(jnp.float32)
    swapped = pltpu.roll(values, wide // 2, 1)
    one = jnp.where(low, values, swapped)
    two = jnp.where(low, swapped, values)
    for start in range(0, full.shape[0], wide):
        number = start // wide * 2.0
        spread[:, start : start + wide] = jnp.where(
            first == number, one, jnp.where(second == number, two, 0.0)
        ).astype(jnp.bfloat16)
    out_ref[...] = (
        jnp.dot(spread[...], full[...], preferred_element_type=jnp.float32)
        .astype(out_ref.dtype)
        .reshape(out_ref.shape)
    )


def input_rows(received, hidden_grad, pieces, before):
    sources, rows, wide = hidden_grad.shape
    joined, features = sum(piece.shape[0] for piece in pieces), pieces[0].shape[1]
    return pl.pallas_call(
        functools.partial(input_kernel, len(pieces)),
        grid=(sources // 2,),
        in_specs=[
            pl.BlockSpec((2, received.shape[1], features), lambda i: (i, 0, 0)),
            pl.BlockSpec((2, rows, wide), lambda i: (i, 0, 0)),
            *[pl.BlockSpec(piece.shape, lambda i: (0, 0)) for piece in pieces],
            *[pl.BlockSpec(memory_space=pl.ANY) for _ in before],
        ],
        out_specs=pl.BlockSpec((2, rows, features), lambda i: (i, 0, 0)),
        out_shape=pltpu.HBM((sources, rows, features), jnp.bfloat16),
        scratch_shapes=[
            pltpu.VMEM((joined, features), jnp.bfloat16),
            pltpu.VMEM((2 * rows, joined), jnp.bfloat16),
        ],
        compiler_params=params(),
        cost_estimate=cost(sources * rows, joined, features),
    )(received, hidden_grad, *in_hbm(*pieces, *before))


def exchange(value, axes):
    return lax.all_to_all(value, axes, split_axis=0, concat_axis=0, tiled=True)


def swap(value, axis):
    return lax.ppermute(value, axis, SWAP)


def add(*terms):
    return sum(term.astype(jnp.float32) for term in terms).astype(jnp.bfloat16)


def body(token_grads, router_gates, expert_ids, saved_hidden, up_weight, down_weight):
    tok_count = token_grads.shape[0]
    local_experts, hidden, width = up_weight.shape
    members, far_count = lax.axis_size(GROUP), lax.axis_size(FAR)
    wide, features = 2 * hidden, width // PAIR
    own_rows = local_experts * hidden
    near = lax.axis_index("near")
    paired = lax.axis_size("high") == PAIR

    def halves(weight):
        flat = weight.reshape(own_rows, width)
        own = lax.dynamic_slice_in_dim(flat, near * features, features, axis=1)
        other = lax.dynamic_slice_in_dim(flat, (1 - near) * features, features, axis=1)
        return own, swap(other, "near")

    down_halves, up_halves = halves(down_weight), halves(up_weight)
    first = [down_halves[1], up_halves[1]]
    far_places = jnp.arange(far_count, dtype=jnp.int32)
    if paired:
        high_place = far_places // PAIR ^ lax.axis_index("high")
        far_places = (far_places % PAIR ^ lax.axis_index("low")) * PAIR + high_place
        beside = [swap(half, "high") for half in down_halves]
        low = [swap(half, "low") for half in down_halves]
        low_beside = [swap(half, "low") for half in beside]
        down_pieces = [*down_halves, *beside, *low, *low_beside]
        first += [beside[0], *low]
        up_low = swap(stack(*up_halves, ()), "low")
        up_own = stack(*up_halves, (beside[1], up_low))
        up_beside = swap(up_own, "high")
    else:
        down_pieces = [lax.all_gather(stack(*down_halves, ()), FAR, tiled=True)]
        up_pieces = [lax.all_gather(stack(*up_halves, ()), FAR, tiled=True)]
    packed, activation, scaled = pack_tokens(
        far_places, expert_ids.T, router_gates.T, saved_hidden, token_grads, members,
        local_experts, first,
    )
    received = exchange(packed, GROUP)

    partial_value = down_partial(
        received, tok_count, wide, own_rows * PAIR * far_count, far_count if paired else 1, ()
    )
    projected = project(received, down_pieces, tok_count, wide, partial_value[:1])
    if paired:
        up_beside = pass_on(up_beside, (projected,))
        up_pieces = [up_own, up_beside, up_low, swap(up_beside, "low")]
    parts = exchange(projected, GROUP)
    gathered = pl.BlockSpec((members, tok_count, wide), lambda i: (0, 0, 0))
    single = pl.BlockSpec((tok_count, wide), lambda i: (0, 0))
    hidden_grad, gate_grads = pl.pallas_call(
        hidden_kernel,
        grid=(1,),
        in_specs=[gathered, single, single],
        out_specs=(gathered, pl.BlockSpec((2, tok_count), lambda i: (0, 0))),
        out_shape=(
            pltpu.HBM((members, tok_count, wide), jnp.bfloat16),
            jax.ShapeDtypeStruct((2, tok_count), jnp.bfloat16),
        ),
        compiler_params=params(),
    )(parts, activation, scaled)
    if paired:
        own, beside, low, low_beside = partial_value
        before = add_pairs([(beside, swap(low_beside, "low"))], ())
        low = swap(low, "low")
        passed, kept = [
            add(own[at], low[at], swap(before[0][at], "high"))
            for at in (slice(own_rows, None), slice(0, own_rows))
        ]
    else:
        before = ()
        sums = lax.psum_scatter(partial_value[0], FAR, scatter_dimension=0, tiled=True)
        kept, passed = sums[:own_rows], sums[own_rows:]
    rows_back = input_rows(received, exchange(hidden_grad, GROUP), up_pieces, before)
    input_grads = unpack_tokens(exchange(rows_back, GROUP))

    down_grads = place_halves(near, kept, swap(passed, "near"), input_grads)
    down_grads = down_grads.reshape(down_weight.shape)
    return (input_grads, gate_grads.T, down_grads)


def solution(mesh):
    sizes = [mesh.shape[name] for name in ("expert", "inner", "outer")]
    expert = ("high", "low", "near")
    split = Mesh(
        mesh.devices.reshape(sizes[0] // PAIR**2, PAIR, PAIR, *sizes[1:]),
        (*expert, "inner", "outer"),
    )
    rows = P((*expert, "inner", "outer"), None)
    weights = P(expert, None, ("inner", "outer"))
    return jax.shard_map(
        body,
        mesh=split,
        in_specs=(rows, rows, rows, rows, weights, weights),
        out_specs=(rows, rows, weights),
        check_vma=False,
    )
```

```python
import functools
import jax
import jax.numpy as jnp
from jax import lax
from jax.experimental import pallas as pl
from jax.experimental.pallas import tpu as pltpu
from jax.sharding import Mesh, PartitionSpec as P

root_half = 0.7071067811865476
inv_root_tau = 0.3989422804014327
GROUP = ("inner", "outer", "near")
FAR = ("high", "low")
PAIR = 2
BLOCK = 256
TILE = 16
MIB = 1 << 20
SWAP = ((0, 1), (1, 0))


def gelu_parts(preact):
    cumulative = 0.5 * (1.0 + lax.erf(preact * root_half))
    density = inv_root_tau * jnp.exp(-0.5 * preact * preact)
    return (preact * cumulative, cumulative + preact * density)


def params(grant=20):
    return pltpu.CompilerParams(vmem_limit_bytes=grant * MIB)


def cost(rows, inner, columns):
    return pl.CostEstimate(
        flops=2 * rows * inner * columns,
        bytes_accessed=2 * (rows * inner + inner * columns + rows * columns),
        transcendentals=0,
    )


def low_half(shape):
    return lax.broadcasted_iota(jnp.int32, shape, len(shape) - 1) < shape[-1] // 2


def columns_of(pair, wide):
    wanted = lax.broadcasted_iota(jnp.int32, (2, wide), 0)
    return [
        lax.dot_general(
            pair.astype(jnp.bfloat16),
            jnp.where(wanted == k, 1.0, 0.0).astype(jnp.bfloat16),
            (((0,), (0,)), ((), ())),
            preferred_element_type=jnp.float32,
        )
        for k in range(2)
    ]


def in_hbm(*arrays):
    return [pltpu.with_memory_space_constraint(array, pltpu.HBM) for array in arrays]


def stack_kernel(own_ref, other_ref, *refs):
    rows = own_ref.shape[0]
    refs[-1][0:rows, :] = own_ref[...]
    refs[-1][rows:, :] = other_ref[...]


def stack(own, other, before):
    return pl.pallas_call(
        stack_kernel,
        in_specs=[
            *[pl.BlockSpec(memory_space=pltpu.VMEM)] * 2,
            *[pl.BlockSpec(memory_space=pl.ANY) for _ in before],
        ],
        out_shape=jax.ShapeDtypeStruct((2 * own.shape[0], own.shape[1]), own.dtype),
        compiler_params=params(),
    )(own, other, *in_hbm(*before))


def pass_on(value, before):
    anywhere = pl.BlockSpec(memory_space=pl.ANY)
    return pl.pallas_call(
        lambda *refs: None,
        in_specs=[anywhere] * (1 + len(before)),
        out_specs=anywhere,
        out_shape=pltpu.HBM(value.shape, value.dtype),
        input_output_aliases={0: 0},
        compiler_params=params(),
    )(*in_hbm(value), *before)


def place_kernel(near_ref, kept_ref, passed_ref, before_ref, out_ref):
    features = kept_ref.shape[1]
    first = near_ref[0] == 0
    kept, passed = kept_ref[...], passed_ref[...]
    out_ref[:, 0:features] = jnp.where(first, kept, passed)
    out_ref[:, features:] = jnp.where(first, passed, kept)


def place_halves(near, kept, passed, before):
    rows, features = kept.shape
    return pl.pallas_call(
        place_kernel,
        in_specs=[
            pl.BlockSpec(memory_space=pltpu.SMEM),
            *[pl.BlockSpec(memory_space=pltpu.VMEM)] * 2,
            pl.BlockSpec(memory_space=pl.ANY),
        ],
        out_shape=jax.ShapeDtypeStruct((rows, PAIR * features), kept.dtype),
        compiler_params=params(),
    )(near[None], kept, passed, *in_hbm(before))


def add_kernel(count, *refs):
    terms, out_refs = refs[: 2 * count], refs[-count:]
    for at in range(count):
        left, right = terms[2 * at][...], terms[2 * at + 1][...]
        total = left.astype(jnp.float32) + right.astype(jnp.float32)
        out_refs[at][...] = total.astype(out_refs[at].dtype)


def add_pairs(pairs, before):
    flat = [term for pair in pairs for term in pair]
    return pl.pallas_call(
        functools.partial(add_kernel, len(pairs)),
        in_specs=[
            *[pl.BlockSpec(memory_space=pltpu.VMEM) for _ in flat],
            *[pl.BlockSpec(memory_space=pl.ANY) for _ in before],
        ],
        out_shape=[jax.ShapeDtypeStruct(pair[0].shape, pair[0].dtype) for pair in pairs],
        compiler_params=params(),
    )(*flat, *in_hbm(*before))


def pack_kernel(
    local_experts, far_ref, ids_ref, gates_ref, preact_ref, tokens_ref, *refs
):
    out_ref, activation_ref, scaled_ref, weighted = refs[-4:]
    blocks, height, features = out_ref.shape
    rows, wide = preact_ref.shape
    far_count = far_ref.shape[0]
    taken = rows * wide // features

    @pl.when(pl.program_id(0) == 0)
    def _():
        activation, slope = gelu_parts(preact_ref[...].astype(jnp.float32))
        gates = jnp.where(low_half((rows, wide)), *columns_of(gates_ref[...], wide))
        activation_ref[...] = activation
        scaled_ref[...] = gates * slope
        weighted[...] = (gates * activation).astype(jnp.bfloat16)

    ids = ids_ref[...]
    local = lax.rem(ids, local_experts)
    line = lax.div(ids, local_experts)
    far, near = lax.div(line, PAIR), lax.rem(line, PAIR)
    far_place = jnp.zeros_like(far)
    for at in range(far_count):
        far_place = jnp.where(far == at, far_ref[at], far_place)
    for block in range(blocks):
        side = lax.rem(near + block, PAIR)
        place = (far_place * PAIR + side) * local_experts + local
        out_ref[block, 0:rows, :] = tokens_ref[:, block * features : (block + 1) * features]
        for at in range(0, features, wide):
            start = at // wide * taken
            out_ref[block, rows : rows + taken, at : at + wide] = weighted[start : start + taken, :]
        last = height - TILE
        out_ref[block, last:, :] = jnp.zeros((TILE, features), jnp.bfloat16)
        out_ref[block, last : last + 2, 0:rows] = place.astype(jnp.bfloat16)


def pack_tokens(far_places, ids, gates, preact, tokens, members, local_experts, before):
    rows, width = tokens.shape
    features = width // members
    each = members // 4
    height = rows + preact.size // features + TILE
    small = jax.ShapeDtypeStruct(preact.shape, jnp.float32)
    whole = [pl.BlockSpec(array.shape, lambda i: (0, 0)) for array in (ids, gates, preact)]
    return pl.pallas_call(
        functools.partial(pack_kernel, local_experts),
        grid=(4,),
        in_specs=[
            pl.BlockSpec(memory_space=pltpu.SMEM),
            *whole,
            pl.BlockSpec((rows, each * features), lambda i: (0, i)),
            *[pl.BlockSpec(memory_space=pl.ANY) for _ in before],
        ],
        out_specs=(pl.BlockSpec((each, height, features), lambda i: (i, 0, 0)), whole[2], whole[2]),
        out_shape=(
            pltpu.HBM((members, height, features), jnp.bfloat16), small, small,
        ),
        scratch_shapes=[pltpu.VMEM(preact.shape, jnp.bfloat16)],
        compiler_params=params(),
    )(far_places, ids, gates, preact, tokens, *in_hbm(*before))


def unpack_kernel(parts_ref, out_ref):
    blocks, _, features = parts_ref.shape
    for block in range(blocks):
        out_ref[:, block * features : (block + 1) * features] = parts_ref[block]


def unpack_tokens(parts):
    members, rows, features = parts.shape
    each = members // 4
    return pl.pallas_call(
        unpack_kernel,
        grid=(4,),
        in_specs=[pl.BlockSpec((each, rows, features), lambda i: (i, 0, 0))],
        out_specs=pl.BlockSpec((rows, each * features), lambda i: (0, i)),
        out_shape=jax.ShapeDtypeStruct((rows, members * features), jnp.bfloat16),
        compiler_params=params(),
    )(parts)


def places_of(received_ref, source, rows):
    at = received_ref.shape[1] - TILE
    return received_ref[source, at : at + 2, 0:rows]


def token_rows(received_ref, rows):
    sources, _, features = received_ref.shape
    return received_ref[:, 0:rows, :].reshape(sources * rows, features)


def down_kernel(rows, wide, count, received_ref, *refs):
    out_refs, (turned, numbers, spread) = refs[-3 - count : -3], refs[-3:]
    sources, _, features = received_ref.shape
    hidden, each = wide // 2, BLOCK // (wide // 2)
    taken = rows * wide // features
    for source in range(sources):
        weighted = jnp.concatenate(
            [
                received_ref[source, rows : rows + taken, at : at + wide].astype(jnp.float32)
                for at in range(0, features, wide)
            ]
        )
        lanes = slice(source * rows, (source + 1) * rows)
        turned[:, lanes] = weighted.T
        numbers[:, lanes] = places_of(received_ref, source, rows).astype(jnp.float32)
    number = 0
    for out_ref in out_refs:
        for start in range(0, out_ref.shape[0], BLOCK):
            for expert in range(each):
                spread[expert * hidden : (expert + 1) * hidden, :] = jnp.where(
                    numbers[0:1, :] == number + expert,
                    turned[0:hidden, :],
                    jnp.where(numbers[1:2, :] == number + expert, turned[hidden:, :], 0.0),
                ).astype(jnp.bfloat16)
            number += each
            out_ref[start : start + BLOCK, :] = jnp.dot(
                spread[...], token_rows(received_ref, rows), preferred_element_type=jnp.float32
            ).astype(out_ref.dtype)


def down_partial(received, rows, wide, total_rows, count, before):
    sources, _, features = received.shape
    total = sources * rows
    return pl.pallas_call(
        functools.partial(down_kernel, rows, wide, count),
        in_specs=[
            pl.BlockSpec(memory_space=pltpu.VMEM),
            *[pl.BlockSpec(memory_space=pl.ANY) for _ in before],
        ],
        out_shape=[jax.ShapeDtypeStruct((total_rows // count, features), jnp.bfloat16)] * count,
        scratch_shapes=[
            pltpu.VMEM((wide, total), jnp.float32),
            pltpu.VMEM((2, total), jnp.float32),
            pltpu.VMEM((BLOCK, total), jnp.bfloat16),
        ],
        compiler_params=params(),
        cost_estimate=cost(total_rows, total, features),
    )(received, *in_hbm(*before))


def lane_numbers(received_ref, rows, wide):
    sources = received_ref.shape[0]
    low = low_half((sources * rows, wide))
    found = [
        columns_of(places_of(received_ref, source, rows), wide)
        for source in range(sources)
    ]
    odd = jnp.where(low, 0.0, 1.0)
    return low, *[jnp.concatenate([pair[k] for pair in found]) - odd for k in range(2)]


def join(piece_refs, full):
    start = 0
    for ref in piece_refs:
        full[start : start + ref.shape[0], :] = ref[...]
        start += ref.shape[0]


def project_kernel(count, received_ref, *refs):
    piece_refs, (out_ref, full) = refs[:count], refs[-2:]
    pl.when(pl.program_id(0) == 0)(lambda: join(piece_refs, full))
    sources, rows, wide = out_ref.shape
    low, first, second = lane_numbers(received_ref, rows, wide)
    tokens = token_rows(received_ref, rows)
    sums = [jnp.zeros((sources * rows, wide), jnp.float32) for _ in range(2)]
    number = 0.0
    for start in range(0, full.shape[0], BLOCK):
        product = lax.dot_general(
            tokens,
            full[start : start + BLOCK, :],
            (((1,), (1,)), ((), ())),
            preferred_element_type=jnp.float32,
        )
        for at in range(0, BLOCK, wide):
            part = product[:, at : at + wide]
            sums[0] = jnp.where(first == number, part, sums[0])
            sums[1] = jnp.where(second == number, part, sums[1])
            number += 2.0
    folded = [value + pltpu.roll(value, wide // 2, 1) for value in sums]
    value = jnp.where(low, folded[0], folded[1]).astype(out_ref.dtype)
    out_ref[...] = value.reshape(out_ref.shape)


def project(received, pieces, rows, wide, before):
    sources, height, features = received.shape
    joined = sum(piece.shape[0] for piece in pieces)
    return pl.pallas_call(
        functools.partial(project_kernel, len(pieces)),
        grid=(sources // 2,),
        in_specs=[
            pl.BlockSpec((2, height, features), lambda i: (i, 0, 0)),
            *[pl.BlockSpec(piece.shape, lambda i: (0, 0)) for piece in pieces],
            *[pl.BlockSpec(memory_space=pl.ANY) for _ in before],
        ],
        out_specs=pl.BlockSpec((2, rows, wide), lambda i: (i, 0, 0)),
        out_shape=pltpu.HBM((sources, rows, wide), jnp.bfloat16),
        scratch_shapes=[pltpu.VMEM((joined, features), jnp.bfloat16)],
        compiler_params=params(),
        cost_estimate=cost(sources * rows, features, joined),
    )(received, *in_hbm(*pieces), *before)


def hidden_kernel(parts_ref, activation_ref, scaled_ref, hidden_ref, gate_ref):
    projected = parts_ref[0].astype(jnp.float32)
    for source in range(1, parts_ref.shape[0]):
        projected = projected + parts_ref[source].astype(jnp.float32)
    wide = projected.shape[1]
    half = lax.broadcasted_iota(jnp.int32, (8, wide), 1) // (wide // 2)
    wanted = lax.broadcasted_iota(jnp.int32, (8, wide), 0)
    sums = lax.dot_general(
        jnp.where(wanted == half, 1.0, 0.0),
        activation_ref[...] * projected,
        (((1,), (1,)), ((), ())),
        precision=lax.Precision.HIGHEST,
        preferred_element_type=jnp.float32,
    )
    gate_ref[...] = sums[0:2, :].astype(gate_ref.dtype)
    hidden = (projected * scaled_ref[...]).astype(hidden_ref.dtype)
    for source in range(hidden_ref.shape[0]):
        hidden_ref[source] = hidden


def input_kernel(count, received_ref, hidden_ref, *refs):
    piece_refs, (out_ref, full, spread) = refs[:count], refs[-3:]
    pl.when(pl.program_id(0) == 0)(lambda: join(piece_refs, full))
    sources, rows, wide = hidden_ref.shape
    low, first, second = lane_numbers(received_ref, rows, wide)
    values = hidden_ref[...].reshape(sources * rows, wide).astype(jnp.float32)
    swapped = pltpu.roll(values, wide // 2, 1)
    one = jnp.where(low, values, swapped)
    two = jnp.where(low, swapped, values)
    for start in range(0, full.shape[0], wide):
        number = start // wide * 2.0
        spread[:, start : start + wide] = jnp.where(
            first == number, one, jnp.where(second == number, two, 0.0)
        ).astype(jnp.bfloat16)
    out_ref[...] = (
        jnp.dot(spread[...], full[...], preferred_element_type=jnp.float32)
        .astype(out_ref.dtype)
        .reshape(out_ref.shape)
    )


def input_rows(received, hidden_grad, pieces, before):
    sources, rows, wide = hidden_grad.shape
    joined, features = sum(piece.shape[0] for piece in pieces), pieces[0].shape[1]
    return pl.pallas_call(
        functools.partial(input_kernel, len(pieces)),
        grid=(sources // 2,),
        in_specs=[
            pl.BlockSpec((2, received.shape[1], features), lambda i: (i, 0, 0)),
            pl.BlockSpec((2, rows, wide), lambda i: (i, 0, 0)),
            *[pl.BlockSpec(piece.shape, lambda i: (0, 0)) for piece in pieces],
            *[pl.BlockSpec(memory_space=pl.ANY) for _ in before],
        ],
        out_specs=pl.BlockSpec((2, rows, features), lambda i: (i, 0, 0)),
        out_shape=pltpu.HBM((sources, rows, features), jnp.bfloat16),
        scratch_shapes=[
            pltpu.VMEM((joined, features), jnp.bfloat16),
            pltpu.VMEM((2 * rows, joined), jnp.bfloat16),
        ],
        compiler_params=params(),
        cost_estimate=cost(sources * rows, joined, features),
    )(received, hidden_grad, *in_hbm(*pieces, *before))


def exchange(value, axes):
    return lax.all_to_all(value, axes, split_axis=0, concat_axis=0, tiled=True)


def swap(value, axis):
    return lax.ppermute(value, axis, SWAP)


def add(*terms):
    return sum(term.astype(jnp.float32) for term in terms).astype(jnp.bfloat16)


def body(token_grads, router_gates, expert_ids, saved_hidden, up_weight, down_weight):
    tok_count = token_grads.shape[0]
    local_experts, hidden, width = up_weight.shape
    members, far_count = lax.axis_size(GROUP), lax.axis_size(FAR)
    wide, features = 2 * hidden, width // PAIR
    own_rows = local_experts * hidden
    near = lax.axis_index("near")
    paired = lax.axis_size("high") == PAIR

    def halves(weight):
        flat = weight.reshape(own_rows, width)
        own = lax.dynamic_slice_in_dim(flat, near * features, features, axis=1)
        other = lax.dynamic_slice_in_dim(flat, (1 - near) * features, features, axis=1)
        return own, swap(other, "near")

    down_halves, up_halves = halves(down_weight), halves(up_weight)
    first = [down_halves[1], up_halves[1]]
    far_places = jnp.arange(far_count, dtype=jnp.int32)
    if paired:
        high_place = far_places // PAIR ^ lax.axis_index("high")
        far_places = (far_places % PAIR ^ lax.axis_index("low")) * PAIR + high_place
        beside = [swap(half, "high") for half in down_halves]
        low = [swap(half, "low") for half in down_halves]
        low_beside = [swap(half, "low") for half in beside]
        down_pieces = [*down_halves, *beside, *low, *low_beside]
        first += [beside[0], *low]
        up_own = stack(*up_halves, (beside[1], low_beside[0]))
        up_beside = swap(up_own, "high")
        up_low = swap(up_own, "low")
    else:
        down_pieces = [lax.all_gather(stack(*down_halves, ()), FAR, tiled=True)]
        up_pieces = [lax.all_gather(stack(*up_halves, ()), FAR, tiled=True)]
    packed, activation, scaled = pack_tokens(
        far_places, expert_ids.T, router_gates.T, saved_hidden, token_grads, members,
        local_experts, first,
    )
    received = exchange(packed, GROUP)

    partial_value = down_partial(
        received, tok_count, wide, own_rows * PAIR * far_count, far_count if paired else 1, ()
    )
    projected = project(received, down_pieces, tok_count, wide, partial_value[:1])
    if paired:
        up_beside = pass_on(up_beside, (projected,))
        up_pieces = [up_own, up_beside, up_low, swap(up_beside, "low")]
    parts = exchange(projected, GROUP)
    gathered = pl.BlockSpec((members, tok_count, wide), lambda i: (0, 0, 0))
    single = pl.BlockSpec((tok_count, wide), lambda i: (0, 0))
    hidden_grad, gate_grads = pl.pallas_call(
        hidden_kernel,
        grid=(1,),
        in_specs=[gathered, single, single],
        out_specs=(gathered, pl.BlockSpec((2, tok_count), lambda i: (0, 0))),
        out_shape=(
            pltpu.HBM((members, tok_count, wide), jnp.bfloat16),
            jax.ShapeDtypeStruct((2, tok_count), jnp.bfloat16),
        ),
        compiler_params=params(),
    )(parts, activation, scaled)
    if paired:
        own, beside, low, low_beside = partial_value
        before = add_pairs([(beside, swap(low_beside, "low"))], ())
        low = swap(low, "low")
        passed, kept = [
            add(own[at], low[at], swap(before[0][at], "high"))
            for at in (slice(own_rows, None), slice(0, own_rows))
        ]
    else:
        before = ()
        sums = lax.psum_scatter(partial_value[0], FAR, scatter_dimension=0, tiled=True)
        kept, passed = sums[:own_rows], sums[own_rows:]
    rows_back = input_rows(received, exchange(hidden_grad, GROUP), up_pieces, before)
    input_grads = unpack_tokens(exchange(rows_back, GROUP))

    down_grads = place_halves(near, kept, swap(passed, "near"), input_grads)
    down_grads = down_grads.reshape(down_weight.shape)
    return (input_grads, gate_grads.T, down_grads)


def solution(mesh):
    sizes = [mesh.shape[name] for name in ("expert", "inner", "outer")]
    expert = ("high", "low", "near")
    split = Mesh(
        mesh.devices.reshape(sizes[0] // PAIR**2, PAIR, PAIR, *sizes[1:]),
        (*expert, "inner", "outer"),
    )
    rows = P((*expert, "inner", "outer"), None)
    weights = P(expert, None, ("inner", "outer"))
    return jax.shard_map(
        body,
        mesh=split,
        in_specs=(rows, rows, rows, rows, weights, weights),
        out_specs=(rows, rows, weights),
        check_vma=False,
    )
```

```python
import functools
import jax
import jax.numpy as jnp
from jax import lax
from jax.experimental import pallas as pl
from jax.experimental.pallas import tpu as pltpu
from jax.sharding import Mesh, PartitionSpec as P

root_half = 0.7071067811865476
inv_root_tau = 0.3989422804014327
GROUP = ("inner", "outer", "near")
FAR = ("high", "low")
PAIR = 2
BLOCK = 256
TILE = 16
MIB = 1 << 20
SWAP = ((0, 1), (1, 0))


def gelu_parts(preact):
    cumulative = 0.5 * (1.0 + lax.erf(preact * root_half))
    density = inv_root_tau * jnp.exp(-0.5 * preact * preact)
    return (preact * cumulative, cumulative + preact * density)


def params(grant=20):
    return pltpu.CompilerParams(vmem_limit_bytes=grant * MIB)


def cost(rows, inner, columns):
    return pl.CostEstimate(
        flops=2 * rows * inner * columns,
        bytes_accessed=2 * (rows * inner + inner * columns + rows * columns),
        transcendentals=0,
    )


def low_half(shape):
    return lax.broadcasted_iota(jnp.int32, shape, len(shape) - 1) < shape[-1] // 2


def columns_of(pair, wide):
    wanted = lax.broadcasted_iota(jnp.int32, (2, wide), 0)
    return [
        lax.dot_general(
            pair.astype(jnp.bfloat16),
            jnp.where(wanted == k, 1.0, 0.0).astype(jnp.bfloat16),
            (((0,), (0,)), ((), ())),
            preferred_element_type=jnp.float32,
        )
        for k in range(2)
    ]


def in_hbm(*arrays):
    return [pltpu.with_memory_space_constraint(array, pltpu.HBM) for array in arrays]


def stack_kernel(own_ref, other_ref, *refs):
    rows = own_ref.shape[0]
    refs[-1][0:rows, :] = own_ref[...]
    refs[-1][rows:, :] = other_ref[...]


def stack(own, other, before):
    return pl.pallas_call(
        stack_kernel,
        in_specs=[
            *[pl.BlockSpec(memory_space=pltpu.VMEM)] * 2,
            *[pl.BlockSpec(memory_space=pl.ANY) for _ in before],
        ],
        out_shape=jax.ShapeDtypeStruct((2 * own.shape[0], own.shape[1]), own.dtype),
        compiler_params=params(),
    )(own, other, *in_hbm(*before))


def pass_on(value, before):
    anywhere = pl.BlockSpec(memory_space=pl.ANY)
    return pl.pallas_call(
        lambda *refs: None,
        in_specs=[anywhere] * (1 + len(before)),
        out_specs=anywhere,
        out_shape=pltpu.HBM(value.shape, value.dtype),
        input_output_aliases={0: 0},
        compiler_params=params(),
    )(*in_hbm(value), *before)


def place_kernel(near_ref, kept_ref, passed_ref, before_ref, out_ref):
    features = kept_ref.shape[1]
    first = near_ref[0] == 0
    kept, passed = kept_ref[...], passed_ref[...]
    out_ref[:, 0:features] = jnp.where(first, kept, passed)
    out_ref[:, features:] = jnp.where(first, passed, kept)


def place_halves(near, kept, passed, before):
    rows, features = kept.shape
    return pl.pallas_call(
        place_kernel,
        in_specs=[
            pl.BlockSpec(memory_space=pltpu.SMEM),
            *[pl.BlockSpec(memory_space=pltpu.VMEM)] * 2,
            pl.BlockSpec(memory_space=pl.ANY),
        ],
        out_shape=jax.ShapeDtypeStruct((rows, PAIR * features), kept.dtype),
        compiler_params=params(),
    )(near[None], kept, passed, *in_hbm(before))


def add_kernel(count, *refs):
    terms, out_refs = refs[: 2 * count], refs[-count:]
    for at in range(count):
        left, right = terms[2 * at][...], terms[2 * at + 1][...]
        total = left.astype(jnp.float32) + right.astype(jnp.float32)
        out_refs[at][...] = total.astype(out_refs[at].dtype)


def add_pairs(pairs, before):
    flat = [term for pair in pairs for term in pair]
    return pl.pallas_call(
        functools.partial(add_kernel, len(pairs)),
        in_specs=[
            *[pl.BlockSpec(memory_space=pltpu.VMEM) for _ in flat],
            *[pl.BlockSpec(memory_space=pl.ANY) for _ in before],
        ],
        out_shape=[jax.ShapeDtypeStruct(pair[0].shape, pair[0].dtype) for pair in pairs],
        compiler_params=params(),
    )(*flat, *in_hbm(*before))


def pack_kernel(
    local_experts, far_ref, ids_ref, gates_ref, preact_ref, tokens_ref, *refs
):
    out_ref, activation_ref, scaled_ref, weighted = refs[-4:]
    blocks, height, features = out_ref.shape
    rows, wide = preact_ref.shape
    far_count = far_ref.shape[0]
    taken = rows * wide // features

    @pl.when(pl.program_id(0) == 0)
    def _():
        activation, slope = gelu_parts(preact_ref[...].astype(jnp.float32))
        gates = jnp.where(low_half((rows, wide)), *columns_of(gates_ref[...], wide))
        activation_ref[...] = activation
        scaled_ref[...] = gates * slope
        weighted[...] = (gates * activation).astype(jnp.bfloat16)

    ids = ids_ref[...]
    local = lax.rem(ids, local_experts)
    line = lax.div(ids, local_experts)
    far, near = lax.div(line, PAIR), lax.rem(line, PAIR)
    far_place = jnp.zeros_like(far)
    for at in range(far_count):
        far_place = jnp.where(far == at, far_ref[at], far_place)
    for block in range(blocks):
        side = lax.rem(near + block, PAIR)
        place = (far_place * PAIR + side) * local_experts + local
        out_ref[block, 0:rows, :] = tokens_ref[:, block * features : (block + 1) * features]
        for at in range(0, features, wide):
            start = at // wide * taken
            out_ref[block, rows : rows + taken, at : at + wide] = weighted[start : start + taken, :]
        last = height - TILE
        out_ref[block, last:, :] = jnp.zeros((TILE, features), jnp.bfloat16)
        out_ref[block, last : last + 2, 0:rows] = place.astype(jnp.bfloat16)


def pack_tokens(far_places, ids, gates, preact, tokens, members, local_experts, before):
    rows, width = tokens.shape
    features = width // members
    each = members // 4
    height = rows + preact.size // features + TILE
    small = jax.ShapeDtypeStruct(preact.shape, jnp.float32)
    whole = [pl.BlockSpec(array.shape, lambda i: (0, 0)) for array in (ids, gates, preact)]
    return pl.pallas_call(
        functools.partial(pack_kernel, local_experts),
        grid=(4,),
        in_specs=[
            pl.BlockSpec(memory_space=pltpu.SMEM),
            *whole,
            pl.BlockSpec((rows, each * features), lambda i: (0, i)),
            *[pl.BlockSpec(memory_space=pl.ANY) for _ in before],
        ],
        out_specs=(pl.BlockSpec((each, height, features), lambda i: (i, 0, 0)), whole[2], whole[2]),
        out_shape=(
            pltpu.HBM((members, height, features), jnp.bfloat16), small, small,
        ),
        scratch_shapes=[pltpu.VMEM(preact.shape, jnp.bfloat16)],
        compiler_params=params(),
    )(far_places, ids, gates, preact, tokens, *in_hbm(*before))


def unpack_kernel(parts_ref, out_ref):
    blocks, _, features = parts_ref.shape
    for block in range(blocks):
        out_ref[:, block * features : (block + 1) * features] = parts_ref[block]


def unpack_tokens(parts):
    members, rows, features = parts.shape
    each = members // 4
    return pl.pallas_call(
        unpack_kernel,
        grid=(4,),
        in_specs=[pl.BlockSpec((each, rows, features), lambda i: (i, 0, 0))],
        out_specs=pl.BlockSpec((rows, each * features), lambda i: (0, i)),
        out_shape=jax.ShapeDtypeStruct((rows, members * features), jnp.bfloat16),
        compiler_params=params(),
    )(parts)


def places_of(received_ref, source, rows):
    at = received_ref.shape[1] - TILE
    return received_ref[source, at : at + 2, 0:rows]


def token_rows(received_ref, rows):
    sources, _, features = received_ref.shape
    return received_ref[:, 0:rows, :].reshape(sources * rows, features)


def down_kernel(rows, wide, count, received_ref, *refs):
    out_refs, (turned, numbers, spread) = refs[-3 - count : -3], refs[-3:]
    sources, _, features = received_ref.shape
    hidden, each = wide // 2, BLOCK // (wide // 2)
    taken = rows * wide // features
    for source in range(sources):
        weighted = jnp.concatenate(
            [
                received_ref[source, rows : rows + taken, at : at + wide].astype(jnp.float32)
                for at in range(0, features, wide)
            ]
        )
        lanes = slice(source * rows, (source + 1) * rows)
        turned[:, lanes] = weighted.T
        numbers[:, lanes] = places_of(received_ref, source, rows).astype(jnp.float32)
    number = 0
    for out_ref in out_refs:
        for start in range(0, out_ref.shape[0], BLOCK):
            for expert in range(each):
                spread[expert * hidden : (expert + 1) * hidden, :] = jnp.where(
                    numbers[0:1, :] == number + expert,
                    turned[0:hidden, :],
                    jnp.where(numbers[1:2, :] == number + expert, turned[hidden:, :], 0.0),
                ).astype(jnp.bfloat16)
            number += each
            out_ref[start : start + BLOCK, :] = jnp.dot(
                spread[...], token_rows(received_ref, rows), preferred_element_type=jnp.float32
            ).astype(out_ref.dtype)


def down_partial(received, rows, wide, total_rows, count, before):
    sources, _, features = received.shape
    total = sources * rows
    return pl.pallas_call(
        functools.partial(down_kernel, rows, wide, count),
        in_specs=[
            pl.BlockSpec(memory_space=pltpu.VMEM),
            *[pl.BlockSpec(memory_space=pl.ANY) for _ in before],
        ],
        out_shape=[jax.ShapeDtypeStruct((total_rows // count, features), jnp.bfloat16)] * count,
        scratch_shapes=[
            pltpu.VMEM((wide, total), jnp.float32),
            pltpu.VMEM((2, total), jnp.float32),
            pltpu.VMEM((BLOCK, total), jnp.bfloat16),
        ],
        compiler_params=params(),
        cost_estimate=cost(total_rows, total, features),
    )(received, *in_hbm(*before))


def lane_numbers(received_ref, rows, wide):
    sources = received_ref.shape[0]
    low = low_half((sources * rows, wide))
    found = [
        columns_of(places_of(received_ref, source, rows), wide)
        for source in range(sources)
    ]
    odd = jnp.where(low, 0.0, 1.0)
    return low, *[jnp.concatenate([pair[k] for pair in found]) - odd for k in range(2)]


def join(piece_refs, full):
    start = 0
    for ref in piece_refs:
        full[start : start + ref.shape[0], :] = ref[...]
        start += ref.shape[0]


def project_kernel(count, received_ref, *refs):
    piece_refs, (out_ref, full) = refs[:count], refs[-2:]
    pl.when(pl.program_id(0) == 0)(lambda: join(piece_refs, full))
    sources, rows, wide = out_ref.shape
    low, first, second = lane_numbers(received_ref, rows, wide)
    tokens = token_rows(received_ref, rows)
    sums = [jnp.zeros((sources * rows, wide), jnp.float32) for _ in range(2)]
    number = 0.0
    for start in range(0, full.shape[0], BLOCK):
        product = lax.dot_general(
            tokens,
            full[start : start + BLOCK, :],
            (((1,), (1,)), ((), ())),
            preferred_element_type=jnp.float32,
        )
        for at in range(0, BLOCK, wide):
            part = product[:, at : at + wide]
            sums[0] = jnp.where(first == number, part, sums[0])
            sums[1] = jnp.where(second == number, part, sums[1])
            number += 2.0
    folded = [value + pltpu.roll(value, wide // 2, 1) for value in sums]
    value = jnp.where(low, folded[0], folded[1]).astype(out_ref.dtype)
    out_ref[...] = value.reshape(out_ref.shape)


def project(received, pieces, rows, wide, before):
    sources, height, features = received.shape
    joined = sum(piece.shape[0] for piece in pieces)
    return pl.pallas_call(
        functools.partial(project_kernel, len(pieces)),
        grid=(sources // 2,),
        in_specs=[
            pl.BlockSpec((2, height, features), lambda i: (i, 0, 0)),
            *[pl.BlockSpec(piece.shape, lambda i: (0, 0)) for piece in pieces],
            *[pl.BlockSpec(memory_space=pl.ANY) for _ in before],
        ],
        out_specs=pl.BlockSpec((2, rows, wide), lambda i: (i, 0, 0)),
        out_shape=pltpu.HBM((sources, rows, wide), jnp.bfloat16),
        scratch_shapes=[pltpu.VMEM((joined, features), jnp.bfloat16)],
        compiler_params=params(),
        cost_estimate=cost(sources * rows, features, joined),
    )(received, *in_hbm(*pieces), *before)


def hidden_kernel(parts_ref, activation_ref, scaled_ref, before_ref, hidden_ref, gate_ref):
    projected = parts_ref[0].astype(jnp.float32)
    for source in range(1, parts_ref.shape[0]):
        projected = projected + parts_ref[source].astype(jnp.float32)
    wide = projected.shape[1]
    half = lax.broadcasted_iota(jnp.int32, (8, wide), 1) // (wide // 2)
    wanted = lax.broadcasted_iota(jnp.int32, (8, wide), 0)
    sums = lax.dot_general(
        jnp.where(wanted == half, 1.0, 0.0),
        activation_ref[...] * projected,
        (((1,), (1,)), ((), ())),
        precision=lax.Precision.HIGHEST,
        preferred_element_type=jnp.float32,
    )
    gate_ref[...] = sums[0:2, :].astype(gate_ref.dtype)
    hidden = (projected * scaled_ref[...]).astype(hidden_ref.dtype)
    for source in range(hidden_ref.shape[0]):
        hidden_ref[source] = hidden


def input_kernel(count, received_ref, hidden_ref, *refs):
    piece_refs, (out_ref, full, spread) = refs[:count], refs[-3:]
    pl.when(pl.program_id(0) == 0)(lambda: join(piece_refs, full))
    sources, rows, wide = hidden_ref.shape
    low, first, second = lane_numbers(received_ref, rows, wide)
    values = hidden_ref[...].reshape(sources * rows, wide).astype(jnp.float32)
    swapped = pltpu.roll(values, wide // 2, 1)
    one = jnp.where(low, values, swapped)
    two = jnp.where(low, swapped, values)
    for start in range(0, full.shape[0], wide):
        number = start // wide * 2.0
        spread[:, start : start + wide] = jnp.where(
            first == number, one, jnp.where(second == number, two, 0.0)
        ).astype(jnp.bfloat16)
    out_ref[...] = (
        jnp.dot(spread[...], full[...], preferred_element_type=jnp.float32)
        .astype(out_ref.dtype)
        .reshape(out_ref.shape)
    )


def input_rows(received, hidden_grad, pieces, before):
    sources, rows, wide = hidden_grad.shape
    joined, features = sum(piece.shape[0] for piece in pieces), pieces[0].shape[1]
    return pl.pallas_call(
        functools.partial(input_kernel, len(pieces)),
        grid=(sources // 2,),
        in_specs=[
            pl.BlockSpec((2, received.shape[1], features), lambda i: (i, 0, 0)),
            pl.BlockSpec((2, rows, wide), lambda i: (i, 0, 0)),
            *[pl.BlockSpec(piece.shape, lambda i: (0, 0)) for piece in pieces],
            *[pl.BlockSpec(memory_space=pl.ANY) for _ in before],
        ],
        out_specs=pl.BlockSpec((2, rows, features), lambda i: (i, 0, 0)),
        out_shape=pltpu.HBM((sources, rows, features), jnp.bfloat16),
        scratch_shapes=[
            pltpu.VMEM((joined, features), jnp.bfloat16),
            pltpu.VMEM((2 * rows, joined), jnp.bfloat16),
        ],
        compiler_params=params(),
        cost_estimate=cost(sources * rows, joined, features),
    )(received, hidden_grad, *in_hbm(*pieces, *before))


def exchange(value, axes):
    return lax.all_to_all(value, axes, split_axis=0, concat_axis=0, tiled=True)


def swap(value, axis):
    return lax.ppermute(value, axis, SWAP)


def add(*terms):
    return sum(term.astype(jnp.float32) for term in terms).astype(jnp.bfloat16)


def body(token_grads, router_gates, expert_ids, saved_hidden, up_weight, down_weight):
    tok_count = token_grads.shape[0]
    local_experts, hidden, width = up_weight.shape
    members, far_count = lax.axis_size(GROUP), lax.axis_size(FAR)
    wide, features = 2 * hidden, width // PAIR
    own_rows = local_experts * hidden
    near = lax.axis_index("near")
    paired = lax.axis_size("high") == PAIR

    def halves(weight):
        flat = weight.reshape(own_rows, width)
        own = lax.dynamic_slice_in_dim(flat, near * features, features, axis=1)
        other = lax.dynamic_slice_in_dim(flat, (1 - near) * features, features, axis=1)
        return own, swap(other, "near")

    down_halves, up_halves = halves(down_weight), halves(up_weight)
    first = [down_halves[1], up_halves[1]]
    far_places = jnp.arange(far_count, dtype=jnp.int32)
    if paired:
        high_place = far_places // PAIR ^ lax.axis_index("high")
        far_places = (far_places % PAIR ^ lax.axis_index("low")) * PAIR + high_place
        beside = [swap(half, "high") for half in down_halves]
        low = [swap(half, "low") for half in down_halves]
        low_beside = [swap(half, "low") for half in beside]
        down_pieces = [*down_halves, *beside, *low, *low_beside]
        first += [beside[0], *low]
        up_own = stack(*up_halves, (beside[1], low_beside[0]))
        up_beside = swap(up_own, "high")
        up_low = swap(up_own, "low")
    else:
        down_pieces = [lax.all_gather(stack(*down_halves, ()), FAR, tiled=True)]
        up_pieces = [lax.all_gather(stack(*up_halves, ()), FAR, tiled=True)]
    packed, activation, scaled = pack_tokens(
        far_places, expert_ids.T, router_gates.T, saved_hidden, token_grads, members,
        local_experts, first,
    )
    received = exchange(packed, GROUP)

    projected = project(received, down_pieces, tok_count, wide, ())
    partial_value = down_partial(
        received, tok_count, wide, own_rows * PAIR * far_count, far_count if paired else 1,
        (projected,),
    )
    if paired:
        up_beside = pass_on(up_beside, (projected,))
        up_pieces = [up_own, up_beside, up_low, swap(up_beside, "low")]
    parts = exchange(projected, GROUP)
    gathered = pl.BlockSpec((members, tok_count, wide), lambda i: (0, 0, 0))
    single = pl.BlockSpec((tok_count, wide), lambda i: (0, 0))
    hidden_grad, gate_grads = pl.pallas_call(
        hidden_kernel,
        grid=(1,),
        in_specs=[gathered, single, single, pl.BlockSpec(memory_space=pl.ANY)],
        out_specs=(gathered, pl.BlockSpec((2, tok_count), lambda i: (0, 0))),
        out_shape=(
            pltpu.HBM((members, tok_count, wide), jnp.bfloat16),
            jax.ShapeDtypeStruct((2, tok_count), jnp.bfloat16),
        ),
        compiler_params=params(),
    )(parts, activation, scaled, partial_value[0])
    if paired:
        own, beside, low, low_beside = partial_value
        before = add_pairs([(beside, swap(low_beside, "low"))], ())
        low = swap(low, "low")
        passed, kept = [
            add(own[at], low[at], swap(before[0][at], "high"))
            for at in (slice(own_rows, None), slice(0, own_rows))
        ]
    else:
        before = ()
        sums = lax.psum_scatter(partial_value[0], FAR, scatter_dimension=0, tiled=True)
        kept, passed = sums[:own_rows], sums[own_rows:]
    rows_back = input_rows(received, exchange(hidden_grad, GROUP), up_pieces, before)
    input_grads = unpack_tokens(exchange(rows_back, GROUP))

    down_grads = place_halves(near, kept, swap(passed, "near"), input_grads)
    down_grads = down_grads.reshape(down_weight.shape)
    return (input_grads, gate_grads.T, down_grads)


def solution(mesh):
    sizes = [mesh.shape[name] for name in ("expert", "inner", "outer")]
    expert = ("high", "low", "near")
    split = Mesh(
        mesh.devices.reshape(sizes[0] // PAIR**2, PAIR, PAIR, *sizes[1:]),
        (*expert, "inner", "outer"),
    )
    rows = P((*expert, "inner", "outer"), None)
    weights = P(expert, None, ("inner", "outer"))
    return jax.shard_map(
        body,
        mesh=split,
        in_specs=(rows, rows, rows, rows, weights, weights),
        out_specs=(rows, rows, weights),
        check_vma=False,
    )
```

```python
import functools
import jax
import jax.numpy as jnp
from jax import lax
from jax.experimental import pallas as pl
from jax.experimental.pallas import tpu as pltpu
from jax.sharding import Mesh, PartitionSpec as P

root_half = 0.7071067811865476
inv_root_tau = 0.3989422804014327
GROUP = ("inner", "outer", "near")
FAR = ("high", "low")
PAIR = 2
BLOCK = 256
TILE = 16
MIB = 1 << 20
SWAP = ((0, 1), (1, 0))


def gelu_parts(preact):
    cumulative = 0.5 * (1.0 + lax.erf(preact * root_half))
    density = inv_root_tau * jnp.exp(-0.5 * preact * preact)
    return (preact * cumulative, cumulative + preact * density)


def params(grant=20):
    return pltpu.CompilerParams(vmem_limit_bytes=grant * MIB)


def cost(rows, inner, columns):
    return pl.CostEstimate(
        flops=2 * rows * inner * columns,
        bytes_accessed=2 * (rows * inner + inner * columns + rows * columns),
        transcendentals=0,
    )


def low_half(shape):
    return lax.broadcasted_iota(jnp.int32, shape, len(shape) - 1) < shape[-1] // 2


def columns_of(pair, wide):
    wanted = lax.broadcasted_iota(jnp.int32, (2, wide), 0)
    return [
        lax.dot_general(
            pair.astype(jnp.bfloat16),
            jnp.where(wanted == k, 1.0, 0.0).astype(jnp.bfloat16),
            (((0,), (0,)), ((), ())),
            preferred_element_type=jnp.float32,
        )
        for k in range(2)
    ]


def in_hbm(*arrays):
    return [pltpu.with_memory_space_constraint(array, pltpu.HBM) for array in arrays]


def stack_kernel(own_ref, other_ref, *refs):
    rows = own_ref.shape[0]
    refs[-1][0:rows, :] = own_ref[...]
    refs[-1][rows:, :] = other_ref[...]


def stack(own, other, before):
    return pl.pallas_call(
        stack_kernel,
        in_specs=[
            *[pl.BlockSpec(memory_space=pltpu.VMEM)] * 2,
            *[pl.BlockSpec(memory_space=pl.ANY) for _ in before],
        ],
        out_shape=jax.ShapeDtypeStruct((2 * own.shape[0], own.shape[1]), own.dtype),
        compiler_params=params(),
    )(own, other, *in_hbm(*before))


def pass_on(value, before):
    anywhere = pl.BlockSpec(memory_space=pl.ANY)
    return pl.pallas_call(
        lambda *refs: None,
        in_specs=[anywhere] * (1 + len(before)),
        out_specs=anywhere,
        out_shape=pltpu.HBM(value.shape, value.dtype),
        input_output_aliases={0: 0},
        compiler_params=params(),
    )(*in_hbm(value), *before)


def place_kernel(near_ref, kept_ref, passed_ref, before_ref, out_ref):
    features = kept_ref.shape[1]
    first = near_ref[0] == 0
    kept, passed = kept_ref[...], passed_ref[...]
    out_ref[:, 0:features] = jnp.where(first, kept, passed)
    out_ref[:, features:] = jnp.where(first, passed, kept)


def place_halves(near, kept, passed, before):
    rows, features = kept.shape
    return pl.pallas_call(
        place_kernel,
        in_specs=[
            pl.BlockSpec(memory_space=pltpu.SMEM),
            *[pl.BlockSpec(memory_space=pltpu.VMEM)] * 2,
            pl.BlockSpec(memory_space=pl.ANY),
        ],
        out_shape=jax.ShapeDtypeStruct((rows, PAIR * features), kept.dtype),
        compiler_params=params(),
    )(near[None], kept, passed, *in_hbm(before))


def add_kernel(count, *refs):
    terms, out_refs = refs[: 2 * count], refs[-count:]
    for at in range(count):
        left, right = terms[2 * at][...], terms[2 * at + 1][...]
        total = left.astype(jnp.float32) + right.astype(jnp.float32)
        out_refs[at][...] = total.astype(out_refs[at].dtype)


def add_pairs(pairs, before):
    flat = [term for pair in pairs for term in pair]
    return pl.pallas_call(
        functools.partial(add_kernel, len(pairs)),
        in_specs=[
            *[pl.BlockSpec(memory_space=pltpu.VMEM) for _ in flat],
            *[pl.BlockSpec(memory_space=pl.ANY) for _ in before],
        ],
        out_shape=[jax.ShapeDtypeStruct(pair[0].shape, pair[0].dtype) for pair in pairs],
        compiler_params=params(),
    )(*flat, *in_hbm(*before))


def pack_kernel(
    local_experts, far_ref, ids_ref, gates_ref, preact_ref, tokens_ref, *refs
):
    out_ref, activation_ref, scaled_ref, weighted = refs[-4:]
    blocks, height, features = out_ref.shape
    rows, wide = preact_ref.shape
    far_count = far_ref.shape[0]
    taken = rows * wide // features

    @pl.when(pl.program_id(0) == 0)
    def _():
        activation, slope = gelu_parts(preact_ref[...].astype(jnp.float32))
        gates = jnp.where(low_half((rows, wide)), *columns_of(gates_ref[...], wide))
        activation_ref[...] = activation
        scaled_ref[...] = gates * slope
        weighted[...] = (gates * activation).astype(jnp.bfloat16)

    ids = ids_ref[...]
    local = lax.rem(ids, local_experts)
    line = lax.div(ids, local_experts)
    far, near = lax.div(line, PAIR), lax.rem(line, PAIR)
    far_place = jnp.zeros_like(far)
    for at in range(far_count):
        far_place = jnp.where(far == at, far_ref[at], far_place)
    for block in range(blocks):
        side = lax.rem(near + block, PAIR)
        place = (far_place * PAIR + side) * local_experts + local
        out_ref[block, 0:rows, :] = tokens_ref[:, block * features : (block + 1) * features]
        for at in range(0, features, wide):
            start = at // wide * taken
            out_ref[block, rows : rows + taken, at : at + wide] = weighted[start : start + taken, :]
        last = height - TILE
        out_ref[block, last:, :] = jnp.zeros((TILE, features), jnp.bfloat16)
        out_ref[block, last : last + 2, 0:rows] = place.astype(jnp.bfloat16)


def pack_tokens(far_places, ids, gates, preact, tokens, members, local_experts, before):
    rows, width = tokens.shape
    features = width // members
    each = members // 4
    height = rows + preact.size // features + TILE
    small = jax.ShapeDtypeStruct(preact.shape, jnp.float32)
    whole = [pl.BlockSpec(array.shape, lambda i: (0, 0)) for array in (ids, gates, preact)]
    return pl.pallas_call(
        functools.partial(pack_kernel, local_experts),
        grid=(4,),
        in_specs=[
            pl.BlockSpec(memory_space=pltpu.SMEM),
            *whole,
            pl.BlockSpec((rows, each * features), lambda i: (0, i)),
            *[pl.BlockSpec(memory_space=pl.ANY) for _ in before],
        ],
        out_specs=(pl.BlockSpec((each, height, features), lambda i: (i, 0, 0)), whole[2], whole[2]),
        out_shape=(
            pltpu.HBM((members, height, features), jnp.bfloat16), small, small,
        ),
        scratch_shapes=[pltpu.VMEM(preact.shape, jnp.bfloat16)],
        compiler_params=params(),
    )(far_places, ids, gates, preact, tokens, *in_hbm(*before))


def unpack_kernel(parts_ref, out_ref):
    blocks, _, features = parts_ref.shape
    for block in range(blocks):
        out_ref[:, block * features : (block + 1) * features] = parts_ref[block]


def unpack_tokens(parts):
    members, rows, features = parts.shape
    each = members // 4
    return pl.pallas_call(
        unpack_kernel,
        grid=(4,),
        in_specs=[pl.BlockSpec((each, rows, features), lambda i: (i, 0, 0))],
        out_specs=pl.BlockSpec((rows, each * features), lambda i: (0, i)),
        out_shape=jax.ShapeDtypeStruct((rows, members * features), jnp.bfloat16),
        compiler_params=params(),
    )(parts)


def places_of(received_ref, source, rows):
    at = received_ref.shape[1] - TILE
    return received_ref[source, at : at + 2, 0:rows]


def token_rows(received_ref, rows):
    sources, _, features = received_ref.shape
    return received_ref[:, 0:rows, :].reshape(sources * rows, features)


def down_kernel(rows, wide, count, received_ref, *refs):
    out_refs, (turned, numbers, spread) = refs[-3 - count : -3], refs[-3:]
    sources, _, features = received_ref.shape
    hidden, each = wide // 2, BLOCK // (wide // 2)
    taken = rows * wide // features
    for source in range(sources):
        weighted = jnp.concatenate(
            [
                received_ref[source, rows : rows + taken, at : at + wide].astype(jnp.float32)
                for at in range(0, features, wide)
            ]
        )
        lanes = slice(source * rows, (source + 1) * rows)
        turned[:, lanes] = weighted.T
        numbers[:, lanes] = places_of(received_ref, source, rows).astype(jnp.float32)
    number = 0
    for out_ref in out_refs:
        for start in range(0, out_ref.shape[0], BLOCK):
            for expert in range(each):
                spread[expert * hidden : (expert + 1) * hidden, :] = jnp.where(
                    numbers[0:1, :] == number + expert,
                    turned[0:hidden, :],
                    jnp.where(numbers[1:2, :] == number + expert, turned[hidden:, :], 0.0),
                ).astype(jnp.bfloat16)
            number += each
            out_ref[start : start + BLOCK, :] = jnp.dot(
                spread[...], token_rows(received_ref, rows), preferred_element_type=jnp.float32
            ).astype(out_ref.dtype)


def down_partial(received, rows, wide, total_rows, count, before):
    sources, _, features = received.shape
    total = sources * rows
    return pl.pallas_call(
        functools.partial(down_kernel, rows, wide, count),
        in_specs=[
            pl.BlockSpec(memory_space=pltpu.VMEM),
            *[pl.BlockSpec(memory_space=pl.ANY) for _ in before],
        ],
        out_shape=[jax.ShapeDtypeStruct((total_rows // count, features), jnp.bfloat16)] * count,
        scratch_shapes=[
            pltpu.VMEM((wide, total), jnp.float32),
            pltpu.VMEM((2, total), jnp.float32),
            pltpu.VMEM((BLOCK, total), jnp.bfloat16),
        ],
        compiler_params=params(),
        cost_estimate=cost(total_rows, total, features),
    )(received, *in_hbm(*before))


def lane_numbers(received_ref, rows, wide):
    sources = received_ref.shape[0]
    low = low_half((sources * rows, wide))
    found = [
        columns_of(places_of(received_ref, source, rows), wide)
        for source in range(sources)
    ]
    odd = jnp.where(low, 0.0, 1.0)
    return low, *[jnp.concatenate([pair[k] for pair in found]) - odd for k in range(2)]


def join(piece_refs, full):
    start = 0
    for ref in piece_refs:
        full[start : start + ref.shape[0], :] = ref[...]
        start += ref.shape[0]


def project_kernel(count, received_ref, *refs):
    piece_refs, (out_ref, full) = refs[:count], refs[-2:]
    pl.when(pl.program_id(0) == 0)(lambda: join(piece_refs, full))
    sources, rows, wide = out_ref.shape
    low, first, second = lane_numbers(received_ref, rows, wide)
    tokens = token_rows(received_ref, rows)
    sums = [jnp.zeros((sources * rows, wide), jnp.float32) for _ in range(2)]
    number = 0.0
    for start in range(0, full.shape[0], BLOCK):
        product = lax.dot_general(
            tokens,
            full[start : start + BLOCK, :],
            (((1,), (1,)), ((), ())),
            preferred_element_type=jnp.float32,
        )
        for at in range(0, BLOCK, wide):
            part = product[:, at : at + wide]
            sums[0] = jnp.where(first == number, part, sums[0])
            sums[1] = jnp.where(second == number, part, sums[1])
            number += 2.0
    folded = [value + pltpu.roll(value, wide // 2, 1) for value in sums]
    value = jnp.where(low, folded[0], folded[1]).astype(out_ref.dtype)
    out_ref[...] = value.reshape(out_ref.shape)


def project(received, pieces, rows, wide, before):
    sources, height, features = received.shape
    joined = sum(piece.shape[0] for piece in pieces)
    return pl.pallas_call(
        functools.partial(project_kernel, len(pieces)),
        grid=(sources // 2,),
        in_specs=[
            pl.BlockSpec((2, height, features), lambda i: (i, 0, 0)),
            *[pl.BlockSpec(piece.shape, lambda i: (0, 0)) for piece in pieces],
            *[pl.BlockSpec(memory_space=pl.ANY) for _ in before],
        ],
        out_specs=pl.BlockSpec((2, rows, wide), lambda i: (i, 0, 0)),
        out_shape=pltpu.HBM((sources, rows, wide), jnp.bfloat16),
        scratch_shapes=[pltpu.VMEM((joined, features), jnp.bfloat16)],
        compiler_params=params(),
        cost_estimate=cost(sources * rows, features, joined),
    )(received, *in_hbm(*pieces), *before)


def hidden_kernel(parts_ref, activation_ref, scaled_ref, hidden_ref, gate_ref):
    projected = parts_ref[0].astype(jnp.float32)
    for source in range(1, parts_ref.shape[0]):
        projected = projected + parts_ref[source].astype(jnp.float32)
    wide = projected.shape[1]
    half = lax.broadcasted_iota(jnp.int32, (8, wide), 1) // (wide // 2)
    wanted = lax.broadcasted_iota(jnp.int32, (8, wide), 0)
    sums = lax.dot_general(
        jnp.where(wanted == half, 1.0, 0.0),
        activation_ref[...] * projected,
        (((1,), (1,)), ((), ())),
        precision=lax.Precision.HIGHEST,
        preferred_element_type=jnp.float32,
    )
    gate_ref[...] = sums[0:2, :].astype(gate_ref.dtype)
    hidden = (projected * scaled_ref[...]).astype(hidden_ref.dtype)
    for source in range(hidden_ref.shape[0]):
        hidden_ref[source] = hidden


def input_kernel(count, received_ref, hidden_ref, *refs):
    piece_refs, (out_ref, full, spread) = refs[:count], refs[-3:]
    pl.when(pl.program_id(0) == 0)(lambda: join(piece_refs, full))
    sources, rows, wide = hidden_ref.shape
    low, first, second = lane_numbers(received_ref, rows, wide)
    values = hidden_ref[...].reshape(sources * rows, wide).astype(jnp.float32)
    swapped = pltpu.roll(values, wide // 2, 1)
    one = jnp.where(low, values, swapped)
    two = jnp.where(low, swapped, values)
    for start in range(0, full.shape[0], wide):
        number = start // wide * 2.0
        spread[:, start : start + wide] = jnp.where(
            first == number, one, jnp.where(second == number, two, 0.0)
        ).astype(jnp.bfloat16)
    out_ref[...] = (
        jnp.dot(spread[...], full[...], preferred_element_type=jnp.float32)
        .astype(out_ref.dtype)
        .reshape(out_ref.shape)
    )


def input_rows(received, hidden_grad, pieces, before):
    sources, rows, wide = hidden_grad.shape
    joined, features = sum(piece.shape[0] for piece in pieces), pieces[0].shape[1]
    return pl.pallas_call(
        functools.partial(input_kernel, len(pieces)),
        grid=(sources // 2,),
        in_specs=[
            pl.BlockSpec((2, received.shape[1], features), lambda i: (i, 0, 0)),
            pl.BlockSpec((2, rows, wide), lambda i: (i, 0, 0)),
            *[pl.BlockSpec(piece.shape, lambda i: (0, 0)) for piece in pieces],
            *[pl.BlockSpec(memory_space=pl.ANY) for _ in before],
        ],
        out_specs=pl.BlockSpec((2, rows, features), lambda i: (i, 0, 0)),
        out_shape=pltpu.HBM((sources, rows, features), jnp.bfloat16),
        scratch_shapes=[
            pltpu.VMEM((joined, features), jnp.bfloat16),
            pltpu.VMEM((2 * rows, joined), jnp.bfloat16),
        ],
        compiler_params=params(),
        cost_estimate=cost(sources * rows, joined, features),
    )(received, hidden_grad, *in_hbm(*pieces, *before))


def exchange(value, axes):
    return lax.all_to_all(value, axes, split_axis=0, concat_axis=0, tiled=True)


def swap(value, axis):
    return lax.ppermute(value, axis, SWAP)


def add(*terms):
    return sum(term.astype(jnp.float32) for term in terms).astype(jnp.bfloat16)


def body(token_grads, router_gates, expert_ids, saved_hidden, up_weight, down_weight):
    tok_count = token_grads.shape[0]
    local_experts, hidden, width = up_weight.shape
    members, far_count = lax.axis_size(GROUP), lax.axis_size(FAR)
    wide, features = 2 * hidden, width // PAIR
    own_rows = local_experts * hidden
    near = lax.axis_index("near")
    paired = lax.axis_size("high") == PAIR

    def halves(weight):
        flat = weight.reshape(own_rows, width)
        own = lax.dynamic_slice_in_dim(flat, near * features, features, axis=1)
        other = lax.dynamic_slice_in_dim(flat, (1 - near) * features, features, axis=1)
        return own, swap(other, "near")

    down_halves, up_halves = halves(down_weight), halves(up_weight)
    first = [down_halves[1], up_halves[1]]
    far_places = jnp.arange(far_count, dtype=jnp.int32)
    if paired:
        high_place = far_places // PAIR ^ lax.axis_index("high")
        far_places = (far_places % PAIR ^ lax.axis_index("low")) * PAIR + high_place
        beside = [swap(half, "high") for half in down_halves]
        low = [swap(half, "low") for half in down_halves]
        low_beside = [swap(half, "low") for half in beside]
        down_pieces = [*down_halves, *beside, *low, *low_beside]
        first += [beside[0], *low]
        up_low = swap(stack(*up_halves, ()), "low")
        up_own = stack(*up_halves, (beside[1], low_beside[0], up_low))
        up_beside = swap(up_own, "high")
    else:
        down_pieces = [lax.all_gather(stack(*down_halves, ()), FAR, tiled=True)]
        up_pieces = [lax.all_gather(stack(*up_halves, ()), FAR, tiled=True)]
    packed, activation, scaled = pack_tokens(
        far_places, expert_ids.T, router_gates.T, saved_hidden, token_grads, members,
        local_experts, first,
    )
    received = exchange(packed, GROUP)

    partial_value = down_partial(
        received, tok_count, wide, own_rows * PAIR * far_count, far_count if paired else 1, ()
    )
    projected = project(received, down_pieces, tok_count, wide, partial_value[:1])
    if paired:
        up_beside = pass_on(up_beside, (projected,))
        up_pieces = [up_own, up_beside, up_low, swap(up_beside, "low")]
    parts = exchange(projected, GROUP)
    gathered = pl.BlockSpec((members, tok_count, wide), lambda i: (0, 0, 0))
    single = pl.BlockSpec((tok_count, wide), lambda i: (0, 0))
    hidden_grad, gate_grads = pl.pallas_call(
        hidden_kernel,
        grid=(1,),
        in_specs=[gathered, single, single],
        out_specs=(gathered, pl.BlockSpec((2, tok_count), lambda i: (0, 0))),
        out_shape=(
            pltpu.HBM((members, tok_count, wide), jnp.bfloat16),
            jax.ShapeDtypeStruct((2, tok_count), jnp.bfloat16),
        ),
        compiler_params=params(),
    )(parts, activation, scaled)
    if paired:
        own, beside, low, low_beside = partial_value
        before = add_pairs([(beside, swap(low_beside, "low"))], ())
        low = swap(low, "low")
        passed, kept = [
            add(own[at], low[at], swap(before[0][at], "high"))
            for at in (slice(own_rows, None), slice(0, own_rows))
        ]
    else:
        before = ()
        sums = lax.psum_scatter(partial_value[0], FAR, scatter_dimension=0, tiled=True)
        kept, passed = sums[:own_rows], sums[own_rows:]
    rows_back = input_rows(received, exchange(hidden_grad, GROUP), up_pieces, before)
    input_grads = unpack_tokens(exchange(rows_back, GROUP))

    down_grads = place_halves(near, kept, swap(passed, "near"), input_grads)
    down_grads = down_grads.reshape(down_weight.shape)
    return (input_grads, gate_grads.T, down_grads)


def solution(mesh):
    sizes = [mesh.shape[name] for name in ("expert", "inner", "outer")]
    expert = ("high", "low", "near")
    split = Mesh(
        mesh.devices.reshape(sizes[0] // PAIR**2, PAIR, PAIR, *sizes[1:]),
        (*expert, "inner", "outer"),
    )
    rows = P((*expert, "inner", "outer"), None)
    weights = P(expert, None, ("inner", "outer"))
    return jax.shard_map(
        body,
        mesh=split,
        in_specs=(rows, rows, rows, rows, weights, weights),
        out_specs=(rows, rows, weights),
        check_vma=False,
    )
```
